768 devices in a mesh: pair: 192 (over z, y_hi, x, core), virt: 4 (over y_lo).
Axes of the slice: x: 4, y: 8 (y_hi: 2, y_lo: 4; y = y_hi * 4 + y_lo), z: 12, core: 2. Of those that a mesh axis runs over, the one named last changes fastest.
Arguments:
- amplitudes: bfloat16 [768, 1600, 200], P('pair', 'virt'), may hold values from -6 to 6
- integrals: bfloat16 [768, 1600, 200], P('pair', 'virt'), may hold values from -6 to 6
- ladder_slab: bfloat16 [16, 1600, 200], P(None, 'virt'), may hold values from -0.4375 to 0.4375
- pair_list: int32 [768, 2], P('pair'), may hold values from 0 to 199, as said below
- mirror_slot: int32 [768], P('pair'), may hold values from 0 to 3, as said below
- occ_irrep: int32 [200], replicated, may hold values from 0 to 7
- occ_energy: float32 [200], replicated, may hold values from -2 to -0.5
- virt_energy: bfloat16 [1600], P('virt'), may hold values from 0.29882812 to 3
Outputs:
- new_amplitudes: bfloat16 [768, 1600, 200], P('pair', 'virt')
The draws below stay inside these ranges and needn't reach their ends.
Inputs may be any that keep to these rules, and one draw needn't show every extreme that they name: `pair_list`: each row is (i, j) with i != j. The pair at slot s of index d of pair has its mirror (j, i) at index (d + 96) mod 192, slot mirror_slot of that row; the mirror of the mirror is the pair itself. `mirror_slot`: on each index of pair the slots of the mirrors form a permutation of 0 to 3.
All inputs are finite; a program needn't handle non-finite values.
Results may differ from the reference program's by a relative error of at most 0.005.
Values may be sent and summed in bfloat16 or wider, within the bound.
No kernel may reach another device: no remote copies, remote signals or barrier semaphores. Data moves between devices by JAX's collectives and lax.ppermute only.
A program may use at most 128 MiB of HBM per device.

```python
import jax
import jax.numpy as jnp
from jax import lax

O = 200
V = 1600
NQ = 16
PAIR_DEV = 4
PAIRS = 768
N_PAIR = 192


def mirror_plan(key):
    half_pairs = N_PAIR // 2
    first_orb = jax.random.randint(jax.random.fold_in(key, 11), (half_pairs, PAIR_DEV), 0, O)
    offset = jax.random.randint(jax.random.fold_in(key, 12), (half_pairs, PAIR_DEV), 1, O)
    second_orb = (first_orb + offset) % O
    scores = jax.random.randint(jax.random.fold_in(key, 13), (half_pairs, PAIR_DEV), 0, 1 << 20) * PAIR_DEV + jnp.arange(PAIR_DEV, dtype=jnp.int32)[None, :]
    slot_order = jnp.argsort(scores, axis=1).astype(jnp.int32)
    inverse = jnp.argsort(slot_order, axis=1).astype(jnp.int32)
    upper_pairs = jnp.stack([first_orb, second_orb], axis=-1)
    lower_first = jnp.take_along_axis(second_orb, slot_order, axis=1)
    lower_second = jnp.take_along_axis(first_orb, slot_order, axis=1)
    lower_pairs = jnp.stack([lower_first, lower_second], axis=-1)
    pairs_all = jnp.concatenate([upper_pairs, lower_pairs], axis=0).reshape(PAIRS, 2).astype(jnp.int32)
    slots_all = jnp.concatenate([inverse, slot_order], axis=0).reshape(PAIRS).astype(jnp.int32)
    return (pairs_all, slots_all)


def draw_pair_list(key, part):
    pairs_all, slots_all = mirror_plan(key)
    return pairs_all


def draw_mirror_slot(key, part):
    pairs_all, slots_all = mirror_plan(key)
    return slots_all


def plant(entries, stream_key, smallest, top_value):
    extent = entries.shape
    spot = [jax.random.randint(jax.random.fold_in(stream_key, axis), (), 0, extent[axis]) for axis in range(len(extent))]
    entries = entries.at[tuple(spot)].set(smallest)
    longest = extent.index(max(extent))
    spot[longest] = (spot[longest] + 1) % extent[longest]
    return entries.at[tuple(spot)].set(top_value)


def steps_of(stream_key, dims, pieces, smallest, top_value):
    def one(axis_at, blocks):
        heights = jax.random.uniform(jax.random.fold_in(jax.random.fold_in(stream_key, 6), axis_at), (blocks,), jnp.float32, smallest / len(pieces), top_value / len(pieces))
        return jnp.repeat(jnp.exp(heights), dims[axis_at] // blocks).reshape((-1,) + (1,) * (len(dims) - axis_at - 1))

    gain = one(*pieces[0])
    for cut in pieces[1:]:
        gain = gain * one(*cut)
    return gain


def scatter_about(stream_key, shape, spread, limit, split=(), held_as=jnp.bfloat16):
    array = jax.random.normal(stream_key, shape, jnp.float32) * spread
    if len(split) > 0:
        array = steps_of(stream_key, shape, split, -0.22, 0.18) * array
    return jnp.clip(array, min=-limit, max=limit).astype(held_as)


def setup_inputs(seed: int = 0) -> dict:
    keys = jax.random.split(jax.random.key(seed), 9)
    return {
        "amplitudes": scatter_about(keys[0], (PAIRS, V, V // 8), 1.0, 6.0, ((0, 192), (1, 4))),
        "integrals": scatter_about(keys[1], (PAIRS, V, V // 8), 1.0, 6.0, ((0, 192), (1, 4))),
        "ladder_slab": scatter_about(keys[2], (NQ, V, V // 8), (V // 8) ** -0.5, 0.4375, ((1, 4),)),
        "pair_list": draw_pair_list(jax.random.fold_in(keys[8], 71), 0),
        "mirror_slot": draw_mirror_slot(jax.random.fold_in(keys[8], 71), 0),
        "occ_irrep": plant(jax.random.randint(keys[5], (O,), 0, 8), jax.random.fold_in(keys[5], 1), 0, 7).astype(jnp.int32),
        "occ_energy": jnp.clip(jax.random.uniform(keys[6], (O,), jnp.float32, -2.0, -0.5), -2.0, -0.5),
        "virt_energy": jnp.clip(0.29882812 + 2.7011719 * jax.random.uniform(keys[7], (V,), jnp.float32) ** steps_of(keys[7], (V,), ((0, 4),), -0.2, 0.2), 0.29882812, 3.0).astype(jnp.bfloat16),
    }


def reference(amplitudes, integrals, ladder_slab, pair_list, mirror_slot, occ_irrep, occ_energy, virt_energy):
    width = V // 8
    irrep_count = 8
    symmetry = jnp.bitwise_xor(occ_irrep[pair_list[:, 0]], occ_irrep[pair_list[:, 1]]).astype(jnp.int32)
    slab_blocks = ladder_slab.astype(jnp.float32).reshape(NQ, irrep_count, width, width)
    block_ids = jnp.arange(irrep_count, dtype=jnp.int32)

    def ladder(inputs):
        amp_tile, int_tile, pair_irrep = inputs
        amp_blocks = amp_tile.astype(jnp.float32).reshape(irrep_count, width, width)
        partner = jnp.bitwise_xor(block_ids, pair_irrep)
        half_done = jnp.einsum("qhac,hcd->qhad", slab_blocks, amp_blocks).astype(jnp.bfloat16)
        right_slab = slab_blocks[:, partner]
        ladder_sum = jnp.einsum("qhad,qhbd->hab", half_done.astype(jnp.float32), right_slab)
        return (int_tile.astype(jnp.float32).reshape(irrep_count, width, width) + ladder_sum).astype(jnp.bfloat16)

    residual = lax.map(ladder, (amplitudes, integrals, symmetry))
    owner = jnp.arange(PAIRS, dtype=jnp.int32) // PAIR_DEV
    mirror = ((owner + N_PAIR // 2) % N_PAIR) * PAIR_DEV + mirror_slot
    energy_blocks = virt_energy.astype(jnp.float32).reshape(irrep_count, width)

    def update(inputs):
        amp_tile, own_resid, pair_irrep, mirror_index, orbitals = inputs
        other_resid = residual[mirror_index]
        partner = jnp.bitwise_xor(block_ids, pair_irrep)
        flipped = jnp.swapaxes(other_resid[partner], 1, 2)
        symmetric = own_resid.astype(jnp.float32) + flipped.astype(jnp.float32)
        far_energy = energy_blocks[partner]
        denominator = occ_energy[orbitals[0]] + occ_energy[orbitals[1]] - energy_blocks[:, :, None] - far_energy[:, None, :]
        amp_blocks = amp_tile.astype(jnp.float32).reshape(irrep_count, width, width)
        return (amp_blocks + symmetric / denominator).astype(jnp.bfloat16).reshape(V, width)

    return lax.map(update, (amplitudes, residual, symmetry, mirror, pair_list))
```

```python
import functools

import jax
import jax.numpy as jnp
from jax import lax
from jax.experimental import pallas as pl
from jax.experimental.pallas import tpu as pltpu
from jax.sharding import PartitionSpec as P

W = 200
NQ = 16
DEEP = NQ * W
TALL = 208
PIECE = 160
UNIT = 4 * PIECE
BF = jnp.bfloat16
F32 = jnp.float32
VMEM_LIMIT = 56 * 1024 * 1024


def permute(value, move):
    layers, halves, width, cores, lines = lax.axis_size("pair") // 16, 2, 4, 2, 4
    pairs = []
    for z in range(layers):
        for y in range(halves * lines):
            for x in range(width):
                for core in range(cores):
                    ends = []
                    for tz, ty, tx, tc in ((z, y, x, core), move(z, y, x, core)):
                        tz, ty, tx, tc = tz % layers, ty % (halves * lines), tx % width, tc % cores
                        pair = ((tz * halves + ty // lines) * width + tx) * cores + tc
                        ends.append(pair * lines + ty % lines)
                    pairs.append(tuple(ends))
    return lax.ppermute(value, ("pair", "virt"), pairs)


def along_y(value):
    return permute(value, lambda z, y, x, core: (z, y + 1 - 2 * core, x, core))


def swap_cores(value):
    return permute(value, lambda z, y, x, core: (z, y, x, 1 - core))


def to_mirror(value):
    half = lax.axis_size("pair") // 32
    return permute(value, lambda z, y, x, core: (z + half, y, x, core))


def params(*semantics):
    return pltpu.CompilerParams(
        dimension_semantics=semantics, vmem_limit_bytes=VMEM_LIMIT
    )


def pack_kernel(order_ref, slab_ref, energy_ref, out_ref):
    for q in range(NQ):
        out_ref[0:W, q * W : (q + 1) * W] = slab_ref[q, 0]
    out_ref[W:TALL, 0:W] = jnp.broadcast_to(energy_ref[0], (TALL - W, W))
    out_ref[W:TALL, W:DEEP] = jnp.zeros((TALL - W, DEEP - W), BF)


def pack_slab(slab, energy, block):
    return pl.pallas_call(
        pack_kernel,
        out_shape=jax.ShapeDtypeStruct((TALL, DEEP), BF),
        grid_spec=pltpu.PrefetchScalarGridSpec(
            num_scalar_prefetch=1,
            grid=(1,),
            in_specs=[
                pl.BlockSpec((NQ, 1, W, W), lambda i, order: (0, order[0], 0, 0)),
                pl.BlockSpec((1, 1, W), lambda i, order: (order[0], 0, 0)),
            ],
            out_specs=pl.BlockSpec((TALL, DEEP), lambda i, order: (0, 0)),
        ),
        compiler_params=params("arbitrary"),
        cost_estimate=pl.CostEstimate(flops=0, bytes_accessed=3_000_000, transcendentals=0),
    )(block, slab, energy)


def half_kernel(slab_ref, amp_ref, out_ref):
    for q in range(NQ):
        out_ref[0, 0, :, q * W : (q + 1) * W] = jnp.dot(
            slab_ref[q, 0], amp_ref[0, 0], preferred_element_type=F32
        ).astype(BF)


def first_half(slab, amplitudes):
    pairs = amplitudes.shape[0]
    return pl.pallas_call(
        half_kernel,
        out_shape=jax.ShapeDtypeStruct((pairs, 2, W, DEEP), BF),
        grid=(2, pairs),
        in_specs=[
            pl.BlockSpec((NQ, 1, W, W), lambda b, p: (0, b, 0, 0)),
            pl.BlockSpec((1, 1, W, W), lambda b, p: (p, b, 0, 0)),
        ],
        out_specs=pl.BlockSpec((1, 1, W, DEEP), lambda b, p: (p, b, 0, 0)),
        compiler_params=params("arbitrary", "arbitrary"),
        cost_estimate=pl.CostEstimate(
            flops=2 * pairs * 2 * NQ * W**3, bytes_accessed=18_000_000, transcendentals=0
        ),
    )(slab, amplitudes)


def put_tile(unit_ref, block, tile):
    unit_ref[block * W : (block + 1) * W, :] = tile[:, 0:128]
    unit_ref[2 * W : 3 * W, block * 64 : (block + 1) * 64] = tile[:, 128:192]
    base = 3 * W + 16 * block
    for c in range(13):
        rows = min(16, W - 16 * c)
        unit_ref[base : base + rows, 8 * c : 8 * c + 8] = tile[16 * c : 16 * c + rows, 192:200]


def get_tile(unit, block):
    base = 3 * W + 16 * block
    tail = [
        unit[base : base + min(16, W - 16 * c), 8 * c : 8 * c + 8] for c in range(13)
    ]
    return jnp.concatenate(
        [
            unit[block * W : (block + 1) * W, :],
            unit[2 * W : 3 * W, block * 64 : (block + 1) * 64],
            jnp.concatenate(tail, axis=0),
        ],
        axis=1,
    )


def ladder_kernel(first, source_ref, half_ref, int_ref, *refs):
    sources, (out_ref, far_ref, right, unit, sems) = refs[:8], refs[8:]
    pair, block = pl.program_id(0), pl.program_id(1)
    step, steps = pair * 2 + block, pl.num_programs(0) * 2
    slot = lax.rem(step, 2)

    def fetch(at, into):
        for r in range(8):

            @pl.when(source_ref[first * 2 + at] == r)
            def _():
                pltpu.make_async_copy(sources[r], right.at[into], sems.at[into]).start()

    @pl.when(step == 0)
    def _():
        fetch(0, 0)
        unit[...] = jnp.zeros_like(unit)

    @pl.when(step + 1 < steps)
    def _():
        fetch(step + 1, 1 - slot)

    pltpu.make_async_copy(sources[0], right.at[slot], sems.at[slot]).wait()
    ladder = lax.dot_general(
        half_ref[0, 0],
        right[slot, 0:W, :],
        (((1,), (1,)), ((), ())),
        preferred_element_type=F32,
    )
    tile = int_ref[0, 0].astype(F32) + ladder
    far_ref[0, 0] = right[slot, W:TALL, 0:W].astype(F32)

    @pl.when(block == 0)
    def _():
        put_tile(unit, 0, tile)

    @pl.when(block == 1)
    def _():
        put_tile(unit, 1, tile)
        for j in range(4):
            out_ref[j, 0] = unit[j * PIECE : (j + 1) * PIECE, :].astype(BF)


def residual_units(first, count, source, half_done, integrals, blocks):
    return pl.pallas_call(
        functools.partial(ladder_kernel, first),
        out_shape=(
            jax.ShapeDtypeStruct((4, count, PIECE, 128), BF),
            jax.ShapeDtypeStruct((count, 2, TALL - W, W), F32),
        ),
        grid_spec=pltpu.PrefetchScalarGridSpec(
            num_scalar_prefetch=1,
            grid=(count, 2),
            in_specs=[
                pl.BlockSpec((1, 1, W, DEEP), lambda p, b, s: (first + p, b, 0, 0)),
                pl.BlockSpec((1, 1, W, W), lambda p, b, s: (first + p, b, 0, 0)),
            ]
            + [pl.BlockSpec(memory_space=pl.ANY)] * 8,
            out_specs=[
                pl.BlockSpec((4, 1, PIECE, 128), lambda p, b, s: (0, p, 0, 0)),
                pl.BlockSpec((1, 1, TALL - W, W), lambda p, b, s: (p, b, 0, 0)),
            ],
            scratch_shapes=[
                pltpu.VMEM((2, TALL, DEEP), BF),
                pltpu.VMEM((UNIT, 128), F32),
                pltpu.SemaphoreType.DMA((2,)),
            ],
        ),
        compiler_params=params("arbitrary", "arbitrary"),
        cost_estimate=pl.CostEstimate(
            flops=4 * count * NQ * W**3, bytes_accessed=count * 2 * 2_700_000, transcendentals=0
        ),
    )(source, half_done, integrals, *blocks)


def update_kernel(
    slot_ref, flip_ref, pair_ref, amp_ref, own_a, own_b, far_a, far_b, mir_a, mir_b, near_ref, out_ref
):
    p = pl.program_id(0)

    def unit(low, high, use_low):
        rows = [jnp.where(use_low, low[j, 0].astype(F32), high[j, 0].astype(F32)) for j in range(4)]
        return jnp.concatenate(rows, axis=0)

    own = unit(own_a, own_b, p < 2)
    other = unit(mir_a, mir_b, slot_ref[p] < 2)
    straight = flip_ref[p] == 0
    tiles = [get_tile(other, b) for b in range(2)]
    for b in range(2):
        mirror = jnp.where(straight, tiles[b], tiles[1 - b])
        square = jnp.pad(mirror, ((0, 56), (0, 56)))
        symmetric = get_tile(own, b) + square.T[0:W, 0:W]
        far = jnp.where(p < 2, far_a[0, b, 0:1, :], far_b[0, b, 0:1, :])
        denominator = pair_ref[p] - near_ref[b] - far
        out_ref[0, b] = (amp_ref[0, b].astype(F32) + symmetric / denominator).astype(BF)


def update(slot, flip, pair_energy, amplitudes, own_a, own_b, far_a, far_b, mir_a, mir_b, near):
    pairs = amplitudes.shape[0]
    low = lambda p, s, f, e: (0, jnp.minimum(p, 1), 0, 0)
    high = lambda p, s, f, e: (0, jnp.maximum(p - 2, 0), 0, 0)
    low_far = lambda p, s, f, e: (jnp.minimum(p, 1), 0, 0, 0)
    high_far = lambda p, s, f, e: (jnp.maximum(p - 2, 0), 0, 0, 0)
    pick = lambda p, s, f, e: (0, jnp.bitwise_and(s[p], 1), 0, 0)
    own = lambda p, s, f, e: (p, 0, 0, 0)
    unit = (4, 1, PIECE, 128)
    return pl.pallas_call(
        update_kernel,
        out_shape=jax.ShapeDtypeStruct((pairs, 2, W, W), BF),
        grid_spec=pltpu.PrefetchScalarGridSpec(
            num_scalar_prefetch=3,
            grid=(pairs,),
            in_specs=[
                pl.BlockSpec((1, 2, W, W), own),
                pl.BlockSpec(unit, low),
                pl.BlockSpec(unit, high),
                pl.BlockSpec((1, 2, TALL - W, W), low_far),
                pl.BlockSpec((1, 2, TALL - W, W), high_far),
                pl.BlockSpec(unit, pick),
                pl.BlockSpec(unit, pick),
                pl.BlockSpec((2, W, 1), lambda p, s, f, e: (0, 0, 0)),
            ],
            out_specs=pl.BlockSpec((1, 2, W, W), own),
        ),
        compiler_params=params("arbitrary"),
    )(slot, flip, pair_energy, amplitudes, own_a, own_b, far_a, far_b, mir_a, mir_b, near)


def across_virt(units, step):
    scattered = lax.all_to_all(units, "virt", 0, 0, tiled=True)
    index = jnp.bitwise_xor(jnp.arange(4, dtype=jnp.int32)[:, None], step[None, :])
    chosen = scattered[index, jnp.arange(units.shape[1], dtype=jnp.int32)[None, :]]
    return lax.all_to_all(chosen, "virt", 0, 0, tiled=True)


def on_device(
    amplitudes, integrals, ladder_slab, pair_list, mirror_slot, occ_irrep, occ_energy, virt_energy
):
    pairs = amplitudes.shape[0]
    amp = amplitudes.reshape(pairs, 2, W, W)
    ints = integrals.reshape(pairs, 2, W, W)
    slab = ladder_slab.reshape(NQ, 2, W, W)
    energy = virt_energy.reshape(2, 1, W)
    core = lax.rem(lax.axis_index("pair"), 2).astype(jnp.int32)
    virt = lax.axis_index("virt").astype(jnp.int32)

    one, two = pack_slab(slab, energy, core[None]), pack_slab(slab, energy, 1 - core[None])
    near_one = along_y(one)
    near_two = along_y(two)
    far_one = along_y(near_one)
    half_done = first_half(slab, amp)
    blocks = (
        one,
        two,
        near_one,
        near_two,
        swap_cores(near_one),
        swap_cores(near_two),
        far_one,
        swap_cores(far_one),
    )

    irrep = jnp.bitwise_xor(occ_irrep[pair_list[:, 0]], occ_irrep[pair_list[:, 1]])
    step, flip = jnp.right_shift(irrep, 1), jnp.bitwise_and(irrep, 1)
    apart = jnp.bitwise_and(jnp.bitwise_xor(virt, step) - virt, 3)[:, None]
    second = (jnp.bitwise_xor(jnp.arange(2)[None, :], flip[:, None]) != core).astype(jnp.int32)
    mine = 2 + second
    theirs = 5 - second
    source = jnp.where(
        apart == 0,
        second,
        jnp.where(apart == 2, 6 + second, jnp.where(apart == 3 - 2 * core, mine, theirs)),
    ).reshape(-1)

    unit_a, far_a = residual_units(0, 2, source, half_done, ints, blocks)
    unit_b, far_b = residual_units(2, 2, source, half_done, ints, blocks)
    slots = jnp.arange(pairs, dtype=jnp.int32)
    mirror_step = jnp.sum(
        jnp.where(mirror_slot[:, None] == slots[None, :], step[:, None], 0), axis=0
    )
    mir_a = to_mirror(unit_a)
    mir_b = to_mirror(across_virt(unit_b, step[2:4]))
    mir_a = across_virt(mir_a, mirror_step[0:2])
    pair_energy = occ_energy[pair_list[:, 0]] + occ_energy[pair_list[:, 1]]
    near = virt_energy.astype(F32).reshape(2, W, 1)
    new = update(
        mirror_slot, flip, pair_energy, amp, unit_a, unit_b, far_a, far_b, mir_a, mir_b, near
    )
    return new.reshape(amplitudes.shape)


def solution(mesh):
    return jax.shard_map(
        on_device,
        mesh=mesh,
        in_specs=(
            P("pair", "virt", None),
            P("pair", "virt", None),
            P(None, "virt", None),
            P("pair", None),
            P("pair"),
            P(),
            P(),
            P("virt"),
        ),
        out_specs=P("pair", "virt", None),
        check_vma=False,
    )
```

```python
import functools

import jax
import jax.numpy as jnp
from jax import lax
from jax.experimental import pallas as pl
from jax.experimental.pallas import tpu as pltpu
from jax.sharding import PartitionSpec as P

W = 200
NQ = 16
DEEP = NQ * W
TALL = 208
PIECE = 160
UNIT = 4 * PIECE
BF = jnp.bfloat16
F32 = jnp.float32
VMEM_LIMIT = 56 * 1024 * 1024


def permute(value, move):
    layers, halves, width, cores, lines = lax.axis_size("pair") // 16, 2, 4, 2, 4
    pairs = []
    for z in range(layers):
        for y in range(halves * lines):
            for x in range(width):
                for core in range(cores):
                    ends = []
                    for tz, ty, tx, tc in ((z, y, x, core), move(z, y, x, core)):
                        tz, ty, tx, tc = tz % layers, ty % (halves * lines), tx % width, tc % cores
                        pair = ((tz * halves + ty // lines) * width + tx) * cores + tc
                        ends.append(pair * lines + ty % lines)
                    pairs.append(tuple(ends))
    return lax.ppermute(value, ("pair", "virt"), pairs)


def along_y(value):
    return permute(value, lambda z, y, x, core: (z, y + 1 - 2 * core, x, core))


def swap_cores(value):
    return permute(value, lambda z, y, x, core: (z, y, x, 1 - core))


def to_mirror(value):
    half = lax.axis_size("pair") // 32
    return permute(value, lambda z, y, x, core: (z + half, y, x, core))


def together(*values):
    return lax.optimization_barrier(values)


def params(*semantics):
    return pltpu.CompilerParams(
        dimension_semantics=semantics, vmem_limit_bytes=VMEM_LIMIT
    )


def pack_kernel(order_ref, slab_ref, energy_ref, out_ref):
    for q in range(NQ):
        out_ref[0:W, q * W : (q + 1) * W] = slab_ref[q, 0]
    both = jnp.broadcast_to(energy_ref[...].reshape(1, 2 * W), (TALL - W, 2 * W))
    out_ref[W:TALL, 0:W] = jnp.where(order_ref[0] == 0, both[:, 0:W], both[:, W : 2 * W])
    out_ref[W:TALL, W:DEEP] = jnp.zeros((TALL - W, DEEP - W), BF)


def pack_slab(slab, energy, block):
    return pl.pallas_call(
        pack_kernel,
        out_shape=jax.ShapeDtypeStruct((TALL, DEEP), BF),
        grid_spec=pltpu.PrefetchScalarGridSpec(
            num_scalar_prefetch=1,
            grid=(1,),
            in_specs=[
                pl.BlockSpec((NQ, 1, W, W), lambda i, order: (0, order[0], 0, 0)),
                pl.BlockSpec((2 * W,), lambda i, order: (0,)),
            ],
            out_specs=pl.BlockSpec((TALL, DEEP), lambda i, order: (0, 0)),
        ),
        compiler_params=params("arbitrary"),
        cost_estimate=pl.CostEstimate(flops=0, bytes_accessed=3_000_000, transcendentals=0),
    )(block, slab, energy)


def half_kernel(slab_ref, amp_ref, out_ref):
    for q in range(NQ):
        out_ref[0, :, q * W : (q + 1) * W] = jnp.dot(
            slab_ref[q, 0], amp_ref[0, 0], preferred_element_type=F32
        ).astype(BF)


def first_half(slab, amplitudes, block):
    pairs = amplitudes.shape[0]
    return pl.pallas_call(
        half_kernel,
        out_shape=jax.ShapeDtypeStruct((pairs, W, DEEP), BF),
        grid=(pairs,),
        in_specs=[
            pl.BlockSpec((NQ, 1, W, W), lambda p: (0, block, 0, 0)),
            pl.BlockSpec((1, 1, W, W), lambda p: (p, block, 0, 0)),
        ],
        out_specs=pl.BlockSpec((1, W, DEEP), lambda p: (p, 0, 0)),
        compiler_params=params("arbitrary"),
        cost_estimate=pl.CostEstimate(
            flops=2 * pairs * NQ * W**3, bytes_accessed=9_000_000, transcendentals=0
        ),
    )(slab, amplitudes)


def put_tile(unit_ref, block, tile):
    unit_ref[block * W : (block + 1) * W, :] = tile[:, 0:128]
    unit_ref[2 * W : 3 * W, block * 64 : (block + 1) * 64] = tile[:, 128:192]
    base = 3 * W + 16 * block
    for c in range(13):
        rows = min(16, W - 16 * c)
        unit_ref[base : base + rows, 8 * c : 8 * c + 8] = tile[16 * c : 16 * c + rows, 192:200]


def get_tile(unit, block):
    base = 3 * W + 16 * block
    tail = [
        unit[base : base + min(16, W - 16 * c), 8 * c : 8 * c + 8] for c in range(13)
    ]
    return jnp.concatenate(
        [
            unit[block * W : (block + 1) * W, :],
            unit[2 * W : 3 * W, block * 64 : (block + 1) * 64],
            jnp.concatenate(tail, axis=0),
        ],
        axis=1,
    )


def ladder_kernel(first, count, source_ref, int_ref, half_zero, half_one, *refs):
    sources, (out_ref, own_ref, far_ref, right, left, unit, sems) = refs[:8], refs[8:]
    halves = (half_zero, half_one)

    for t in range(2 * count):
        pltpu.make_async_copy(halves[t % 2].at[first + t // 2], left.at[t], sems.at[0, t]).start()
        for r in range(8):

            @pl.when(source_ref[first * 2 + t] == r)
            def _():
                pltpu.make_async_copy(sources[r], right.at[t], sems.at[1, t]).start()

    unit[3 * W : UNIT, :] = jnp.zeros((UNIT - 3 * W, 128), F32)
    for t in range(2 * count):
        pair, block = t // 2, t % 2
        pltpu.make_async_copy(halves[0].at[first], left.at[t], sems.at[0, t]).wait()
        pltpu.make_async_copy(sources[0], right.at[t], sems.at[1, t]).wait()
        ladder = lax.dot_general(
            left[t], right[t, 0:W, :], (((1,), (1,)), ((), ())), preferred_element_type=F32
        )
        tile = int_ref[pair, block].astype(F32) + ladder
        own_ref[pair, block] = tile.astype(BF)
        far_ref[pair, block] = right[t, W:TALL, 0:W].astype(F32)
        put_tile(unit, block, tile)
        if block == 1:
            for j in range(4):
                out_ref[j, pair] = unit[j * PIECE : (j + 1) * PIECE, :].astype(BF)


def residual_units(first, count, source, halves, integrals, blocks):
    return pl.pallas_call(
        functools.partial(ladder_kernel, first, count),
        out_shape=(
            jax.ShapeDtypeStruct((4, count, PIECE, 128), BF),
            jax.ShapeDtypeStruct((count, 2, W, W), BF),
            jax.ShapeDtypeStruct((count, 2, TALL - W, W), F32),
        ),
        grid_spec=pltpu.PrefetchScalarGridSpec(
            num_scalar_prefetch=1,
            grid=(1,),
            in_specs=[pl.BlockSpec((count, 2, W, W), lambda i, s: (first // count, 0, 0, 0))]
            + [pl.BlockSpec(memory_space=pl.ANY)] * 10,
            out_specs=[
                pl.BlockSpec((4, count, PIECE, 128), lambda i, s: (0, 0, 0, 0)),
                pl.BlockSpec((count, 2, W, W), lambda i, s: (0, 0, 0, 0)),
                pl.BlockSpec((count, 2, TALL - W, W), lambda i, s: (0, 0, 0, 0)),
            ],
            scratch_shapes=[
                pltpu.VMEM((2 * count, TALL, DEEP), BF),
                pltpu.VMEM((2 * count, W, DEEP), BF),
                pltpu.VMEM((UNIT, 128), F32),
                pltpu.SemaphoreType.DMA((2, 2 * count)),
            ],
        ),
        compiler_params=params("arbitrary"),
        cost_estimate=pl.CostEstimate(
            flops=4 * count * NQ * W**3, bytes_accessed=count * 2 * 2_700_000, transcendentals=0
        ),
    )(source, integrals, *halves, *blocks)


def update_kernel(
    slot_ref, flip_ref, pair_ref, amp_ref, own_a, own_b, far_a, far_b, mir_a, mir_b, near_ref, out_ref
):
    p = pl.program_id(0)
    low = slot_ref[p] < 2
    other = jnp.concatenate(
        [jnp.where(low, mir_a[j, 0].astype(F32), mir_b[j, 0].astype(F32)) for j in range(4)], axis=0
    )
    straight = flip_ref[p] == 0
    tiles = [get_tile(other, b) for b in range(2)]
    for b in range(2):
        mirror = jnp.where(straight, tiles[b], tiles[1 - b])
        square = jnp.pad(mirror, ((0, 56), (0, 56)))
        own = jnp.where(p < 2, own_a[0, b].astype(F32), own_b[0, b].astype(F32))
        symmetric = own + square.T[0:W, 0:W]
        far = jnp.where(p < 2, far_a[0, b, 0:1, :], far_b[0, b, 0:1, :])
        denominator = pair_ref[p] - near_ref[b] - far
        out_ref[0, b] = (amp_ref[0, b].astype(F32) + symmetric / denominator).astype(BF)


def update(slot, flip, pair_energy, amplitudes, own_a, own_b, far_a, far_b, mir_a, mir_b, near):
    pairs = amplitudes.shape[0]
    low = lambda p, s, f, e: (jnp.minimum(p, 1), 0, 0, 0)
    high = lambda p, s, f, e: (jnp.maximum(p - 2, 0), 0, 0, 0)
    pick = lambda p, s, f, e: (0, jnp.bitwise_and(s[p], 1), 0, 0)
    own = lambda p, s, f, e: (p, 0, 0, 0)
    return pl.pallas_call(
        update_kernel,
        out_shape=jax.ShapeDtypeStruct((pairs, 2, W, W), BF),
        grid_spec=pltpu.PrefetchScalarGridSpec(
            num_scalar_prefetch=3,
            grid=(pairs,),
            in_specs=[
                pl.BlockSpec((1, 2, W, W), own),
                pl.BlockSpec((1, 2, W, W), low),
                pl.BlockSpec((1, 2, W, W), high),
                pl.BlockSpec((1, 2, TALL - W, W), low),
                pl.BlockSpec((1, 2, TALL - W, W), high),
                pl.BlockSpec((4, 1, PIECE, 128), pick),
                pl.BlockSpec((4, 1, PIECE, 128), pick),
                pl.BlockSpec((2, W, 1), lambda p, s, f, e: (0, 0, 0)),
            ],
            out_specs=pl.BlockSpec((1, 2, W, W), own),
        ),
        compiler_params=params("arbitrary"),
    )(slot, flip, pair_energy, amplitudes, own_a, own_b, far_a, far_b, mir_a, mir_b, near)


def across_virt(units, step):
    scattered = lax.all_to_all(units, "virt", 0, 0, tiled=True)
    index = jnp.bitwise_xor(jnp.arange(4, dtype=jnp.int32)[:, None], step[None, :])
    chosen = scattered[index, jnp.arange(units.shape[1], dtype=jnp.int32)[None, :]]
    return lax.all_to_all(chosen, "virt", 0, 0, tiled=True)


def on_device(
    amplitudes, integrals, ladder_slab, pair_list, mirror_slot, occ_irrep, occ_energy, virt_energy
):
    pairs = amplitudes.shape[0]
    amp = amplitudes.reshape(pairs, 2, W, W)
    ints = integrals.reshape(pairs, 2, W, W)
    slab = ladder_slab.reshape(NQ, 2, W, W)
    core = lax.rem(lax.axis_index("pair"), 2).astype(jnp.int32)
    virt = lax.axis_index("virt").astype(jnp.int32)

    irrep = jnp.bitwise_xor(occ_irrep[pair_list[:, 0]], occ_irrep[pair_list[:, 1]])
    step, flip = jnp.right_shift(irrep, 1), jnp.bitwise_and(irrep, 1)
    apart = jnp.bitwise_and(jnp.bitwise_xor(virt, step) - virt, 3)[:, None]
    second = (jnp.bitwise_xor(jnp.arange(2)[None, :], flip[:, None]) != core).astype(jnp.int32)
    mine = 2 + second
    theirs = 5 - second
    source = jnp.where(
        apart == 0,
        second,
        jnp.where(apart == 2, 6 + second, jnp.where(apart == 3 - 2 * core, mine, theirs)),
    ).reshape(-1)
    slots = jnp.arange(pairs, dtype=jnp.int32)
    mirror_step = jnp.sum(
        jnp.where(mirror_slot[:, None] == slots[None, :], step[:, None], 0), axis=0
    )
    pair_energy = occ_energy[pair_list[:, 0]] + occ_energy[pair_list[:, 1]]
    near = virt_energy.astype(F32).reshape(2, W, 1)

    one = pack_slab(slab, virt_energy, core[None])
    two = pack_slab(slab, virt_energy, 1 - core[None])
    near_one = along_y(one)
    near_two = along_y(two)
    half_zero = first_half(slab, amp, 0)
    near_one, half_zero, source, near = together(near_one, half_zero, source, near)
    far_one = along_y(near_one)
    swapped_one = swap_cores(near_one)
    half_one = first_half(slab, amp, 1)
    near_two, half_one, flip, mirror_step, pair_energy, step = together(
        near_two, half_one, flip, mirror_step, pair_energy, step
    )
    swapped_two = swap_cores(near_two)
    blocks = (
        one, two, near_one, near_two, swapped_one, swapped_two, far_one, swap_cores(far_one)
    )
    halves = (half_zero, half_one)

    unit_a, own_a, far_a = residual_units(0, 2, source, halves, ints, blocks)
    unit_a, source = together(unit_a, source)
    mir_a = to_mirror(unit_a)
    unit_b, own_b, far_b = residual_units(2, 2, source, halves, ints, blocks)
    crossed_b = across_virt(unit_b, step[2:4])
    mir_a, crossed_b = together(mir_a, crossed_b)
    mir_b = to_mirror(crossed_b)
    mir_a = across_virt(mir_a, mirror_step[0:2])
    new = update(
        mirror_slot, flip, pair_energy, amp, own_a, own_b, far_a, far_b, mir_a, mir_b, near
    )
    return new.reshape(amplitudes.shape)


def solution(mesh):
    return jax.shard_map(
        on_device,
        mesh=mesh,
        in_specs=(
            P("pair", "virt", None),
            P("pair", "virt", None),
            P(None, "virt", None),
            P("pair", None),
            P("pair"),
            P(),
            P(),
            P("virt"),
        ),
        out_specs=P("pair", "virt", None),
        check_vma=False,
    )
```

```python
import functools

import jax
import jax.numpy as jnp
from jax import lax
from jax.experimental import pallas as pl
from jax.experimental.pallas import tpu as pltpu
from jax.sharding import PartitionSpec as P

W = 200
NQ = 16
DEEP = NQ * W
TALL = 208
PIECE = 160
UNIT = 4 * PIECE
BF = jnp.bfloat16
F32 = jnp.float32
VMEM_LIMIT = 20 * 1024 * 1024


def permute(value, move):
    layers, halves, width, cores, lines = lax.axis_size("pair") // 16, 2, 4, 2, 4
    pairs = []
    for z in range(layers):
        for y in range(halves * lines):
            for x in range(width):
                for core in range(cores):
                    ends = []
                    for tz, ty, tx, tc in ((z, y, x, core), move(z, y, x, core)):
                        tz, ty, tx, tc = tz % layers, ty % (halves * lines), tx % width, tc % cores
                        pair = ((tz * halves + ty // lines) * width + tx) * cores + tc
                        ends.append(pair * lines + ty % lines)
                    pairs.append(tuple(ends))
    return lax.ppermute(value, ("pair", "virt"), pairs)


def along_y(value):
    return permute(value, lambda z, y, x, core: (z, y + 1 - 2 * core, x, core))


def swap_cores(value):
    return permute(value, lambda z, y, x, core: (z, y, x, 1 - core))


def to_mirror(value):
    half = lax.axis_size("pair") // 32
    return permute(value, lambda z, y, x, core: (z + half, y, x, core))


def together(*values):
    return lax.optimization_barrier(values)


def params(*semantics):
    return pltpu.CompilerParams(
        dimension_semantics=semantics, vmem_limit_bytes=VMEM_LIMIT
    )


def pack_kernel(order_ref, slab_ref, energy_ref, out_ref):
    for q in range(NQ):
        out_ref[0:W, q * W : (q + 1) * W] = slab_ref[q, 0]
    both = jnp.broadcast_to(energy_ref[...].reshape(1, 2 * W), (TALL - W, 2 * W))
    out_ref[W:TALL, 0:W] = jnp.where(order_ref[0] == 0, both[:, 0:W], both[:, W : 2 * W])
    out_ref[W:TALL, W:DEEP] = jnp.zeros((TALL - W, DEEP - W), BF)


def pack_slab(slab, energy, block):
    return pl.pallas_call(
        pack_kernel,
        out_shape=jax.ShapeDtypeStruct((TALL, DEEP), BF),
        grid_spec=pltpu.PrefetchScalarGridSpec(
            num_scalar_prefetch=1,
            grid=(1,),
            in_specs=[
                pl.BlockSpec((NQ, 1, W, W), lambda i, order: (0, order[0], 0, 0)),
                pl.BlockSpec((2 * W,), lambda i, order: (0,)),
            ],
            out_specs=pl.BlockSpec((TALL, DEEP), lambda i, order: (0, 0)),
        ),
        compiler_params=params("arbitrary"),
        cost_estimate=pl.CostEstimate(flops=0, bytes_accessed=3_000_000, transcendentals=0),
    )(block, slab, energy)


def half_kernel(slab_ref, amp_ref, out_ref):
    p = pl.program_id(0)
    for q in range(NQ):
        out_ref[p, :, q * W : (q + 1) * W] = jnp.dot(
            slab_ref[q, 0], amp_ref[0, 0], preferred_element_type=F32
        ).astype(BF)


def first_half(slab, amplitudes, block):
    pairs = amplitudes.shape[0]
    return pl.pallas_call(
        half_kernel,
        out_shape=pltpu.VMEM((pairs, W, DEEP), BF),
        grid=(pairs,),
        in_specs=[
            pl.BlockSpec((NQ, 1, W, W), lambda p: (0, block, 0, 0)),
            pl.BlockSpec((1, 1, W, W), lambda p: (p, block, 0, 0)),
        ],
        out_specs=pl.BlockSpec(memory_space=pltpu.VMEM),
        compiler_params=params("arbitrary"),
        cost_estimate=pl.CostEstimate(
            flops=2 * pairs * NQ * W**3, bytes_accessed=9_000_000, transcendentals=0
        ),
    )(slab, amplitudes)


def put_tile(unit_ref, block, tile):
    unit_ref[block * W : (block + 1) * W, :] = tile[:, 0:128]
    unit_ref[2 * W : 3 * W, block * 64 : (block + 1) * 64] = tile[:, 128:192]
    base = 3 * W + 16 * block
    for c in range(13):
        rows = min(16, W - 16 * c)
        unit_ref[base : base + rows, 8 * c : 8 * c + 8] = tile[16 * c : 16 * c + rows, 192:200]


def get_tile(unit, block):
    base = 3 * W + 16 * block
    tail = [
        unit[base : base + min(16, W - 16 * c), 8 * c : 8 * c + 8] for c in range(13)
    ]
    return jnp.concatenate(
        [
            unit[block * W : (block + 1) * W, :],
            unit[2 * W : 3 * W, block * 64 : (block + 1) * 64],
            jnp.concatenate(tail, axis=0),
        ],
        axis=1,
    )


def ladder_kernel(source_ref, int_ref, *refs):
    halves, sources, (low_ref, high_ref, late_ref, own_ref, far_ref, unit, sums) = (
        refs[:2], refs[2:10], refs[10:]
    )
    pairs = int_ref.shape[0]

    @pl.loop(0, pairs)
    def _(p):
        for block in range(2):
            for r in range(8):

                @pl.when(source_ref[2 * p + block] == r)
                def _():
                    sums[2 * p + block] = lax.dot_general(
                        halves[block][p],
                        sources[r][0:W, :],
                        (((1,), (1,)), ((), ())),
                        preferred_element_type=F32,
                    )
                    far_ref[p, block] = sources[r][W:TALL, 0:W].astype(F32)

    unit[3 * W : UNIT, :] = jnp.zeros((UNIT - 3 * W, 128), F32)
    for p in range(pairs):
        for block in range(2):
            tile = int_ref[p, block].astype(F32) + sums[2 * p + block]
            own_ref[p, block] = tile.astype(BF)
            put_tile(unit, block, tile)
        for j in range(4):
            piece = unit[j * PIECE : (j + 1) * PIECE, :].astype(BF)
            if p >= 2:
                late_ref[j, p - 2] = piece
            elif j < 2:
                low_ref[j, p] = piece
            else:
                high_ref[j - 2, p] = piece


def residual_units(source, halves, integrals, blocks):
    pairs = integrals.shape[0]
    whole = pl.BlockSpec(memory_space=pltpu.VMEM)
    held = [pltpu.with_memory_space_constraint(x, pltpu.VMEM) for x in (*halves, *blocks)]
    return pl.pallas_call(
        ladder_kernel,
        out_shape=(
            jax.ShapeDtypeStruct((2, 2, PIECE, 128), BF),
            jax.ShapeDtypeStruct((2, 2, PIECE, 128), BF),
            jax.ShapeDtypeStruct((4, 2, PIECE, 128), BF),
            jax.ShapeDtypeStruct((pairs, 2, W, W), BF),
            jax.ShapeDtypeStruct((pairs, 2, TALL - W, W), F32),
        ),
        in_specs=[pl.BlockSpec(memory_space=pltpu.SMEM)] + [whole] * 11,
        out_specs=[whole] * 5,
        scratch_shapes=[
            pltpu.VMEM((UNIT, 128), F32),
            pltpu.VMEM((2 * pairs, W, W), F32),
        ],
        compiler_params=params(),
        cost_estimate=pl.CostEstimate(
            flops=4 * pairs * NQ * W**3, bytes_accessed=5_000_000, transcendentals=0
        ),
    )(source, integrals, *held)


def update_kernel(
    slot_ref, flip_ref, pair_ref, amp_ref, own_ref, far_ref, mir_a, low_b, high_b, near_ref, out_ref
):
    p = pl.program_id(0)
    first = slot_ref[p] < 2
    mir_b = (low_b.at[0, 0], low_b.at[1, 0], high_b.at[0, 0], high_b.at[1, 0])
    other = jnp.concatenate(
        [
            jnp.where(first, mir_a[j, 0].astype(F32), mir_b[j][...].astype(F32))
            for j in range(4)
        ],
        axis=0,
    )
    straight = flip_ref[p] == 0
    tiles = [get_tile(other, b) for b in range(2)]
    for b in range(2):
        mirror = jnp.where(straight, tiles[b], tiles[1 - b])
        square = jnp.pad(mirror, ((0, 56), (0, 56)))
        symmetric = own_ref[0, b].astype(F32) + square.T[0:W, 0:W]
        denominator = pair_ref[p] - near_ref[b] - far_ref[0, b, 0:1, :]
        out_ref[0, b] = (amp_ref[0, b].astype(F32) + symmetric / denominator).astype(BF)


def update(slot, flip, pair_energy, amplitudes, own, far, mir_a, low_b, high_b, near):
    pairs = amplitudes.shape[0]
    pick = lambda p, s, f, e: (0, jnp.bitwise_and(s[p], 1), 0, 0)
    here = lambda p, s, f, e: (p, 0, 0, 0)
    return pl.pallas_call(
        update_kernel,
        out_shape=jax.ShapeDtypeStruct((pairs, 2, W, W), BF),
        grid_spec=pltpu.PrefetchScalarGridSpec(
            num_scalar_prefetch=3,
            grid=(pairs,),
            in_specs=[
                pl.BlockSpec((1, 2, W, W), here),
                pl.BlockSpec((1, 2, W, W), here),
                pl.BlockSpec((1, 2, TALL - W, W), here),
                pl.BlockSpec((4, 1, PIECE, 128), pick),
                pl.BlockSpec((2, 1, PIECE, 128), pick),
                pl.BlockSpec((2, 1, PIECE, 128), pick),
                pl.BlockSpec((2, W, 1), lambda p, s, f, e: (0, 0, 0)),
            ],
            out_specs=pl.BlockSpec((1, 2, W, W), here),
        ),
        compiler_params=params("arbitrary"),
    )(slot, flip, pair_energy, amplitudes, own, far, mir_a, low_b, high_b, near)


def exchange(units):
    return lax.all_to_all(units, "virt", 0, 0, tiled=True)


def reorder(scattered, step):
    index = jnp.bitwise_xor(jnp.arange(4, dtype=jnp.int32)[:, None], step[None, :])
    return scattered[index, jnp.arange(scattered.shape[1], dtype=jnp.int32)[None, :]]


def on_device(
    amplitudes, integrals, ladder_slab, pair_list, mirror_slot, occ_irrep, occ_energy, virt_energy
):
    pairs = amplitudes.shape[0]
    amp = amplitudes.reshape(pairs, 2, W, W)
    ints = integrals.reshape(pairs, 2, W, W)
    slab = ladder_slab.reshape(NQ, 2, W, W)
    core = lax.rem(lax.axis_index("pair"), 2).astype(jnp.int32)
    virt = lax.axis_index("virt").astype(jnp.int32)

    irrep = jnp.bitwise_xor(occ_irrep[pair_list[:, 0]], occ_irrep[pair_list[:, 1]])
    step, flip = jnp.right_shift(irrep, 1), jnp.bitwise_and(irrep, 1)
    apart = jnp.bitwise_and(jnp.bitwise_xor(virt, step) - virt, 3)[:, None]
    second = (jnp.bitwise_xor(jnp.arange(2)[None, :], flip[:, None]) != core).astype(jnp.int32)
    mine = 2 + second
    theirs = 5 - second
    source = jnp.where(
        apart == 0,
        second,
        jnp.where(apart == 2, 6 + second, jnp.where(apart == 3 - 2 * core, mine, theirs)),
    ).reshape(-1)
    slots = jnp.arange(pairs, dtype=jnp.int32)
    mirror_step = jnp.sum(
        jnp.where(mirror_slot[:, None] == slots[None, :], step[:, None], 0), axis=0
    )
    pair_energy = occ_energy[pair_list[:, 0]] + occ_energy[pair_list[:, 1]]
    near = virt_energy.astype(F32).reshape(2, W, 1)

    one = pack_slab(slab, virt_energy, core[None])
    two = pack_slab(slab, virt_energy, 1 - core[None])
    near_one = along_y(one)
    near_two = along_y(two)
    half_zero = first_half(slab, amp, 0)
    near_one, half_zero, source, near = together(near_one, half_zero, source, near)
    far_one = along_y(near_one)
    swapped_one = swap_cores(near_one)
    half_one = first_half(slab, amp, 1)
    near_two, half_one, flip, mirror_step, pair_energy, step = together(
        near_two, half_one, flip, mirror_step, pair_energy, step
    )
    swapped_two = swap_cores(near_two)
    blocks = (
        one, two, near_one, near_two, swapped_one, swapped_two, far_one, swap_cores(far_one)
    )
    halves = (half_zero, half_one)

    low_a, high_a, unit_b, own, far = residual_units(source, halves, ints, blocks)
    low_a, scattered_b = together(to_mirror(low_a), exchange(unit_b))
    crossed_b = exchange(reorder(scattered_b, step[2:4]))
    high_a, crossed_b = together(to_mirror(high_a), crossed_b)
    low_b, scattered_a = together(
        to_mirror(crossed_b[0:2]), exchange(jnp.concatenate([low_a, high_a], axis=0))
    )
    crossed_a = exchange(reorder(scattered_a, mirror_step[0:2]))
    high_b = to_mirror(crossed_b[2:4])
    new = update(
        mirror_slot, flip, pair_energy, amp, own, far, crossed_a, low_b, high_b, near
    )
    return new.reshape(amplitudes.shape)


def solution(mesh):
    return jax.shard_map(
        on_device,
        mesh=mesh,
        in_specs=(
            P("pair", "virt", None),
            P("pair", "virt", None),
            P(None, "virt", None),
            P("pair", None),
            P("pair"),
            P(),
            P(),
            P("virt"),
        ),
        out_specs=P("pair", "virt", None),
        check_vma=False,
    )
```

```python
import jax
import jax.numpy as jnp
from jax import lax
from jax.experimental import pallas as pl
from jax.experimental.pallas import tpu as pltpu
from jax.sharding import PartitionSpec as P

W = 200
NQ = 16
DEEP = NQ * W
TALL = 208
PART = 1664
PIECE = 160
UNIT = 4 * PIECE
BF = jnp.bfloat16
F32 = jnp.float32
VMEM_LIMIT = 20 * 1024 * 1024


def permute(value, move):
    layers, halves, width, cores, lines = lax.axis_size("pair") // 16, 2, 4, 2, 4
    pairs = []
    for z in range(layers):
        for y in range(halves * lines):
            for x in range(width):
                for core in range(cores):
                    ends = []
                    for tz, ty, tx, tc in ((z, y, x, core), move(z, y, x, core)):
                        tz, ty, tx, tc = tz % layers, ty % (halves * lines), tx % width, tc % cores
                        pair = ((tz * halves + ty // lines) * width + tx) * cores + tc
                        ends.append(pair * lines + ty % lines)
                    pairs.append(tuple(ends))
    return lax.ppermute(value, ("pair", "virt"), pairs)


def along_y(value):
    return permute(value, lambda z, y, x, core: (z, y + 1 - 2 * core, x, core))


def along_x(value):
    return permute(value, lambda z, y, x, core: (z, y, x + 1 - 2 * core, core))


def swap_cores(value):
    return permute(value, lambda z, y, x, core: (z, y, x, 1 - core))


def to_mirror(value):
    half = lax.axis_size("pair") // 32
    return permute(value, lambda z, y, x, core: (z + half, y, x, core))


def exchange(units):
    return lax.all_to_all(units, "virt", 0, 0, tiled=True)


def reorder(scattered, step):
    index = jnp.bitwise_xor(jnp.arange(4, dtype=jnp.int32)[:, None], step[None, :])
    return scattered[index, jnp.arange(scattered.shape[1], dtype=jnp.int32)[None, :]]


def together(*values):
    return lax.optimization_barrier(values)


def params(*semantics):
    return pltpu.CompilerParams(
        dimension_semantics=semantics or None, vmem_limit_bytes=VMEM_LIMIT
    )


def cost(flops, moved):
    return pl.CostEstimate(flops=flops, bytes_accessed=moved, transcendentals=0)


def in_vmem(*values):
    return [pltpu.with_memory_space_constraint(x, pltpu.VMEM) for x in values]


WHOLE = pl.BlockSpec(memory_space=pltpu.VMEM)
SCALARS = pl.BlockSpec(memory_space=pltpu.SMEM)


def pack_kernel(order_ref, slab_ref, energy_ref, out_ref):
    for q in range(NQ):
        out_ref[0:W, q * W : (q + 1) * W] = slab_ref[q, 0]
    both = jnp.broadcast_to(energy_ref[...].reshape(1, 2 * W), (TALL - W, 2 * W))
    out_ref[W:TALL, 0:W] = jnp.where(order_ref[0] == 0, both[:, 0:W], both[:, W : 2 * W])
    out_ref[W:TALL, W:DEEP] = jnp.zeros((TALL - W, DEEP - W), BF)


def pack_slab(slab, energy, block):
    return pl.pallas_call(
        pack_kernel,
        out_shape=jax.ShapeDtypeStruct((TALL, DEEP), BF),
        grid_spec=pltpu.PrefetchScalarGridSpec(
            num_scalar_prefetch=1,
            grid=(1,),
            in_specs=[
                pl.BlockSpec((NQ, 1, W, W), lambda i, order: (0, order[0], 0, 0)),
                pl.BlockSpec((2 * W,), lambda i, order: (0,)),
            ],
            out_specs=pl.BlockSpec((TALL, DEEP), lambda i, order: (0, 0)),
        ),
        compiler_params=params("arbitrary"),
        cost_estimate=cost(0, 3_000_000),
    )(block, slab, energy)


def put_tile(unit_ref, block, tile):
    unit_ref[block * W : (block + 1) * W, :] = tile[:, 0:128]
    unit_ref[2 * W : 3 * W, block * 64 : (block + 1) * 64] = tile[:, 128:192]
    base = 3 * W + 16 * block
    for c in range(13):
        rows = min(16, W - 16 * c)
        unit_ref[base : base + rows, 8 * c : 8 * c + 8] = tile[16 * c : 16 * c + rows, 192:200]


def get_tile(unit, block):
    base = 3 * W + 16 * block
    tail = [
        unit[base : base + min(16, W - 16 * c), 8 * c : 8 * c + 8] for c in range(13)
    ]
    return jnp.concatenate(
        [
            unit[block * W : (block + 1) * W, :],
            unit[2 * W : 3 * W, block * 64 : (block + 1) * 64],
            jnp.concatenate(tail, axis=0),
        ],
        axis=1,
    )


def whole_unit(j, *refs):
    pieces = [ref[i, j].astype(F32) for ref in refs for i in range(ref.shape[0])]
    return jnp.concatenate(pieces, axis=0)


def turned(tile):
    return jnp.pad(tile, ((0, 56), (0, 56))).T[0:W, 0:W]


def tiles_kernel(pick_ref, amp_ref, int_ref, *refs):
    *outs, unit = refs
    unit[3 * W : UNIT, :] = jnp.zeros((UNIT - 3 * W, 128), F32)
    j = pl.program_id(0)
    for kind, ref in enumerate((amp_ref, int_ref)):
        for block in range(2):
            put_tile(unit, block, ref[0, block].astype(F32))
        for i in range(4):
            piece = unit[i * PIECE : (i + 1) * PIECE, :].astype(BF)
            if len(outs) == 2:
                outs[kind][i, j] = piece
            else:
                outs[0][i, 2 * kind + j] = piece


def pack_tiles(pick, amplitudes, integrals, arrays):
    tile = pl.BlockSpec((1, 2, W, W), lambda j, pick: (pick[j], 0, 0, 0))
    shape = (4, 4 // arrays, PIECE, 128)
    return pl.pallas_call(
        tiles_kernel,
        out_shape=[jax.ShapeDtypeStruct(shape, BF)] * arrays,
        grid_spec=pltpu.PrefetchScalarGridSpec(
            num_scalar_prefetch=1,
            grid=(2,),
            in_specs=[tile, tile],
            out_specs=[pl.BlockSpec(shape, lambda j, pick: (0, 0, 0, 0))] * arrays,
            scratch_shapes=[pltpu.VMEM((UNIT, 128), F32)],
        ),
        compiler_params=params("arbitrary"),
        cost_estimate=cost(0, 1_500_000),
    )(pick, amplitudes, integrals)


def half_kernel(flip_ref, slab_ref, amp_ref, add_ref, cross_ref, half_ref, int_ref):
    @pl.loop(0, 2)
    def _(j):
        straight = flip_ref[j] == 0

        def sums(ref, at):
            local, cross = whole_unit(j, ref), whole_unit(at, cross_ref)
            tiles = [get_tile(cross, b) for b in range(2)]
            return [
                get_tile(local, b) + turned(jnp.where(straight, tiles[b], tiles[1 - b]))
                for b in range(2)
            ]

        for b, tile in enumerate(sums(add_ref, 2 + j)):
            int_ref[2 * j + b] = tile
        for b, tile in enumerate(sums(amp_ref, j)):
            both = tile.astype(BF)
            for q in range(NQ):
                half_ref[2 * j + b, :, q * W : (q + 1) * W] = jnp.dot(
                    slab_ref[q, b], both, preferred_element_type=F32
                ).astype(BF)


def first_half(flip, slab, amp, add, cross):
    return pl.pallas_call(
        half_kernel,
        out_shape=(pltpu.VMEM((4, W, DEEP), BF), pltpu.VMEM((4, W, W), F32)),
        in_specs=[SCALARS] + [WHOLE] * 4,
        out_specs=[WHOLE, WHOLE],
        compiler_params=params(),
        cost_estimate=cost(8 * NQ * W**3, 4_000_000),
    )(flip, slab, amp, add, cross)


def ladder_kernel(source_ref, core_ref, half_ref, int_ref, *refs):
    full, (near, near_x, far, far_x), (out_ref, low_ref, high_ref, table_ref, unit, sums) = (
        refs[:6], refs[6:10], refs[10:]
    )
    even = core_ref[0] == 0
    odd = core_ref[0] != 0
    split = ((even, near, far), (even, near_x, far_x), (odd, far, near), (odd, far_x, near_x))
    dims = (((1,), (1,)), ((), ()))

    @pl.loop(0, 4)
    def _(t):
        for r in range(6):

            @pl.when(source_ref[t] == r)
            def _():
                sums[t] = lax.dot_general(
                    half_ref[t], full[r][0:W, :], dims, preferred_element_type=F32
                )

        for r, (on, low, high) in enumerate(split):

            @pl.when(jnp.logical_and(on, source_ref[t] == 6 + r % 2))
            def _():
                sums[t] = lax.dot_general(
                    half_ref[t, :, 0:PART], low[0:W, :], dims, preferred_element_type=F32
                ) + lax.dot_general(
                    half_ref[t, :, PART:DEEP],
                    high[0:W, 2 * PART - DEEP : PART],
                    dims,
                    preferred_element_type=F32,
                )

    for r in range(6):
        table_ref[r] = full[r][W:TALL, 0:W].astype(F32)
    for r, (on, low, _) in enumerate(split):

        @pl.when(on)
        def _():
            table_ref[6 + r % 2] = low[W:TALL, 0:W].astype(F32)

    unit[3 * W : UNIT, :] = jnp.zeros((UNIT - 3 * W, 128), F32)
    for j in range(2):
        for b in range(2):
            put_tile(unit, b, int_ref[2 * j + b] + sums[2 * j + b])
        for i in range(4):
            piece = unit[i * PIECE : (i + 1) * PIECE, :].astype(BF)
            out_ref[i, j] = piece
            (low_ref if i < 2 else high_ref)[i % 2, j] = piece


def symmetric_units(source, core, half_done, integrals, full, parts):
    return pl.pallas_call(
        ladder_kernel,
        out_shape=(
            jax.ShapeDtypeStruct((4, 2, PIECE, 128), BF),
            jax.ShapeDtypeStruct((2, 2, PIECE, 128), BF),
            jax.ShapeDtypeStruct((2, 2, PIECE, 128), BF),
            jax.ShapeDtypeStruct((8, TALL - W, W), F32),
        ),
        in_specs=[SCALARS, SCALARS] + [WHOLE] * 12,
        out_specs=[WHOLE] * 4,
        scratch_shapes=[pltpu.VMEM((UNIT, 128), F32), pltpu.VMEM((4, W, W), F32)],
        compiler_params=params(),
        cost_estimate=cost(8 * NQ * W**3, 3_000_000),
    )(source, core, *in_vmem(half_done, integrals, *full, *parts))


def update_kernel(
    kept_ref, at_ref, flip_ref, source_ref, pair_ref,
    amp_ref, cross_ref, low_ref, high_ref, table_ref, near_ref, out_ref
):
    p = pl.program_id(0)

    def finish(block, symmetric):
        far = table_ref[source_ref[2 * p + block], 0:1, :]
        denominator = pair_ref[p] - near_ref[block] - far
        old = amp_ref[0, block].astype(F32)
        out_ref[0, block] = (old + symmetric / denominator).astype(BF)

    @pl.when(kept_ref[p] == 1)
    def _():
        unit = whole_unit(0, cross_ref)
        tiles = [get_tile(unit, b) for b in range(2)]
        straight = flip_ref[p] == 0
        for b in range(2):
            finish(b, turned(jnp.where(straight, tiles[b], tiles[1 - b])))

    @pl.when(kept_ref[p] == 0)
    def _():
        unit = whole_unit(0, low_ref, high_ref)
        for b in range(2):
            finish(b, get_tile(unit, b))


def update(kept, at, flip, source, pair_energy, amplitudes, cross, low, high, table, near):
    pairs = amplitudes.shape[0]
    pick = lambda p, k, a, f, s, e: (0, a[p], 0, 0)
    here = lambda p, k, a, f, s, e: (p, 0, 0, 0)
    fixed = lambda p, k, a, f, s, e: (0, 0, 0)
    return pl.pallas_call(
        update_kernel,
        out_shape=jax.ShapeDtypeStruct((pairs, 2, W, W), BF),
        grid_spec=pltpu.PrefetchScalarGridSpec(
            num_scalar_prefetch=5,
            grid=(pairs,),
            in_specs=[
                pl.BlockSpec((1, 2, W, W), here),
                pl.BlockSpec((4, 1, PIECE, 128), pick),
                pl.BlockSpec((2, 1, PIECE, 128), pick),
                pl.BlockSpec((2, 1, PIECE, 128), pick),
                pl.BlockSpec((8, TALL - W, W), fixed),
                pl.BlockSpec((2, W, 1), fixed),
            ],
            out_specs=pl.BlockSpec((1, 2, W, W), here),
        ),
        compiler_params=params("arbitrary"),
    )(kept, at, flip, source, pair_energy, amplitudes, cross, low, high, table, near)


def on_device(
    amplitudes, integrals, ladder_slab, pair_list, mirror_slot, occ_irrep, occ_energy, virt_energy
):
    pairs = amplitudes.shape[0]
    amp = amplitudes.reshape(pairs, 2, W, W)
    ints = integrals.reshape(pairs, 2, W, W)
    slab = ladder_slab.reshape(NQ, 2, W, W)
    place = lax.axis_index("pair").astype(jnp.int32)
    virt = lax.axis_index("virt").astype(jnp.int32)
    core = jnp.bitwise_and(place, 1)
    parity = jnp.bitwise_and(jnp.right_shift(place, 1), 1)
    upper = (place >= lax.axis_size("pair") // 2).astype(jnp.int32)

    slots = jnp.arange(pairs, dtype=jnp.int32)
    label = jnp.where(upper == 0, slots, mirror_slot)
    kept = (jnp.right_shift(label, 1) == upper).astype(jnp.int32)
    at = jnp.bitwise_and(label, 1)

    def among(values, group):
        chosen = label[:, None] == jnp.arange(2, dtype=jnp.int32)[None, :] + 2 * group
        return jnp.sum(jnp.where(chosen, values[:, None], 0), axis=0)

    keep, send = among(slots, upper), among(slots, 1 - upper)

    one = pack_slab(slab, virt_energy, parity[None])
    y_one = along_y(one)
    sent_amp, sent_int = pack_tiles(send, amp, ints, 2)
    local_amp = to_mirror(sent_amp)
    scattered = exchange(pack_tiles(keep, amp, ints, 1)[0])

    irrep = jnp.bitwise_xor(occ_irrep[pair_list[:, 0]], occ_irrep[pair_list[:, 1]])
    step, flip = jnp.right_shift(irrep, 1), jnp.bitwise_and(irrep, 1)
    keep_step, keep_flip = among(step, upper), among(flip, upper)
    pair_energy = occ_energy[pair_list[:, 0]] + occ_energy[pair_list[:, 1]]
    near = virt_energy.astype(F32).reshape(2, W, 1)

    def sources(step, flip):
        apart = jnp.bitwise_and(jnp.bitwise_xor(virt, step) - virt, 3)[:, None]
        second = (jnp.bitwise_xor(jnp.arange(2)[None, :], flip[:, None]) != parity).astype(jnp.int32)
        side = jnp.where(apart == 3 - 2 * core, 2, 4)
        start = jnp.where(apart == 0, 0, jnp.where(apart == 2, 6, side))
        return (start + second).reshape(-1)

    y_one, local_amp, scattered, sent_int = together(y_one, local_amp, scattered, sent_int)
    x_one = along_x(y_one)
    y_far = along_y(lax.dynamic_slice(y_one, (0, core * (DEEP - PART)), (TALL, PART)))
    local_int = to_mirror(sent_int)
    cross = exchange(reorder(scattered, jnp.concatenate([keep_step, keep_step])))
    swapped = swap_cores(y_one)
    two = pack_slab(slab, virt_energy, 1 - parity[None])
    x_far = along_x(y_far)
    x_one, local_int, two, cross = together(x_one, local_int, two, cross)
    full = (one, two, y_one, x_one, swapped, swap_cores(x_one))
    parts = (y_far, x_far, swap_cores(y_far), swap_cores(x_far))

    half_done, both_ints = first_half(keep_flip, slab, local_amp, local_int, cross)
    result, low, high, table = symmetric_units(
        sources(keep_step, keep_flip), core[None], half_done, both_ints, full, parts
    )
    low, scattered = together(to_mirror(low), exchange(result))
    crossed = exchange(reorder(scattered, keep_step))
    high = to_mirror(high)
    new = update(
        kept, at, flip, sources(step, flip), pair_energy, amp, crossed, low, high, table, near
    )
    return new.reshape(amplitudes.shape)


def solution(mesh):
    return jax.shard_map(
        on_device,
        mesh=mesh,
        in_specs=(
            P("pair", "virt", None),
            P("pair", "virt", None),
            P(None, "virt", None),
            P("pair", None),
            P("pair"),
            P(),
            P(),
            P("virt"),
        ),
        out_specs=P("pair", "virt", None),
        check_vma=False,
    )
```

```python
import jax
import jax.numpy as jnp
from jax import lax
from jax.experimental import pallas as pl
from jax.experimental.pallas import tpu as pltpu
from jax.sharding import PartitionSpec as P

W = 200
NQ = 16
DEEP = NQ * W
TALL = 208
PART = 1664
PIECE = 160
UNIT = 4 * PIECE
BF = jnp.bfloat16
F32 = jnp.float32
VMEM_LIMIT = 20 * 1024 * 1024


def permute(value, move):
    layers, halves, width, cores, lines = lax.axis_size("pair") // 16, 2, 4, 2, 4
    pairs = []
    for z in range(layers):
        for y in range(halves * lines):
            for x in range(width):
                for core in range(cores):
                    ends = []
                    for tz, ty, tx, tc in ((z, y, x, core), move(z, y, x, core)):
                        tz, ty, tx, tc = tz % layers, ty % (halves * lines), tx % width, tc % cores
                        pair = ((tz * halves + ty // lines) * width + tx) * cores + tc
                        ends.append(pair * lines + ty % lines)
                    pairs.append(tuple(ends))
    return lax.ppermute(value, ("pair", "virt"), pairs)


def along_y(value):
    return permute(value, lambda z, y, x, core: (z, y + 1 - 2 * core, x, core))


def along_x(value):
    return permute(value, lambda z, y, x, core: (z, y, x + 1 - 2 * core, core))


def swap_cores(value):
    return permute(value, lambda z, y, x, core: (z, y, x, 1 - core))


def to_mirror(value):
    half = lax.axis_size("pair") // 32
    return permute(value, lambda z, y, x, core: (z + half, y, x, core))


def exchange(units):
    return lax.all_to_all(units, "virt", 0, 0, tiled=True)


def reorder(scattered, step):
    index = jnp.bitwise_xor(jnp.arange(4, dtype=jnp.int32)[:, None], step[None, :])
    return scattered[index, jnp.arange(scattered.shape[1], dtype=jnp.int32)[None, :]]


def together(*values):
    return lax.optimization_barrier(values)


def as_unit(ready, work, *values):
    def empty(*values):
        return jax.tree.map(lambda x: jnp.zeros(x.shape, x.dtype), jax.eval_shape(work, *values))

    return lax.cond(ready, work, empty, *values)


def params(*semantics):
    return pltpu.CompilerParams(
        dimension_semantics=semantics or None, vmem_limit_bytes=VMEM_LIMIT
    )


def cost(flops, moved):
    return pl.CostEstimate(flops=flops, bytes_accessed=moved, transcendentals=0)


def in_vmem(*values):
    return [pltpu.with_memory_space_constraint(x, pltpu.VMEM) for x in values]


WHOLE = pl.BlockSpec(memory_space=pltpu.VMEM)
SCALARS = pl.BlockSpec(memory_space=pltpu.SMEM)


def pack_kernel(order_ref, slab_ref, energy_ref, out_ref):
    for q in range(NQ):
        out_ref[0:W, q * W : (q + 1) * W] = slab_ref[q, 0]
    both = jnp.broadcast_to(energy_ref[...].reshape(1, 2 * W), (TALL - W, 2 * W))
    out_ref[W:TALL, 0:W] = jnp.where(order_ref[0] == 0, both[:, 0:W], both[:, W : 2 * W])
    out_ref[W:TALL, W:DEEP] = jnp.zeros((TALL - W, DEEP - W), BF)


def pack_slab(slab, energy, block):
    return pl.pallas_call(
        pack_kernel,
        out_shape=jax.ShapeDtypeStruct((TALL, DEEP), BF),
        grid_spec=pltpu.PrefetchScalarGridSpec(
            num_scalar_prefetch=1,
            grid=(1,),
            in_specs=[
                pl.BlockSpec((NQ, 1, W, W), lambda i, order: (0, order[0], 0, 0)),
                pl.BlockSpec((2 * W,), lambda i, order: (0,)),
            ],
            out_specs=pl.BlockSpec((TALL, DEEP), lambda i, order: (0, 0)),
        ),
        compiler_params=params("arbitrary"),
        cost_estimate=cost(0, 3_000_000),
    )(block, slab, energy)


def put_tile(unit_ref, block, tile):
    unit_ref[block * W : (block + 1) * W, :] = tile[:, 0:128]
    unit_ref[2 * W : 3 * W, block * 64 : (block + 1) * 64] = tile[:, 128:192]
    base = 3 * W + 16 * block
    for c in range(13):
        rows = min(16, W - 16 * c)
        unit_ref[base : base + rows, 8 * c : 8 * c + 8] = tile[16 * c : 16 * c + rows, 192:200]


def get_tile(unit, block):
    base = 3 * W + 16 * block
    tail = [
        unit[base : base + min(16, W - 16 * c), 8 * c : 8 * c + 8] for c in range(13)
    ]
    return jnp.concatenate(
        [
            unit[block * W : (block + 1) * W, :],
            unit[2 * W : 3 * W, block * 64 : (block + 1) * 64],
            jnp.concatenate(tail, axis=0),
        ],
        axis=1,
    )


def whole_unit(j, *refs):
    pieces = [ref[i, j].astype(F32) for ref in refs for i in range(ref.shape[0])]
    return jnp.concatenate(pieces, axis=0)


def turned(tile):
    return jnp.pad(tile, ((0, 56), (0, 56))).T[0:W, 0:W]


def tiles_kernel(pick_ref, amp_ref, int_ref, *refs):
    *outs, unit = refs
    unit[3 * W : UNIT, :] = jnp.zeros((UNIT - 3 * W, 128), F32)
    j = pl.program_id(0)
    for kind, ref in enumerate((amp_ref, int_ref)):
        for block in range(2):
            put_tile(unit, block, ref[0, block].astype(F32))
        for i in range(4):
            piece = unit[i * PIECE : (i + 1) * PIECE, :].astype(BF)
            if len(outs) == 2:
                outs[kind][i, j] = piece
            else:
                outs[0][i, 2 * kind + j] = piece


def pack_tiles(pick, amplitudes, integrals, arrays):
    tile = pl.BlockSpec((1, 2, W, W), lambda j, pick: (pick[j], 0, 0, 0))
    shape = (4, 4 // arrays, PIECE, 128)
    return pl.pallas_call(
        tiles_kernel,
        out_shape=[jax.ShapeDtypeStruct(shape, BF)] * arrays,
        grid_spec=pltpu.PrefetchScalarGridSpec(
            num_scalar_prefetch=1,
            grid=(2,),
            in_specs=[tile, tile],
            out_specs=[pl.BlockSpec(shape, lambda j, pick: (0, 0, 0, 0))] * arrays,
            scratch_shapes=[pltpu.VMEM((UNIT, 128), F32)],
        ),
        compiler_params=params("arbitrary"),
        cost_estimate=cost(0, 1_500_000),
    )(pick, amplitudes, integrals)


def half_kernel(flip_ref, slab_ref, local_ref, cross_ref, half_ref, int_ref):
    @pl.loop(0, 2)
    def _(j):
        straight = flip_ref[j] == 0

        def sums(at):
            local, cross = whole_unit(at, local_ref), whole_unit(at, cross_ref)
            tiles = [get_tile(cross, b) for b in range(2)]
            return [
                get_tile(local, b) + turned(jnp.where(straight, tiles[b], tiles[1 - b]))
                for b in range(2)
            ]

        for b, tile in enumerate(sums(2 + j)):
            int_ref[2 * j + b] = tile
        for b, tile in enumerate(sums(j)):
            both = tile.astype(BF)
            for q in range(NQ):
                half_ref[2 * j + b, :, q * W : (q + 1) * W] = jnp.dot(
                    slab_ref[q, b], both, preferred_element_type=F32
                ).astype(BF)


def first_half(flip, slab, local, cross):
    return pl.pallas_call(
        half_kernel,
        out_shape=(pltpu.VMEM((4, W, DEEP), BF), pltpu.VMEM((4, W, W), F32)),
        in_specs=[SCALARS] + [WHOLE] * 3,
        out_specs=[WHOLE, WHOLE],
        compiler_params=params(),
        cost_estimate=cost(8 * NQ * W**3, 4_000_000),
    )(flip, slab, local, cross)


def ladder_kernel(source_ref, core_ref, half_ref, int_ref, *refs):
    full, (near, near_x, far, far_x), (out_ref, table_ref, unit, sums) = (
        refs[:6], refs[6:10], refs[10:]
    )
    even = core_ref[0] == 0
    odd = core_ref[0] != 0
    split = ((even, near, far), (even, near_x, far_x), (odd, far, near), (odd, far_x, near_x))
    dims = (((1,), (1,)), ((), ()))

    @pl.loop(0, 4)
    def _(t):
        for r in range(6):

            @pl.when(source_ref[t] == r)
            def _():
                sums[t] = lax.dot_general(
                    half_ref[t], full[r][0:W, :], dims, preferred_element_type=F32
                )

        for r, (on, low, high) in enumerate(split):

            @pl.when(jnp.logical_and(on, source_ref[t] == 6 + r % 2))
            def _():
                sums[t] = lax.dot_general(
                    half_ref[t, :, 0:PART], low[0:W, :], dims, preferred_element_type=F32
                ) + lax.dot_general(
                    half_ref[t, :, PART:DEEP],
                    high[0:W, 2 * PART - DEEP : PART],
                    dims,
                    preferred_element_type=F32,
                )

    for r in range(6):
        table_ref[r] = full[r][W:TALL, 0:W].astype(F32)
    for r, (on, low, _) in enumerate(split):

        @pl.when(on)
        def _():
            table_ref[6 + r % 2] = low[W:TALL, 0:W].astype(F32)

    unit[3 * W : UNIT, :] = jnp.zeros((UNIT - 3 * W, 128), F32)
    for j in range(2):
        for b in range(2):
            put_tile(unit, b, int_ref[2 * j + b] + sums[2 * j + b])
        for i in range(4):
            out_ref[i, j] = unit[i * PIECE : (i + 1) * PIECE, :].astype(BF)


def symmetric_units(source, core, half_done, integrals, full, parts):
    return pl.pallas_call(
        ladder_kernel,
        out_shape=(
            jax.ShapeDtypeStruct((4, 2, PIECE, 128), BF),
            jax.ShapeDtypeStruct((8, TALL - W, W), F32),
        ),
        in_specs=[SCALARS, SCALARS] + [WHOLE] * 12,
        out_specs=[WHOLE] * 2,
        scratch_shapes=[pltpu.VMEM((UNIT, 128), F32), pltpu.VMEM((4, W, W), F32)],
        compiler_params=params(),
        cost_estimate=cost(8 * NQ * W**3, 3_000_000),
    )(source, core, *in_vmem(half_done, integrals, *full, *parts))


def update_kernel(
    kept_ref, at_ref, flip_ref, source_ref, pair_ref,
    amp_ref, cross_ref, mirror_ref, table_ref, near_ref, out_ref
):
    p = pl.program_id(0)

    def finish(block, symmetric):
        far = table_ref[source_ref[2 * p + block], 0:1, :]
        denominator = pair_ref[p] - near_ref[block] - far
        old = amp_ref[0, block].astype(F32)
        out_ref[0, block] = (old + symmetric / denominator).astype(BF)

    @pl.when(kept_ref[p] == 1)
    def _():
        unit = whole_unit(0, cross_ref)
        tiles = [get_tile(unit, b) for b in range(2)]
        straight = flip_ref[p] == 0
        for b in range(2):
            finish(b, turned(jnp.where(straight, tiles[b], tiles[1 - b])))

    @pl.when(kept_ref[p] == 0)
    def _():
        unit = whole_unit(0, mirror_ref)
        for b in range(2):
            finish(b, get_tile(unit, b))


def update(kept, at, flip, source, pair_energy, amplitudes, cross, mirror, table, near):
    pairs = amplitudes.shape[0]
    pick = lambda p, k, a, f, s, e: (0, a[p], 0, 0)
    here = lambda p, k, a, f, s, e: (p, 0, 0, 0)
    fixed = lambda p, k, a, f, s, e: (0, 0, 0)
    return pl.pallas_call(
        update_kernel,
        out_shape=jax.ShapeDtypeStruct((pairs, 2, W, W), BF),
        grid_spec=pltpu.PrefetchScalarGridSpec(
            num_scalar_prefetch=5,
            grid=(pairs,),
            in_specs=[
                pl.BlockSpec((1, 2, W, W), here),
                pl.BlockSpec((4, 1, PIECE, 128), pick),
                pl.BlockSpec((4, 1, PIECE, 128), pick),
                pl.BlockSpec((8, TALL - W, W), fixed),
                pl.BlockSpec((2, W, 1), fixed),
            ],
            out_specs=pl.BlockSpec((1, 2, W, W), here),
        ),
        compiler_params=params("arbitrary"),
    )(kept, at, flip, source, pair_energy, amplitudes, cross, mirror, table, near)


def on_device(
    amplitudes, integrals, ladder_slab, pair_list, mirror_slot, occ_irrep, occ_energy, virt_energy
):
    pairs = amplitudes.shape[0]
    amp = amplitudes.reshape(pairs, 2, W, W)
    ints = integrals.reshape(pairs, 2, W, W)
    slab = ladder_slab.reshape(NQ, 2, W, W)
    place = lax.axis_index("pair").astype(jnp.int32)
    virt = lax.axis_index("virt").astype(jnp.int32)
    core = jnp.bitwise_and(place, 1)
    parity = jnp.bitwise_and(jnp.right_shift(place, 1), 1)
    upper = (place >= lax.axis_size("pair") // 2).astype(jnp.int32)

    slots = jnp.arange(pairs, dtype=jnp.int32)
    label = jnp.where(upper == 0, slots, mirror_slot)
    kept = (jnp.right_shift(label, 1) == upper).astype(jnp.int32)
    at = jnp.bitwise_and(label, 1)

    def among(values, group):
        chosen = label[:, None] == jnp.arange(2, dtype=jnp.int32)[None, :] + 2 * group
        return jnp.sum(jnp.where(chosen, values[:, None], 0), axis=0)

    keep, send = among(slots, upper), among(slots, 1 - upper)

    sent = pack_tiles(send, amp, ints, 1)[0]
    local = to_mirror(sent)
    ready = pair_list[0, 0] >= 0

    irrep = jnp.bitwise_xor(occ_irrep[pair_list[:, 0]], occ_irrep[pair_list[:, 1]])
    step, flip = jnp.right_shift(irrep, 1), jnp.bitwise_and(irrep, 1)
    keep_step, keep_flip = among(step, upper), among(flip, upper)
    pair_energy = occ_energy[pair_list[:, 0]] + occ_energy[pair_list[:, 1]]
    near = virt_energy.astype(F32).reshape(2, W, 1)

    def sources(step, flip):
        apart = jnp.bitwise_and(jnp.bitwise_xor(virt, step) - virt, 3)[:, None]
        second = (jnp.bitwise_xor(jnp.arange(2)[None, :], flip[:, None]) != parity).astype(jnp.int32)
        side = jnp.where(apart == 3 - 2 * core, 2, 4)
        start = jnp.where(apart == 0, 0, jnp.where(apart == 2, 6, side))
        return (start + second).reshape(-1)

    def bring(slab, virt_energy, amp, ints):
        one = pack_slab(slab, virt_energy, parity[None])
        y_one = along_y(one)
        scattered = exchange(pack_tiles(keep, amp, ints, 1)[0])
        x_one = along_x(y_one)
        y_far = along_y(lax.dynamic_slice(y_one, (0, core * (DEEP - PART)), (TALL, PART)))
        cross = exchange(reorder(scattered, jnp.concatenate([keep_step, keep_step])))
        return one, y_one, x_one, y_far, along_x(y_far), cross

    one, y_one, x_one, y_far, x_far, cross = as_unit(ready, bring, slab, virt_energy, amp, ints)
    y_one, x_one, y_far, x_far, cross, local = together(y_one, x_one, y_far, x_far, cross, local)
    two = pack_slab(slab, virt_energy, 1 - parity[None])
    full = (one, two, y_one, x_one, swap_cores(y_one), swap_cores(x_one))
    parts = (y_far, x_far, swap_cores(y_far), swap_cores(x_far))

    half_done, both_ints = first_half(keep_flip, slab, local, cross)
    result, table = symmetric_units(
        sources(keep_step, keep_flip), core[None], half_done, both_ints, full, parts
    )
    mirrored = to_mirror(result)
    crossed = as_unit(ready, lambda x: exchange(reorder(exchange(x), keep_step)), result)
    new = update(
        kept, at, flip, sources(step, flip), pair_energy, amp, crossed, mirrored, table, near
    )
    return new.reshape(amplitudes.shape)


def solution(mesh):
    return jax.shard_map(
        on_device,
        mesh=mesh,
        in_specs=(
            P("pair", "virt", None),
            P("pair", "virt", None),
            P(None, "virt", None),
            P("pair", None),
            P("pair"),
            P(),
            P(),
            P("virt"),
        ),
        out_specs=P("pair", "virt", None),
        check_vma=False,
    )
```

```python
import jax
import jax.numpy as jnp
from jax import lax
from jax.experimental import pallas as pl
from jax.experimental.pallas import tpu as pltpu
from jax.sharding import PartitionSpec as P

W = 200
NQ = 16
DEEP = NQ * W
TALL = 208
PART = 1664
PIECE = 160
UNIT = 4 * PIECE
BF = jnp.bfloat16
F32 = jnp.float32
VMEM_LIMIT = 20 * 1024 * 1024


def permute(value, move):
    layers, halves, width, cores, lines = lax.axis_size("pair") // 16, 2, 4, 2, 4
    pairs = []
    for z in range(layers):
        for y in range(halves * lines):
            for x in range(width):
                for core in range(cores):
                    ends = []
                    for tz, ty, tx, tc in ((z, y, x, core), move(z, y, x, core)):
                        tz, ty, tx, tc = tz % layers, ty % (halves * lines), tx % width, tc % cores
                        pair = ((tz * halves + ty // lines) * width + tx) * cores + tc
                        ends.append(pair * lines + ty % lines)
                    pairs.append(tuple(ends))
    return lax.ppermute(value, ("pair", "virt"), pairs)


def along_y(value):
    return permute(value, lambda z, y, x, core: (z, y + 1 - 2 * core, x, core))


def along_x(value):
    return permute(value, lambda z, y, x, core: (z, y, x + 1 - 2 * core, core))


def swap_cores(value):
    return permute(value, lambda z, y, x, core: (z, y, x, 1 - core))


def to_mirror(value):
    half = lax.axis_size("pair") // 32
    return permute(value, lambda z, y, x, core: (z + half, y, x, core))


def exchange(units):
    return lax.all_to_all(units, "virt", 0, 0, tiled=True)


def reorder(scattered, step):
    index = jnp.bitwise_xor(jnp.arange(4, dtype=jnp.int32)[:, None], step[None, :])
    return scattered[index, jnp.arange(scattered.shape[1], dtype=jnp.int32)[None, :]]


def together(*values):
    return lax.optimization_barrier(values)


def as_unit(ready, work, *values):
    def empty(*values):
        return jax.tree.map(lambda x: jnp.zeros(x.shape, x.dtype), jax.eval_shape(work, *values))

    return lax.cond(ready, work, empty, *values)


def params(*semantics):
    return pltpu.CompilerParams(
        dimension_semantics=semantics or None, vmem_limit_bytes=VMEM_LIMIT
    )


def cost(flops, moved):
    return pl.CostEstimate(flops=flops, bytes_accessed=moved, transcendentals=0)


def in_vmem(*values):
    return [pltpu.with_memory_space_constraint(x, pltpu.VMEM) for x in values]


WHOLE = pl.BlockSpec(memory_space=pltpu.VMEM)
SCALARS = pl.BlockSpec(memory_space=pltpu.SMEM)


def pack_kernel(order_ref, slab_ref, energy_ref, out_ref):
    for q in range(NQ):
        out_ref[0:W, q * W : (q + 1) * W] = slab_ref[q, 0]
    both = jnp.broadcast_to(energy_ref[...].reshape(1, 2 * W), (TALL - W, 2 * W))
    out_ref[W:TALL, 0:W] = jnp.where(order_ref[0] == 0, both[:, 0:W], both[:, W : 2 * W])
    out_ref[W:TALL, W:DEEP] = jnp.zeros((TALL - W, DEEP - W), BF)


def pack_slab(slab, energy, block):
    return pl.pallas_call(
        pack_kernel,
        out_shape=jax.ShapeDtypeStruct((TALL, DEEP), BF),
        grid_spec=pltpu.PrefetchScalarGridSpec(
            num_scalar_prefetch=1,
            grid=(1,),
            in_specs=[
                pl.BlockSpec((NQ, 1, W, W), lambda i, order: (0, order[0], 0, 0)),
                pl.BlockSpec((2 * W,), lambda i, order: (0,)),
            ],
            out_specs=pl.BlockSpec((TALL, DEEP), lambda i, order: (0, 0)),
        ),
        compiler_params=params("arbitrary"),
        cost_estimate=cost(0, 3_000_000),
    )(block, slab, energy)


def put_tile(unit_ref, block, tile):
    unit_ref[block * W : (block + 1) * W, :] = tile[:, 0:128]
    unit_ref[2 * W : 3 * W, block * 64 : (block + 1) * 64] = tile[:, 128:192]
    base = 3 * W + 16 * block
    for c in range(13):
        rows = min(16, W - 16 * c)
        unit_ref[base : base + rows, 8 * c : 8 * c + 8] = tile[16 * c : 16 * c + rows, 192:200]


def get_tile(unit, block):
    base = 3 * W + 16 * block
    tail = [
        unit[base : base + min(16, W - 16 * c), 8 * c : 8 * c + 8] for c in range(13)
    ]
    return jnp.concatenate(
        [
            unit[block * W : (block + 1) * W, :],
            unit[2 * W : 3 * W, block * 64 : (block + 1) * 64],
            jnp.concatenate(tail, axis=0),
        ],
        axis=1,
    )


def whole_unit(j, *refs):
    pieces = [ref[i, j].astype(F32) for ref in refs for i in range(ref.shape[0])]
    return jnp.concatenate(pieces, axis=0)


def turned(tile):
    return jnp.pad(tile, ((0, 56), (0, 56))).T[0:W, 0:W]


def tiles_kernel(pick_ref, amp_ref, int_ref, *refs):
    *outs, unit = refs
    unit[3 * W : UNIT, :] = jnp.zeros((UNIT - 3 * W, 128), F32)
    j = pl.program_id(0)
    for kind, ref in enumerate((amp_ref, int_ref)):
        for block in range(2):
            put_tile(unit, block, ref[0, block].astype(F32))
        for i in range(4):
            piece = unit[i * PIECE : (i + 1) * PIECE, :].astype(BF)
            if len(outs) == 2:
                outs[kind][i, j] = piece
            else:
                outs[0][i, 2 * kind + j] = piece


def pack_tiles(pick, amplitudes, integrals, arrays):
    tile = pl.BlockSpec((1, 2, W, W), lambda j, pick: (pick[j], 0, 0, 0))
    shape = (4, 4 // arrays, PIECE, 128)
    return pl.pallas_call(
        tiles_kernel,
        out_shape=[jax.ShapeDtypeStruct(shape, BF)] * arrays,
        grid_spec=pltpu.PrefetchScalarGridSpec(
            num_scalar_prefetch=1,
            grid=(2,),
            in_specs=[tile, tile],
            out_specs=[pl.BlockSpec(shape, lambda j, pick: (0, 0, 0, 0))] * arrays,
            scratch_shapes=[pltpu.VMEM((UNIT, 128), F32)],
        ),
        compiler_params=params("arbitrary"),
        cost_estimate=cost(0, 1_500_000),
    )(pick, amplitudes, integrals)


def half_kernel(flip_ref, slab_ref, local_ref, cross_ref, half_ref, int_ref):
    @pl.loop(0, 2)
    def _(j):
        straight = flip_ref[j] == 0

        def sums(at):
            local, cross = whole_unit(at, local_ref), whole_unit(at, cross_ref)
            tiles = [get_tile(cross, b) for b in range(2)]
            return [
                get_tile(local, b) + turned(jnp.where(straight, tiles[b], tiles[1 - b]))
                for b in range(2)
            ]

        for b, tile in enumerate(sums(2 + j)):
            int_ref[2 * j + b] = tile
        for b, tile in enumerate(sums(j)):
            both = tile.astype(BF)
            for q in range(NQ):
                half_ref[2 * j + b, :, q * W : (q + 1) * W] = jnp.dot(
                    slab_ref[q, b], both, preferred_element_type=F32
                ).astype(BF)


def first_half(flip, slab, local, cross):
    return pl.pallas_call(
        half_kernel,
        out_shape=(pltpu.VMEM((4, W, DEEP), BF), pltpu.VMEM((4, W, W), F32)),
        in_specs=[SCALARS] + [WHOLE] * 3,
        out_specs=[WHOLE, WHOLE],
        compiler_params=params(),
        cost_estimate=cost(8 * NQ * W**3, 4_000_000),
    )(flip, slab, local, cross)


def ladder_kernel(source_ref, core_ref, half_ref, int_ref, *refs):
    full, (near, near_x, far, far_x), (out_ref, table_ref, unit, sums) = (
        refs[:6], refs[6:10], refs[10:]
    )
    even = core_ref[0] == 0
    odd = core_ref[0] != 0
    split = ((even, near, far), (even, near_x, far_x), (odd, far, near), (odd, far_x, near_x))
    dims = (((1,), (1,)), ((), ()))

    @pl.loop(0, 4)
    def _(t):
        for r in range(6):

            @pl.when(source_ref[t] == r)
            def _():
                sums[t] = lax.dot_general(
                    half_ref[t], full[r][0:W, :], dims, preferred_element_type=F32
                )

        for r, (on, low, high) in enumerate(split):

            @pl.when(jnp.logical_and(on, source_ref[t] == 6 + r % 2))
            def _():
                sums[t] = lax.dot_general(
                    half_ref[t, :, 0:PART], low[0:W, :], dims, preferred_element_type=F32
                ) + lax.dot_general(
                    half_ref[t, :, PART:DEEP],
                    high[0:W, 2 * PART - DEEP : PART],
                    dims,
                    preferred_element_type=F32,
                )

    for r in range(6):
        table_ref[r] = full[r][W:TALL, 0:W].astype(F32)
    for r, (on, low, _) in enumerate(split):

        @pl.when(on)
        def _():
            table_ref[6 + r % 2] = low[W:TALL, 0:W].astype(F32)

    unit[3 * W : UNIT, :] = jnp.zeros((UNIT - 3 * W, 128), F32)
    for j in range(2):
        for b in range(2):
            put_tile(unit, b, int_ref[2 * j + b] + sums[2 * j + b])
        for i in range(4):
            out_ref[i, j] = unit[i * PIECE : (i + 1) * PIECE, :].astype(BF)


def symmetric_units(source, core, half_done, integrals, full, parts):
    return pl.pallas_call(
        ladder_kernel,
        out_shape=(
            jax.ShapeDtypeStruct((4, 2, PIECE, 128), BF),
            jax.ShapeDtypeStruct((8, TALL - W, W), F32),
        ),
        in_specs=[SCALARS, SCALARS] + [WHOLE] * 12,
        out_specs=[WHOLE] * 2,
        scratch_shapes=[pltpu.VMEM((UNIT, 128), F32), pltpu.VMEM((4, W, W), F32)],
        compiler_params=params(),
        cost_estimate=cost(8 * NQ * W**3, 3_000_000),
    )(source, core, *in_vmem(half_done, integrals, *full, *parts))


def update_kernel(
    kept_ref, at_ref, flip_ref, source_ref, pair_ref,
    amp_ref, cross_ref, mirror_ref, table_ref, near_ref, out_ref
):
    p = pl.program_id(0)

    def finish(block, symmetric):
        far = table_ref[source_ref[2 * p + block], 0:1, :]
        denominator = pair_ref[p] - near_ref[block] - far
        old = amp_ref[0, block].astype(F32)
        out_ref[0, block] = (old + symmetric / denominator).astype(BF)

    @pl.when(kept_ref[p] == 1)
    def _():
        unit = whole_unit(0, cross_ref)
        tiles = [get_tile(unit, b) for b in range(2)]
        straight = flip_ref[p] == 0
        for b in range(2):
            finish(b, turned(jnp.where(straight, tiles[b], tiles[1 - b])))

    @pl.when(kept_ref[p] == 0)
    def _():
        unit = whole_unit(0, mirror_ref)
        for b in range(2):
            finish(b, get_tile(unit, b))


def update(kept, at, flip, source, pair_energy, amplitudes, cross, mirror, table, near):
    pairs = amplitudes.shape[0]
    pick = lambda p, k, a, f, s, e: (0, a[p], 0, 0)
    here = lambda p, k, a, f, s, e: (p, 0, 0, 0)
    fixed = lambda p, k, a, f, s, e: (0, 0, 0)
    return pl.pallas_call(
        update_kernel,
        out_shape=jax.ShapeDtypeStruct((pairs, 2, W, W), BF),
        grid_spec=pltpu.PrefetchScalarGridSpec(
            num_scalar_prefetch=5,
            grid=(pairs,),
            in_specs=[
                pl.BlockSpec((1, 2, W, W), here),
                pl.BlockSpec((4, 1, PIECE, 128), pick),
                pl.BlockSpec((4, 1, PIECE, 128), pick),
                pl.BlockSpec((8, TALL - W, W), fixed),
                pl.BlockSpec((2, W, 1), fixed),
            ],
            out_specs=pl.BlockSpec((1, 2, W, W), here),
        ),
        compiler_params=params("arbitrary"),
    )(kept, at, flip, source, pair_energy, amplitudes, cross, mirror, table, near)


def on_device(
    amplitudes, integrals, ladder_slab, pair_list, mirror_slot, occ_irrep, occ_energy, virt_energy
):
    pairs = amplitudes.shape[0]
    amp = amplitudes.reshape(pairs, 2, W, W)
    ints = integrals.reshape(pairs, 2, W, W)
    slab = ladder_slab.reshape(NQ, 2, W, W)
    place = lax.axis_index("pair").astype(jnp.int32)
    virt = lax.axis_index("virt").astype(jnp.int32)
    core = jnp.bitwise_and(place, 1)
    parity = jnp.bitwise_and(jnp.right_shift(place, 1), 1)
    upper = (place >= lax.axis_size("pair") // 2).astype(jnp.int32)

    slots = jnp.arange(pairs, dtype=jnp.int32)
    label = jnp.where(upper == 0, slots, mirror_slot)
    kept = (jnp.right_shift(label, 1) == upper).astype(jnp.int32)
    at = jnp.bitwise_and(label, 1)

    def among(values, group):
        chosen = label[:, None] == jnp.arange(2, dtype=jnp.int32)[None, :] + 2 * group
        return jnp.sum(jnp.where(chosen, values[:, None], 0), axis=0)

    keep, send = among(slots, upper), among(slots, 1 - upper)

    one = pack_slab(slab, virt_energy, parity[None])
    y_one = along_y(one)
    local = to_mirror(pack_tiles(send, amp, ints, 1)[0])
    kept_tiles = pack_tiles(keep, amp, ints, 1)[0]

    irrep = jnp.bitwise_xor(occ_irrep[pair_list[:, 0]], occ_irrep[pair_list[:, 1]])
    step, flip = jnp.right_shift(irrep, 1), jnp.bitwise_and(irrep, 1)
    keep_step, keep_flip = among(step, upper), among(flip, upper)
    pair_energy = occ_energy[pair_list[:, 0]] + occ_energy[pair_list[:, 1]]
    near = virt_energy.astype(F32).reshape(2, W, 1)

    def sources(step, flip):
        apart = jnp.bitwise_and(jnp.bitwise_xor(virt, step) - virt, 3)[:, None]
        second = (jnp.bitwise_xor(jnp.arange(2)[None, :], flip[:, None]) != parity).astype(jnp.int32)
        side = jnp.where(apart == 3 - 2 * core, 2, 4)
        start = jnp.where(apart == 0, 0, jnp.where(apart == 2, 6, side))
        return (start + second).reshape(-1)

    keep_source, source = sources(keep_step, keep_flip), sources(step, flip)
    ready = pair_list[0, 0] >= 0
    (
        y_one, kept_tiles, keep_step, keep_flip, pair_energy, near, keep_source, source
    ) = together(
        y_one, kept_tiles, keep_step, keep_flip, pair_energy, near, keep_source, source
    )

    def bring(y_one, kept_tiles, keep_step, slab, virt_energy):
        scattered = exchange(kept_tiles)
        x_one = along_x(y_one)
        y_far = along_y(lax.dynamic_slice(y_one, (0, core * (DEEP - PART)), (TALL, PART)))
        cross = exchange(reorder(scattered, jnp.concatenate([keep_step, keep_step])))
        two = pack_slab(slab, virt_energy, 1 - parity[None])
        return (
            two, x_one, swap_cores(y_one), swap_cores(x_one),
            y_far, along_x(y_far), swap_cores(y_far), cross,
        )

    brought = as_unit(ready, bring, y_one, kept_tiles, keep_step, slab, virt_energy)
    two, x_one, y_swap, x_swap, y_far, x_far, y_far_swap, cross, local = together(*brought, local)
    full = (one, two, y_one, x_one, y_swap, x_swap)
    parts = (y_far, x_far, y_far_swap, swap_cores(x_far))

    half_done, both_ints = first_half(keep_flip, slab, local, cross)
    result, table = symmetric_units(
        keep_source, core[None], half_done, both_ints, full, parts
    )
    mirrored = to_mirror(result)
    crossed = as_unit(ready, lambda x: exchange(reorder(exchange(x), keep_step)), result)
    new = update(
        kept, at, flip, source, pair_energy, amp, crossed, mirrored, table, near
    )
    return new.reshape(amplitudes.shape)


def solution(mesh):
    return jax.shard_map(
        on_device,
        mesh=mesh,
        in_specs=(
            P("pair", "virt", None),
            P("pair", "virt", None),
            P(None, "virt", None),
            P("pair", None),
            P("pair"),
            P(),
            P(),
            P("virt"),
        ),
        out_specs=P("pair", "virt", None),
        check_vma=False,
    )
```

```python
import functools

import jax
import jax.numpy as jnp
from jax import lax
from jax.experimental import pallas as pl
from jax.experimental.pallas import tpu as pltpu
from jax.sharding import PartitionSpec as P

W = 200
NQ = 16
DEEP = NQ * W
TALL = 208
PART = 1664
PIECE = 160
UNIT = 4 * PIECE
BF = jnp.bfloat16
F32 = jnp.float32
VMEM_LIMIT = 20 * 1024 * 1024


def permute(value, move):
    layers, halves, width, cores, lines = lax.axis_size("pair") // 16, 2, 4, 2, 4
    pairs = []
    for z in range(layers):
        for y in range(halves * lines):
            for x in range(width):
                for core in range(cores):
                    ends = []
                    for tz, ty, tx, tc in ((z, y, x, core), move(z, y, x, core)):
                        tz, ty, tx, tc = tz % layers, ty % (halves * lines), tx % width, tc % cores
                        pair = ((tz * halves + ty // lines) * width + tx) * cores + tc
                        ends.append(pair * lines + ty % lines)
                    pairs.append(tuple(ends))
    return lax.ppermute(value, ("pair", "virt"), pairs)


def along_y(value):
    return permute(value, lambda z, y, x, core: (z, y + 1 - 2 * core, x, core))


def along_x(value):
    return permute(value, lambda z, y, x, core: (z, y, x + 1 - 2 * core, core))


def swap_cores(value):
    return permute(value, lambda z, y, x, core: (z, y, x, 1 - core))


def to_mirror(value):
    half = lax.axis_size("pair") // 32
    return permute(value, lambda z, y, x, core: (z + half, y, x, core))


def exchange(units):
    return lax.all_to_all(units, "virt", 0, 0, tiled=True)


def together(*values):
    return lax.optimization_barrier(values)


def as_unit(ready, work, *values):
    def empty(*values):
        return jax.tree.map(lambda x: jnp.zeros(x.shape, x.dtype), jax.eval_shape(work, *values))

    return lax.cond(ready, work, empty, *values)


def params(*semantics):
    return pltpu.CompilerParams(
        dimension_semantics=semantics or None, vmem_limit_bytes=VMEM_LIMIT
    )


def cost(flops, moved):
    return pl.CostEstimate(flops=flops, bytes_accessed=moved, transcendentals=0)


def in_vmem(*values):
    return [pltpu.with_memory_space_constraint(x, pltpu.VMEM) for x in values]


WHOLE = pl.BlockSpec(memory_space=pltpu.VMEM)
SCALARS = pl.BlockSpec(memory_space=pltpu.SMEM)


def reorder_kernel(step_ref, in_ref, out_ref):
    for p in range(in_ref.shape[1]):
        for v in range(4):
            out_ref[v, p] = in_ref[jnp.bitwise_xor(step_ref[p % 2], v), p]


def reorder(scattered, step):
    return pl.pallas_call(
        reorder_kernel,
        out_shape=jax.ShapeDtypeStruct(scattered.shape, BF),
        in_specs=[SCALARS, WHOLE],
        out_specs=WHOLE,
        compiler_params=params(),
        cost_estimate=cost(0, 1_300_000),
    )(step, scattered)


def part_kernel(core_ref, in_ref, out_ref, sem):
    for c in range(2):

        @pl.when(core_ref[0] == c)
        def _():
            copy = pltpu.make_async_copy(
                in_ref.at[:, pl.ds(c * (DEEP - PART), PART)], out_ref, sem
            )
            copy.start()
            copy.wait()


def part_of(core, block):
    return pl.pallas_call(
        part_kernel,
        out_shape=jax.ShapeDtypeStruct((TALL, PART), BF),
        in_specs=[SCALARS, pl.BlockSpec(memory_space=pl.ANY)],
        out_specs=WHOLE,
        scratch_shapes=[pltpu.SemaphoreType.DMA],
        compiler_params=params(),
        cost_estimate=cost(0, 1_400_000),
    )(core, block)


def pack_kernel(order_ref, slab_ref, energy_ref, out_ref):
    for q in range(NQ):
        out_ref[0:W, q * W : (q + 1) * W] = slab_ref[q, 0]
    both = jnp.broadcast_to(energy_ref[...].reshape(1, 2 * W), (TALL - W, 2 * W))
    out_ref[W:TALL, 0:W] = jnp.where(order_ref[0] == 0, both[:, 0:W], both[:, W : 2 * W])
    out_ref[W:TALL, W:DEEP] = jnp.zeros((TALL - W, DEEP - W), BF)


def pack_slab(slab, energy, block):
    return pl.pallas_call(
        pack_kernel,
        out_shape=jax.ShapeDtypeStruct((TALL, DEEP), BF),
        grid_spec=pltpu.PrefetchScalarGridSpec(
            num_scalar_prefetch=1,
            grid=(1,),
            in_specs=[
                pl.BlockSpec((NQ, 1, W, W), lambda i, order: (0, order[0], 0, 0)),
                pl.BlockSpec((2 * W,), lambda i, order: (0,)),
            ],
            out_specs=pl.BlockSpec((TALL, DEEP), lambda i, order: (0, 0)),
        ),
        compiler_params=params("arbitrary"),
        cost_estimate=cost(0, 3_000_000),
    )(block, slab, energy)


def put_tile(unit_ref, block, tile):
    unit_ref[block * W : (block + 1) * W, :] = tile[:, 0:128]
    unit_ref[2 * W : 3 * W, block * 64 : (block + 1) * 64] = tile[:, 128:192]
    base = 3 * W + 16 * block
    for c in range(13):
        rows = min(16, W - 16 * c)
        unit_ref[base : base + rows, 8 * c : 8 * c + 8] = tile[16 * c : 16 * c + rows, 192:200]


def get_tile(unit, block):
    base = 3 * W + 16 * block
    tail = [
        unit[base : base + min(16, W - 16 * c), 8 * c : 8 * c + 8] for c in range(13)
    ]
    return jnp.concatenate(
        [
            unit[block * W : (block + 1) * W, :],
            unit[2 * W : 3 * W, block * 64 : (block + 1) * 64],
            jnp.concatenate(tail, axis=0),
        ],
        axis=1,
    )


def whole_unit(j, *refs):
    pieces = [ref[i, j].astype(F32) for ref in refs for i in range(ref.shape[0])]
    return jnp.concatenate(pieces, axis=0)


def turned(tile):
    return jnp.pad(tile, ((0, 56), (0, 56))).T[0:W, 0:W]


def tiles_kernel(turn, pick_ref, amp_ref, int_ref, out_ref, unit):
    unit[3 * W : UNIT, :] = jnp.zeros((UNIT - 3 * W, 128), F32)
    j = pl.program_id(0)
    for kind, ref in enumerate((amp_ref, int_ref)):
        for block in range(2):
            tile = ref[0, block].astype(F32)
            put_tile(unit, block, turned(tile) if turn else tile)
        for i in range(4):
            out_ref[i, 2 * kind + j] = unit[i * PIECE : (i + 1) * PIECE, :].astype(BF)


def pack_tiles(pick, amplitudes, integrals, turn):
    tile = pl.BlockSpec((1, 2, W, W), lambda j, pick: (pick[j], 0, 0, 0))
    shape = (4, 4, PIECE, 128)
    return pl.pallas_call(
        functools.partial(tiles_kernel, turn),
        out_shape=jax.ShapeDtypeStruct(shape, BF),
        grid_spec=pltpu.PrefetchScalarGridSpec(
            num_scalar_prefetch=1,
            grid=(2,),
            in_specs=[tile, tile],
            out_specs=pl.BlockSpec(shape, lambda j, pick: (0, 0, 0, 0)),
            scratch_shapes=[pltpu.VMEM((UNIT, 128), F32)],
        ),
        compiler_params=params("arbitrary"),
        cost_estimate=cost(0, 1_500_000),
    )(pick, amplitudes, integrals)


def ladder_kernel(source_ref, flip_ref, core_ref, *refs):
    slab_ref, local_ref, cross_ref, *refs = refs
    full, (near, near_x, far, far_x), (out_ref, table_ref, *refs) = refs[:6], refs[6:10], refs[10:]
    local, cross, slab, right, rows, half, unit, one_sem, slab_sem, right_sem, row_sem = refs
    even, odd = core_ref[0] == 0, core_ref[0] != 0
    split = ((even, near, far), (even, near_x, far_x), (odd, far, near), (odd, far_x, near_x))

    copies = [
        pltpu.make_async_copy(local_ref, local, one_sem.at[0]),
        pltpu.make_async_copy(cross_ref, cross, one_sem.at[1]),
        pltpu.make_async_copy(slab_ref.at[:, 0], slab.at[0], slab_sem.at[0]),
        pltpu.make_async_copy(slab_ref.at[:, 1], slab.at[1], slab_sem.at[1]),
    ]
    for copy in copies:
        copy.start()
    for t in range(4):
        for r in range(6):

            @pl.when(source_ref[t] == r)
            def _():
                pltpu.make_async_copy(full[r], right.at[t], right_sem.at[t]).start()

        for r, (on, low, high) in enumerate(split):

            @pl.when(jnp.logical_and(on, source_ref[t] == 6 + r % 2))
            def _():
                pltpu.make_async_copy(
                    low, right.at[t, :, pl.ds(0, PART)], right_sem.at[t]
                ).start()
                pltpu.make_async_copy(
                    high.at[:, pl.ds(2 * PART - DEEP, DEEP - PART)],
                    right.at[t, :, pl.ds(PART, DEEP - PART)],
                    right_sem.at[t],
                ).start()

    corner = (pl.ds(TALL - 16, 16), pl.ds(0, 256))
    for r in range(6):
        pltpu.make_async_copy(full[r].at[corner], rows.at[r], row_sem.at[r]).start()
    for r, (on, low, _) in enumerate(split):

        @pl.when(on)
        def _():
            pltpu.make_async_copy(low.at[corner], rows.at[6 + r % 2], row_sem.at[6 + r % 2]).start()

    copies[0].wait()
    copies[1].wait()
    unit[3 * W : UNIT, :] = jnp.zeros((UNIT - 3 * W, 128), F32)

    @pl.loop(0, 2)
    def _(j):
        straight = flip_ref[j] == 0

        def sums(at):
            here, there = whole_unit(at, local), whole_unit(at, cross)
            tiles = [get_tile(there, b) for b in range(2)]
            return [
                get_tile(here, b) + jnp.where(straight, tiles[b], tiles[1 - b]) for b in range(2)
            ]

        amp, add = sums(j), sums(2 + j)
        for b in range(2):
            t = 2 * j + b

            @pl.when(j == 0)
            def _():
                copies[2 + b].wait()

            both = amp[b].astype(BF)
            for q in range(NQ):
                half[:, q * W : (q + 1) * W] = jnp.dot(
                    slab[b, q], both, preferred_element_type=F32
                ).astype(BF)
            pltpu.make_async_copy(full[0], right.at[t], right_sem.at[t]).wait()
            ladder = lax.dot_general(
                half[...], right[t, 0:W, :], (((1,), (1,)), ((), ())), preferred_element_type=F32
            )
            put_tile(unit, b, add[b] + ladder)
        for i in range(4):
            out_ref[i, j] = unit[i * PIECE : (i + 1) * PIECE, :].astype(BF)

    for r in range(8):
        pltpu.make_async_copy(full[0].at[corner], rows.at[r], row_sem.at[r]).wait()
        table_ref[r] = rows[r].astype(F32)[8:16, 0:W]


def symmetric_units(source, flip, core, slab, local, cross, full, parts):
    dma = pltpu.SemaphoreType.DMA
    return pl.pallas_call(
        ladder_kernel,
        out_shape=(
            jax.ShapeDtypeStruct((4, 2, PIECE, 128), BF),
            jax.ShapeDtypeStruct((8, TALL - W, W), F32),
        ),
        in_specs=[SCALARS] * 3 + [pl.BlockSpec(memory_space=pl.ANY)] * 13,
        out_specs=[WHOLE] * 2,
        scratch_shapes=[
            pltpu.VMEM((4, 4, PIECE, 128), BF),
            pltpu.VMEM((4, 4, PIECE, 128), BF),
            pltpu.VMEM((2, NQ, W, W), BF),
            pltpu.VMEM((4, TALL, DEEP), BF),
            pltpu.VMEM((8, 16, 256), BF),
            pltpu.VMEM((W, DEEP), BF),
            pltpu.VMEM((UNIT, 128), F32),
            dma((2,)),
            dma((2,)),
            dma((4,)),
            dma((8,)),
        ],
        compiler_params=params(),
        cost_estimate=cost(16 * NQ * W**3, 10_000_000),
    )(source, flip, core, slab, local, cross, *full, *parts)


def update_kernel(
    kept_ref, at_ref, flip_ref, source_ref, pair_ref,
    amp_ref, cross_ref, mirror_ref, table_ref, near_ref, out_ref
):
    p = pl.program_id(0)

    def finish(block, symmetric):
        far = table_ref[source_ref[2 * p + block], 0:1, :]
        denominator = pair_ref[p] - near_ref[block, :, 0:1] - far
        old = amp_ref[0, block].astype(F32)
        out_ref[0, block] = (old + symmetric / denominator).astype(BF)

    @pl.when(kept_ref[p] == 1)
    def _():
        unit = whole_unit(0, cross_ref)
        tiles = [get_tile(unit, b) for b in range(2)]
        straight = flip_ref[p] == 0
        for b in range(2):
            finish(b, turned(jnp.where(straight, tiles[b], tiles[1 - b])))

    @pl.when(kept_ref[p] == 0)
    def _():
        unit = whole_unit(0, mirror_ref)
        for b in range(2):
            finish(b, get_tile(unit, b))


def update(kept, at, flip, source, pair_energy, amplitudes, cross, mirror, table, near):
    pairs = amplitudes.shape[0]
    pick = lambda p, k, a, f, s, e: (0, a[p], 0, 0)
    here = lambda p, k, a, f, s, e: (p, 0, 0, 0)
    fixed = lambda p, k, a, f, s, e: (0, 0, 0)
    return pl.pallas_call(
        update_kernel,
        out_shape=jax.ShapeDtypeStruct((pairs, 2, W, W), BF),
        grid_spec=pltpu.PrefetchScalarGridSpec(
            num_scalar_prefetch=5,
            grid=(pairs,),
            in_specs=[
                pl.BlockSpec((1, 2, W, W), here),
                pl.BlockSpec((4, 1, PIECE, 128), pick),
                pl.BlockSpec((4, 1, PIECE, 128), pick),
                pl.BlockSpec((8, TALL - W, W), fixed),
                pl.BlockSpec((2, W, 128), fixed),
            ],
            out_specs=pl.BlockSpec((1, 2, W, W), here),
        ),
        compiler_params=params("arbitrary"),
    )(kept, at, flip, source, pair_energy, amplitudes, cross, mirror, table, near)


def on_device(
    amplitudes, integrals, ladder_slab, pair_list, mirror_slot, occ_irrep, occ_energy, virt_energy
):
    pairs = amplitudes.shape[0]
    amp = amplitudes.reshape(pairs, 2, W, W)
    ints = integrals.reshape(pairs, 2, W, W)
    slab = ladder_slab.reshape(NQ, 2, W, W)
    place = lax.axis_index("pair").astype(jnp.int32)
    virt = lax.axis_index("virt").astype(jnp.int32)
    core = jnp.bitwise_and(place, 1)
    parity = jnp.bitwise_and(jnp.right_shift(place, 1), 1)
    upper = (place >= lax.axis_size("pair") // 2).astype(jnp.int32)

    slots = jnp.arange(pairs, dtype=jnp.int32)
    label = jnp.where(upper == 0, slots, mirror_slot)
    kept = (jnp.right_shift(label, 1) == upper).astype(jnp.int32)
    at = jnp.bitwise_and(label, 1)

    def among(values, group):
        chosen = label[:, None] == jnp.arange(2, dtype=jnp.int32)[None, :] + 2 * group
        return jnp.sum(jnp.where(chosen, values[:, None], 0), axis=0)

    keep, send = among(slots, upper), among(slots, 1 - upper)

    one = pack_slab(slab, virt_energy, parity[None])
    y_one = along_y(one)
    local = to_mirror(pack_tiles(send, amp, ints, False))
    kept_tiles = pack_tiles(keep, amp, ints, True)

    irrep = jnp.bitwise_xor(occ_irrep[pair_list[:, 0]], occ_irrep[pair_list[:, 1]])
    step, flip = jnp.right_shift(irrep, 1), jnp.bitwise_and(irrep, 1)
    keep_step, keep_flip = among(step, upper), among(flip, upper)
    pair_energy = occ_energy[pair_list[:, 0]] + occ_energy[pair_list[:, 1]]
    near = jnp.broadcast_to(virt_energy.astype(F32).reshape(2, W, 1), (2, W, 128))

    def sources(step, flip):
        apart = jnp.bitwise_and(jnp.bitwise_xor(virt, step) - virt, 3)[:, None]
        second = (jnp.bitwise_xor(jnp.arange(2)[None, :], flip[:, None]) != parity).astype(jnp.int32)
        side = jnp.where(apart == 3 - 2 * core, 2, 4)
        start = jnp.where(apart == 0, 0, jnp.where(apart == 2, 6, side))
        return (start + second).reshape(-1)

    keep_source, source = sources(keep_step, keep_flip), sources(step, flip)
    ready = pair_list[0, 0] >= 0
    (
        y_one, kept_tiles, keep_step, keep_flip, pair_energy, near, keep_source, source
    ) = together(
        y_one, kept_tiles, keep_step, keep_flip, pair_energy, near, keep_source, source
    )

    def bring(y_one, kept_tiles, keep_step, slab, virt_energy):
        scattered = exchange(kept_tiles)
        x_one = along_x(y_one)
        y_far = along_y(part_of(core[None], y_one))
        cross = exchange(reorder(scattered, keep_step))
        two = pack_slab(slab, virt_energy, 1 - parity[None])
        x_far = along_x(y_far)
        return (
            two, x_one, swap_cores(y_one), swap_cores(x_one),
            y_far, x_far, swap_cores(y_far), swap_cores(x_far), cross,
        )

    brought = as_unit(ready, bring, y_one, kept_tiles, keep_step, slab, virt_energy)
    two, x_one, y_swap, x_swap, *parts, cross, local = together(*brought, local)
    full = (one, two, y_one, x_one, y_swap, x_swap)
    result, table = symmetric_units(
        keep_source, keep_flip, core[None], slab, local, cross, full, parts
    )
    mirrored = to_mirror(result)
    crossed = as_unit(ready, lambda x: exchange(reorder(exchange(x), keep_step)), result)
    new = update(
        kept, at, flip, source, pair_energy, amp, crossed, mirrored, table, near
    )
    return new.reshape(amplitudes.shape)


def solution(mesh):
    return jax.shard_map(
        on_device,
        mesh=mesh,
        in_specs=(
            P("pair", "virt", None),
            P("pair", "virt", None),
            P(None, "virt", None),
            P("pair", None),
            P("pair"),
            P(),
            P(),
            P("virt"),
        ),
        out_specs=P("pair", "virt", None),
        check_vma=False,
    )
```

```python
import functools

import jax
import jax.numpy as jnp
from jax import lax
from jax.experimental import pallas as pl
from jax.experimental.pallas import tpu as pltpu
from jax.sharding import PartitionSpec as P

W = 200
NQ = 16
DEEP = NQ * W
TALL = 208
PART = 1664
PIECE = 160
UNIT = 4 * PIECE
BF = jnp.bfloat16
F32 = jnp.float32
VMEM_LIMIT = 20 * 1024 * 1024


def permute(value, move):
    layers, halves, width, cores, lines = lax.axis_size("pair") // 16, 2, 4, 2, 4
    pairs = []
    for z in range(layers):
        for y in range(halves * lines):
            for x in range(width):
                for core in range(cores):
                    ends = []
                    for tz, ty, tx, tc in ((z, y, x, core), move(z, y, x, core)):
                        tz, ty, tx, tc = tz % layers, ty % (halves * lines), tx % width, tc % cores
                        pair = ((tz * halves + ty // lines) * width + tx) * cores + tc
                        ends.append(pair * lines + ty % lines)
                    pairs.append(tuple(ends))
    return lax.ppermute(value, ("pair", "virt"), pairs)


def along_y(value):
    return permute(value, lambda z, y, x, core: (z, y + 1 - 2 * core, x, core))


def along_x(value):
    return permute(value, lambda z, y, x, core: (z, y, x + 1 - 2 * core, core))


def swap_cores(value):
    return permute(value, lambda z, y, x, core: (z, y, x, 1 - core))


def to_mirror(value):
    half = lax.axis_size("pair") // 32
    return permute(value, lambda z, y, x, core: (z + half, y, x, core))


def exchange(units):
    return lax.all_to_all(units, "virt", 0, 0, tiled=True)


def reorder(scattered, step):
    index = jnp.bitwise_xor(jnp.arange(4, dtype=jnp.int32)[:, None], step[None, :])
    return scattered[index, jnp.arange(scattered.shape[1], dtype=jnp.int32)[None, :]]


def together(*values):
    return lax.optimization_barrier(values)


def as_unit(ready, work, *values):
    def empty(*values):
        return jax.tree.map(lambda x: jnp.zeros(x.shape, x.dtype), jax.eval_shape(work, *values))

    return lax.cond(ready, work, empty, *values)


def params(*semantics):
    return pltpu.CompilerParams(
        dimension_semantics=semantics or None, vmem_limit_bytes=VMEM_LIMIT
    )


def cost(flops, moved):
    return pl.CostEstimate(flops=flops, bytes_accessed=moved, transcendentals=0)


def in_vmem(*values):
    return [pltpu.with_memory_space_constraint(x, pltpu.VMEM) for x in values]


WHOLE = pl.BlockSpec(memory_space=pltpu.VMEM)
SCALARS = pl.BlockSpec(memory_space=pltpu.SMEM)


def pack_kernel(order_ref, slab_ref, energy_ref, out_ref):
    for q in range(NQ):
        out_ref[0:W, q * W : (q + 1) * W] = slab_ref[q, 0]
    both = jnp.broadcast_to(energy_ref[...].reshape(1, 2 * W), (TALL - W, 2 * W))
    out_ref[W:TALL, 0:W] = jnp.where(order_ref[0] == 0, both[:, 0:W], both[:, W : 2 * W])
    out_ref[W:TALL, W:DEEP] = jnp.zeros((TALL - W, DEEP - W), BF)


def pack_slab(slab, energy, block):
    return pl.pallas_call(
        pack_kernel,
        out_shape=jax.ShapeDtypeStruct((TALL, DEEP), BF),
        grid_spec=pltpu.PrefetchScalarGridSpec(
            num_scalar_prefetch=1,
            grid=(1,),
            in_specs=[
                pl.BlockSpec((NQ, 1, W, W), lambda i, order: (0, order[0], 0, 0)),
                pl.BlockSpec((2 * W,), lambda i, order: (0,)),
            ],
            out_specs=pl.BlockSpec((TALL, DEEP), lambda i, order: (0, 0)),
        ),
        compiler_params=params("arbitrary"),
        cost_estimate=cost(0, 3_000_000),
    )(block, slab, energy)


def put_tile(unit_ref, block, tile):
    unit_ref[block * W : (block + 1) * W, :] = tile[:, 0:128]
    unit_ref[2 * W : 3 * W, block * 64 : (block + 1) * 64] = tile[:, 128:192]
    base = 3 * W + 16 * block
    for c in range(13):
        rows = min(16, W - 16 * c)
        unit_ref[base : base + rows, 8 * c : 8 * c + 8] = tile[16 * c : 16 * c + rows, 192:200]


def get_tile(unit, block):
    base = 3 * W + 16 * block
    tail = [
        unit[base : base + min(16, W - 16 * c), 8 * c : 8 * c + 8] for c in range(13)
    ]
    return jnp.concatenate(
        [
            unit[block * W : (block + 1) * W, :],
            unit[2 * W : 3 * W, block * 64 : (block + 1) * 64],
            jnp.concatenate(tail, axis=0),
        ],
        axis=1,
    )


def whole_unit(j, *refs):
    pieces = [ref[i, j].astype(F32) for ref in refs for i in range(ref.shape[0])]
    return jnp.concatenate(pieces, axis=0)


def turned(tile):
    return jnp.pad(tile, ((0, 56), (0, 56))).T[0:W, 0:W]


def tiles_kernel(turn, pick_ref, amp_ref, int_ref, out_ref, unit):
    unit[3 * W : UNIT, :] = jnp.zeros((UNIT - 3 * W, 128), F32)
    j = pl.program_id(0)
    for kind, ref in enumerate((amp_ref, int_ref)):
        for block in range(2):
            tile = ref[0, block].astype(F32)
            put_tile(unit, block, turned(tile) if turn else tile)
        for i in range(4):
            out_ref[i, 2 * kind + j] = unit[i * PIECE : (i + 1) * PIECE, :].astype(BF)


def pack_tiles(pick, amplitudes, integrals, turn):
    tile = pl.BlockSpec((1, 2, W, W), lambda j, pick: (pick[j], 0, 0, 0))
    shape = (4, 4, PIECE, 128)
    return pl.pallas_call(
        functools.partial(tiles_kernel, turn),
        out_shape=jax.ShapeDtypeStruct(shape, BF),
        grid_spec=pltpu.PrefetchScalarGridSpec(
            num_scalar_prefetch=1,
            grid=(2,),
            in_specs=[tile, tile],
            out_specs=pl.BlockSpec(shape, lambda j, pick: (0, 0, 0, 0)),
            scratch_shapes=[pltpu.VMEM((UNIT, 128), F32)],
        ),
        compiler_params=params("arbitrary"),
        cost_estimate=cost(0, 1_500_000),
    )(pick, amplitudes, integrals)


def half_kernel(flip_ref, slab_ref, local_ref, cross_ref, half_ref, int_ref, *refs):
    local, cross, slab, unit_sem, slab_sem = refs
    copies = []
    for i in range(4):
        copies.append(pltpu.make_async_copy(local_ref.at[i], local.at[i], unit_sem.at[0, i]))
        copies.append(pltpu.make_async_copy(cross_ref.at[i], cross.at[i], unit_sem.at[1, i]))
    parts = [
        [
            pltpu.make_async_copy(
                slab_ref.at[pl.ds(4 * i, 4), b], slab.at[b, pl.ds(4 * i, 4)], slab_sem.at[b, i]
            )
            for i in range(4)
        ]
        for b in range(2)
    ]
    for copy in (*copies, *parts[0], *parts[1]):
        copy.start()
    for copy in copies:
        copy.wait()

    @pl.loop(0, 2)
    def _(j):
        straight = flip_ref[j] == 0

        def sums(at):
            here, there = whole_unit(at, local), whole_unit(at, cross)
            tiles = [get_tile(there, b) for b in range(2)]
            return [
                get_tile(here, b) + jnp.where(straight, tiles[b], tiles[1 - b]) for b in range(2)
            ]

        for b, tile in enumerate(sums(2 + j)):
            int_ref[2 * j + b] = tile
        for b, tile in enumerate(sums(j)):
            both = tile.astype(BF)

            @pl.when(j == 0)
            def _():
                for copy in parts[b]:
                    copy.wait()

            for q in range(NQ):
                half_ref[2 * j + b, :, q * W : (q + 1) * W] = jnp.dot(
                    slab[b, q], both, preferred_element_type=F32
                ).astype(BF)


def first_half(flip, slab, local, cross):
    return pl.pallas_call(
        half_kernel,
        out_shape=(pltpu.VMEM((4, W, DEEP), BF), pltpu.VMEM((4, W, W), F32)),
        in_specs=[SCALARS] + [pl.BlockSpec(memory_space=pl.ANY)] * 3,
        out_specs=[WHOLE, WHOLE],
        scratch_shapes=[
            pltpu.VMEM((4, 4, PIECE, 128), BF),
            pltpu.VMEM((4, 4, PIECE, 128), BF),
            pltpu.VMEM((2, NQ, W, W), BF),
            pltpu.SemaphoreType.DMA((2, 4)),
            pltpu.SemaphoreType.DMA((2, 4)),
        ],
        compiler_params=params(),
        cost_estimate=cost(8 * NQ * W**3, 4_000_000),
    )(flip, slab, local, cross)


CHUNKS = ((0, 64), (64, 48), (112, 48), (160, 48))


def ladder_kernel(source_ref, core_ref, half_ref, int_ref, *refs):
    full, (near, near_x, far, far_x), (out_ref, table_ref, *refs) = refs[:6], refs[6:10], refs[10:]
    right, rows, unit, right_sem, row_sem = refs
    even, odd = core_ref[0] == 0, core_ref[0] != 0
    split = ((even, near, far), (even, near_x, far_x), (odd, far, near), (odd, far_x, near_x))

    for t in range(4):
        for r in range(6):

            @pl.when(source_ref[t] == r)
            def _():
                for i, chunk in enumerate(CHUNKS):
                    here = pl.ds(*chunk)
                    pltpu.make_async_copy(
                        full[r].at[here], right.at[t, here], right_sem.at[t, i]
                    ).start()

        for r, (on, low, high) in enumerate(split):

            @pl.when(jnp.logical_and(on, source_ref[t] == 6 + r % 2))
            def _():
                for i, chunk in enumerate(CHUNKS):
                    here = pl.ds(*chunk)
                    pltpu.make_async_copy(
                        low.at[here], right.at[t, here, pl.ds(0, PART)], right_sem.at[t, i]
                    ).start()
                    pltpu.make_async_copy(
                        high.at[here, pl.ds(2 * PART - DEEP, DEEP - PART)],
                        right.at[t, here, pl.ds(PART, DEEP - PART)],
                        right_sem.at[t, i],
                    ).start()

    corner = (pl.ds(TALL - 16, 16), pl.ds(0, 256))
    for r in range(6):
        pltpu.make_async_copy(full[r].at[corner], rows.at[r], row_sem.at[r]).start()
    for r, (on, low, _) in enumerate(split):

        @pl.when(on)
        def _():
            pltpu.make_async_copy(low.at[corner], rows.at[6 + r % 2], row_sem.at[6 + r % 2]).start()

    unit[3 * W : UNIT, :] = jnp.zeros((UNIT - 3 * W, 128), F32)

    @pl.loop(0, 2)
    def _(j):
        for b in range(2):
            t = 2 * j + b
            for i, chunk in enumerate(CHUNKS):
                here = pl.ds(*chunk)
                pltpu.make_async_copy(
                    full[0].at[here], right.at[t, here], right_sem.at[t, i]
                ).wait()
            ladder = lax.dot_general(
                half_ref[t], right[t, 0:W, :], (((1,), (1,)), ((), ())), preferred_element_type=F32
            )
            put_tile(unit, b, int_ref[t] + ladder)
        for i in range(4):
            out_ref[i, j] = unit[i * PIECE : (i + 1) * PIECE, :].astype(BF)

    for r in range(8):
        pltpu.make_async_copy(full[0].at[corner], rows.at[r], row_sem.at[r]).wait()
        table_ref[r] = rows[r].astype(F32)[8:16, 0:W]


def symmetric_units(source, core, half_done, integrals, full, parts):
    return pl.pallas_call(
        ladder_kernel,
        out_shape=(
            jax.ShapeDtypeStruct((4, 2, PIECE, 128), BF),
            jax.ShapeDtypeStruct((8, TALL - W, W), F32),
        ),
        in_specs=[SCALARS] * 2 + [WHOLE] * 2 + [pl.BlockSpec(memory_space=pl.ANY)] * 10,
        out_specs=[WHOLE] * 2,
        scratch_shapes=[
            pltpu.VMEM((4, TALL, DEEP), BF),
            pltpu.VMEM((8, 16, 256), BF),
            pltpu.VMEM((UNIT, 128), F32),
            pltpu.SemaphoreType.DMA((4, 4)),
            pltpu.SemaphoreType.DMA((8,)),
        ],
        compiler_params=params(),
        cost_estimate=cost(8 * NQ * W**3, 6_000_000),
    )(source, core, *in_vmem(half_done, integrals), *full, *parts)


def update_kernel(
    kept_ref, at_ref, flip_ref, source_ref, pair_ref,
    amp_ref, cross_ref, mirror_ref, table_ref, near_ref, out_ref
):
    p = pl.program_id(0)

    def finish(block, symmetric):
        far = table_ref[source_ref[2 * p + block], 0:1, :]
        denominator = pair_ref[p] - near_ref[block, :, 0:1] - far
        old = amp_ref[0, block].astype(F32)
        out_ref[0, block] = (old + symmetric / denominator).astype(BF)

    @pl.when(kept_ref[p] == 1)
    def _():
        unit = whole_unit(0, cross_ref)
        tiles = [get_tile(unit, b) for b in range(2)]
        straight = flip_ref[p] == 0
        for b in range(2):
            finish(b, turned(jnp.where(straight, tiles[b], tiles[1 - b])))

    @pl.when(kept_ref[p] == 0)
    def _():
        unit = whole_unit(0, mirror_ref)
        for b in range(2):
            finish(b, get_tile(unit, b))


def update(kept, at, flip, source, pair_energy, amplitudes, cross, mirror, table, near):
    pairs = amplitudes.shape[0]
    pick = lambda p, k, a, f, s, e: (0, a[p], 0, 0)
    here = lambda p, k, a, f, s, e: (p, 0, 0, 0)
    fixed = lambda p, k, a, f, s, e: (0, 0, 0)
    return pl.pallas_call(
        update_kernel,
        out_shape=jax.ShapeDtypeStruct((pairs, 2, W, W), BF),
        grid_spec=pltpu.PrefetchScalarGridSpec(
            num_scalar_prefetch=5,
            grid=(pairs,),
            in_specs=[
                pl.BlockSpec((1, 2, W, W), here),
                pl.BlockSpec((4, 1, PIECE, 128), pick),
                pl.BlockSpec((4, 1, PIECE, 128), pick),
                pl.BlockSpec((8, TALL - W, W), fixed),
                pl.BlockSpec((2, W, 128), fixed),
            ],
            out_specs=pl.BlockSpec((1, 2, W, W), here),
        ),
        compiler_params=params("arbitrary"),
    )(kept, at, flip, source, pair_energy, amplitudes, cross, mirror, table, near)


def on_device(
    amplitudes, integrals, ladder_slab, pair_list, mirror_slot, occ_irrep, occ_energy, virt_energy
):
    pairs = amplitudes.shape[0]
    amp = amplitudes.reshape(pairs, 2, W, W)
    ints = integrals.reshape(pairs, 2, W, W)
    slab = ladder_slab.reshape(NQ, 2, W, W)
    place = lax.axis_index("pair").astype(jnp.int32)
    virt = lax.axis_index("virt").astype(jnp.int32)
    core = jnp.bitwise_and(place, 1)
    parity = jnp.bitwise_and(jnp.right_shift(place, 1), 1)
    upper = (place >= lax.axis_size("pair") // 2).astype(jnp.int32)

    slots = jnp.arange(pairs, dtype=jnp.int32)
    label = jnp.where(upper == 0, slots, mirror_slot)
    kept = (jnp.right_shift(label, 1) == upper).astype(jnp.int32)
    at = jnp.bitwise_and(label, 1)

    def among(values, group):
        chosen = label[:, None] == jnp.arange(2, dtype=jnp.int32)[None, :] + 2 * group
        return jnp.sum(jnp.where(chosen, values[:, None], 0), axis=0)

    keep, send = among(slots, upper), among(slots, 1 - upper)

    one = pack_slab(slab, virt_energy, parity[None])
    y_one = along_y(one)
    local = to_mirror(pack_tiles(send, amp, ints, False))
    kept_tiles = pack_tiles(keep, amp, ints, True)

    irrep = jnp.bitwise_xor(occ_irrep[pair_list[:, 0]], occ_irrep[pair_list[:, 1]])
    step, flip = jnp.right_shift(irrep, 1), jnp.bitwise_and(irrep, 1)
    keep_step, keep_flip = among(step, upper), among(flip, upper)
    pair_energy = occ_energy[pair_list[:, 0]] + occ_energy[pair_list[:, 1]]
    near = jnp.broadcast_to(virt_energy.astype(F32).reshape(2, W, 1), (2, W, 128))

    def sources(step, flip):
        apart = jnp.bitwise_and(jnp.bitwise_xor(virt, step) - virt, 3)[:, None]
        second = (jnp.bitwise_xor(jnp.arange(2)[None, :], flip[:, None]) != parity).astype(jnp.int32)
        side = jnp.where(apart == 3 - 2 * core, 2, 4)
        start = jnp.where(apart == 0, 0, jnp.where(apart == 2, 6, side))
        return (start + second).reshape(-1)

    keep_source, source = sources(keep_step, keep_flip), sources(step, flip)
    ready = pair_list[0, 0] >= 0
    (
        y_one, kept_tiles, keep_step, keep_flip, pair_energy, near, keep_source, source
    ) = together(
        y_one, kept_tiles, keep_step, keep_flip, pair_energy, near, keep_source, source
    )

    def bring(y_one, kept_tiles, keep_step, slab, virt_energy):
        scattered = exchange(kept_tiles)
        x_one = along_x(y_one)
        y_far = along_y(lax.dynamic_slice(y_one, (0, core * (DEEP - PART)), (TALL, PART)))
        cross = exchange(reorder(scattered, jnp.concatenate([keep_step, keep_step])))
        two = pack_slab(slab, virt_energy, 1 - parity[None])
        return (
            two, x_one, swap_cores(y_one), swap_cores(x_one),
            y_far, along_x(y_far), swap_cores(y_far), cross,
        )

    brought = as_unit(ready, bring, y_one, kept_tiles, keep_step, slab, virt_energy)
    two, x_one, y_swap, x_swap, y_far, x_far, y_far_swap, cross, local = together(*brought, local)
    full = (one, two, y_one, x_one, y_swap, x_swap)
    parts = (y_far, x_far, y_far_swap, swap_cores(x_far))

    half_done, both_ints = first_half(keep_flip, slab, local, cross)
    result, table = symmetric_units(
        keep_source, core[None], half_done, both_ints, full, parts
    )
    mirrored = to_mirror(result)
    scattered = exchange(result)
    crossed = as_unit(ready, lambda x: exchange(reorder(x, keep_step)), scattered)
    new = update(
        kept, at, flip, source, pair_energy, amp, crossed, mirrored, table, near
    )
    return new.reshape(amplitudes.shape)


def solution(mesh):
    return jax.shard_map(
        on_device,
        mesh=mesh,
        in_specs=(
            P("pair", "virt", None),
            P("pair", "virt", None),
            P(None, "virt", None),
            P("pair", None),
            P("pair"),
            P(),
            P(),
            P("virt"),
        ),
        out_specs=P("pair", "virt", None),
        check_vma=False,
    )
```

```python
import functools

import jax
import jax.numpy as jnp
from jax import lax
from jax.experimental import pallas as pl
from jax.experimental.pallas import tpu as pltpu
from jax.sharding import PartitionSpec as P

W = 200
NQ = 16
DEEP = NQ * W
TALL = 208
PART = 1664
PIECE = 160
UNIT = 4 * PIECE
BF = jnp.bfloat16
F32 = jnp.float32
VMEM_LIMIT = 20 * 1024 * 1024


def permute(value, move):
    layers, halves, width, cores, lines = lax.axis_size("pair") // 16, 2, 4, 2, 4
    pairs = []
    for z in range(layers):
        for y in range(halves * lines):
            for x in range(width):
                for core in range(cores):
                    ends = []
                    for tz, ty, tx, tc in ((z, y, x, core), move(z, y, x, core)):
                        tz, ty, tx, tc = tz % layers, ty % (halves * lines), tx % width, tc % cores
                        pair = ((tz * halves + ty // lines) * width + tx) * cores + tc
                        ends.append(pair * lines + ty % lines)
                    pairs.append(tuple(ends))
    return lax.ppermute(value, ("pair", "virt"), pairs)


def along_y(value):
    return permute(value, lambda z, y, x, core: (z, y + 1 - 2 * core, x, core))


def along_x(value):
    return permute(value, lambda z, y, x, core: (z, y, x + 1 - 2 * core, core))


def swap_cores(value):
    return permute(value, lambda z, y, x, core: (z, y, x, 1 - core))


def to_mirror(value):
    half = lax.axis_size("pair") // 32
    return permute(value, lambda z, y, x, core: (z + half, y, x, core))


def exchange(units):
    return lax.all_to_all(units, "virt", 0, 0, tiled=True)


def reorder(scattered, step):
    index = jnp.bitwise_xor(jnp.arange(4, dtype=jnp.int32)[:, None], step[None, :])
    return scattered[index, jnp.arange(scattered.shape[1], dtype=jnp.int32)[None, :]]


def together(*values):
    return lax.optimization_barrier(values)


def as_unit(ready, work, *values):
    def empty(*values):
        return jax.tree.map(lambda x: jnp.zeros(x.shape, x.dtype), jax.eval_shape(work, *values))

    return lax.cond(ready, work, empty, *values)


def params(*semantics):
    return pltpu.CompilerParams(
        dimension_semantics=semantics or None, vmem_limit_bytes=VMEM_LIMIT
    )


def cost(flops, moved):
    return pl.CostEstimate(flops=flops, bytes_accessed=moved, transcendentals=0)


def in_vmem(*values):
    return [pltpu.with_memory_space_constraint(x, pltpu.VMEM) for x in values]


WHOLE = pl.BlockSpec(memory_space=pltpu.VMEM)
SCALARS = pl.BlockSpec(memory_space=pltpu.SMEM)


def pack_kernel(order_ref, slab_ref, energy_ref, out_ref):
    for q in range(NQ):
        out_ref[0:W, q * W : (q + 1) * W] = slab_ref[q, 0]
    both = jnp.broadcast_to(energy_ref[...].reshape(1, 2 * W), (TALL - W, 2 * W))
    out_ref[W:TALL, 0:W] = jnp.where(order_ref[0] == 0, both[:, 0:W], both[:, W : 2 * W])
    out_ref[W:TALL, W:DEEP] = jnp.zeros((TALL - W, DEEP - W), BF)


def pack_slab(slab, energy, block):
    return pl.pallas_call(
        pack_kernel,
        out_shape=jax.ShapeDtypeStruct((TALL, DEEP), BF),
        grid_spec=pltpu.PrefetchScalarGridSpec(
            num_scalar_prefetch=1,
            grid=(1,),
            in_specs=[
                pl.BlockSpec((NQ, 1, W, W), lambda i, order: (0, order[0], 0, 0)),
                pl.BlockSpec((2 * W,), lambda i, order: (0,)),
            ],
            out_specs=pl.BlockSpec((TALL, DEEP), lambda i, order: (0, 0)),
        ),
        compiler_params=params("arbitrary"),
        cost_estimate=cost(0, 3_000_000),
    )(block, slab, energy)


def put_tile(unit_ref, block, tile):
    unit_ref[block * W : (block + 1) * W, :] = tile[:, 0:128]
    unit_ref[2 * W : 3 * W, block * 64 : (block + 1) * 64] = tile[:, 128:192]
    base = 3 * W + 16 * block
    for c in range(13):
        rows = min(16, W - 16 * c)
        unit_ref[base : base + rows, 8 * c : 8 * c + 8] = tile[16 * c : 16 * c + rows, 192:200]


def get_tile(unit, block):
    base = 3 * W + 16 * block
    tail = [
        unit[base : base + min(16, W - 16 * c), 8 * c : 8 * c + 8] for c in range(13)
    ]
    return jnp.concatenate(
        [
            unit[block * W : (block + 1) * W, :],
            unit[2 * W : 3 * W, block * 64 : (block + 1) * 64],
            jnp.concatenate(tail, axis=0),
        ],
        axis=1,
    )


def whole_unit(j, *refs):
    pieces = [ref[i, j].astype(F32) for ref in refs for i in range(ref.shape[0])]
    return jnp.concatenate(pieces, axis=0)


def turned(tile):
    return jnp.pad(tile, ((0, 56), (0, 56))).T[0:W, 0:W]


def tiles_kernel(turn, pick_ref, flip_ref, amp_ref, int_ref, out_ref, unit):
    unit[3 * W : UNIT, :] = jnp.zeros((UNIT - 3 * W, 128), F32)
    j = pl.program_id(0)
    for kind, ref in enumerate((amp_ref, int_ref)):
        tiles = [ref[0, block].astype(F32) for block in range(2)]
        if turn:
            straight = flip_ref[j] == 0
            tiles = [turned(jnp.where(straight, tiles[b], tiles[1 - b])) for b in range(2)]
        for block in range(2):
            put_tile(unit, block, tiles[block])
        for i in range(4):
            out_ref[i, 2 * kind + j] = unit[i * PIECE : (i + 1) * PIECE, :].astype(BF)


def pack_tiles(pick, flip, amplitudes, integrals, turn):
    tile = pl.BlockSpec((1, 2, W, W), lambda j, pick, flip: (pick[j], 0, 0, 0))
    shape = (4, 4, PIECE, 128)
    return pl.pallas_call(
        functools.partial(tiles_kernel, turn),
        out_shape=jax.ShapeDtypeStruct(shape, BF),
        grid_spec=pltpu.PrefetchScalarGridSpec(
            num_scalar_prefetch=2,
            grid=(2,),
            in_specs=[tile, tile],
            out_specs=pl.BlockSpec(shape, lambda j, pick, flip: (0, 0, 0, 0)),
            scratch_shapes=[pltpu.VMEM((UNIT, 128), F32)],
        ),
        compiler_params=params("arbitrary"),
        cost_estimate=cost(0, 1_500_000),
    )(pick, flip, amplitudes, integrals)


def half_kernel(slab_ref, local_ref, cross_ref, half_ref, int_ref):
    for i in range(4):
        for j in range(2):
            int_ref[i, j] = local_ref[i, 2 + j].astype(F32) + cross_ref[i, 2 + j].astype(F32)

    @pl.loop(0, 2)
    def _(j):
        unit = whole_unit(j, local_ref) + whole_unit(j, cross_ref)
        for b in range(2):
            both = get_tile(unit, b).astype(BF)
            for q in range(NQ):
                half_ref[2 * j + b, :, q * W : (q + 1) * W] = jnp.dot(
                    slab_ref[q, b], both, preferred_element_type=F32
                ).astype(BF)


def first_half(slab, local, cross):
    return pl.pallas_call(
        half_kernel,
        out_shape=(pltpu.VMEM((4, W, DEEP), BF), pltpu.VMEM((4, 2, PIECE, 128), F32)),
        in_specs=[WHOLE] * 3,
        out_specs=[WHOLE] * 2,
        compiler_params=params(),
        cost_estimate=cost(8 * NQ * W**3, 4_000_000),
    )(slab, local, cross)


def ladder_kernel(source_ref, core_ref, half_ref, int_ref, *refs):
    full, (near, near_x, far, far_x), (out_ref, table_ref, unit, sums) = (
        refs[:6], refs[6:10], refs[10:]
    )
    even = core_ref[0] == 0
    odd = core_ref[0] != 0
    split = ((even, near, far), (even, near_x, far_x), (odd, far, near), (odd, far_x, near_x))
    dims = (((1,), (1,)), ((), ()))

    @pl.loop(0, 4)
    def _(t):
        for r in range(6):

            @pl.when(source_ref[t] == r)
            def _():
                sums[t] = lax.dot_general(
                    half_ref[t], full[r][0:W, :], dims, preferred_element_type=F32
                )

        for r, (on, low, high) in enumerate(split):

            @pl.when(jnp.logical_and(on, source_ref[t] == 6 + r % 2))
            def _():
                sums[t] = lax.dot_general(
                    half_ref[t, :, 0:PART], low[0:W, :], dims, preferred_element_type=F32
                ) + lax.dot_general(
                    half_ref[t, :, PART:DEEP],
                    high[0:W, 2 * PART - DEEP : PART],
                    dims,
                    preferred_element_type=F32,
                )

    for r in range(6):
        table_ref[r] = full[r][W:TALL, 0:W].astype(F32)
    for r, (on, low, _) in enumerate(split):

        @pl.when(on)
        def _():
            table_ref[6 + r % 2] = low[W:TALL, 0:W].astype(F32)

    unit[3 * W : UNIT, :] = jnp.zeros((UNIT - 3 * W, 128), F32)
    for j in range(2):
        for b in range(2):
            put_tile(unit, b, sums[2 * j + b])
        for i in range(4):
            out_ref[i, j] = (unit[i * PIECE : (i + 1) * PIECE, :] + int_ref[i, j]).astype(BF)


def symmetric_units(source, core, half_done, integrals, full, parts):
    return pl.pallas_call(
        ladder_kernel,
        out_shape=(
            jax.ShapeDtypeStruct((4, 2, PIECE, 128), BF),
            jax.ShapeDtypeStruct((8, TALL - W, W), F32),
        ),
        in_specs=[SCALARS, SCALARS] + [WHOLE] * 12,
        out_specs=[WHOLE] * 2,
        scratch_shapes=[pltpu.VMEM((UNIT, 128), F32), pltpu.VMEM((4, W, W), F32)],
        compiler_params=params(),
        cost_estimate=cost(8 * NQ * W**3, 3_000_000),
    )(source, core, *in_vmem(half_done, integrals, *full, *parts))


def update_kernel(
    kept_ref, at_ref, flip_ref, source_ref, pair_ref,
    amp_ref, cross_ref, mirror_ref, table_ref, near_ref, out_ref
):
    p = pl.program_id(0)

    def finish(block, symmetric):
        far = table_ref[source_ref[2 * p + block], 0:1, :]
        denominator = pair_ref[p] - near_ref[block, :, 0:1] - far
        old = amp_ref[0, block].astype(F32)
        out_ref[0, block] = (old + symmetric / denominator).astype(BF)

    @pl.when(kept_ref[p] == 1)
    def _():
        unit = whole_unit(0, cross_ref)
        tiles = [get_tile(unit, b) for b in range(2)]
        straight = flip_ref[p] == 0
        for b in range(2):
            finish(b, turned(jnp.where(straight, tiles[b], tiles[1 - b])))

    @pl.when(kept_ref[p] == 0)
    def _():
        unit = whole_unit(0, mirror_ref)
        for b in range(2):
            finish(b, get_tile(unit, b))


def update(kept, at, flip, source, pair_energy, amplitudes, cross, mirror, table, near):
    pairs = amplitudes.shape[0]
    pick = lambda p, k, a, f, s, e: (0, a[p], 0, 0)
    here = lambda p, k, a, f, s, e: (p, 0, 0, 0)
    fixed = lambda p, k, a, f, s, e: (0, 0, 0)
    return pl.pallas_call(
        update_kernel,
        out_shape=jax.ShapeDtypeStruct((pairs, 2, W, W), BF),
        grid_spec=pltpu.PrefetchScalarGridSpec(
            num_scalar_prefetch=5,
            grid=(pairs,),
            in_specs=[
                pl.BlockSpec((1, 2, W, W), here),
                pl.BlockSpec((4, 1, PIECE, 128), pick),
                pl.BlockSpec((4, 1, PIECE, 128), pick),
                pl.BlockSpec((8, TALL - W, W), fixed),
                pl.BlockSpec((2, W, 128), fixed),
            ],
            out_specs=pl.BlockSpec((1, 2, W, W), here),
        ),
        compiler_params=params("arbitrary"),
    )(kept, at, flip, source, pair_energy, amplitudes, cross, mirror, table, near)


def on_device(
    amplitudes, integrals, ladder_slab, pair_list, mirror_slot, occ_irrep, occ_energy, virt_energy
):
    pairs = amplitudes.shape[0]
    amp = amplitudes.reshape(pairs, 2, W, W)
    ints = integrals.reshape(pairs, 2, W, W)
    slab = ladder_slab.reshape(NQ, 2, W, W)
    place = lax.axis_index("pair").astype(jnp.int32)
    virt = lax.axis_index("virt").astype(jnp.int32)
    core = jnp.bitwise_and(place, 1)
    parity = jnp.bitwise_and(jnp.right_shift(place, 1), 1)
    upper = (place >= lax.axis_size("pair") // 2).astype(jnp.int32)

    slots = jnp.arange(pairs, dtype=jnp.int32)
    label = jnp.where(upper == 0, slots, mirror_slot)
    kept = (jnp.right_shift(label, 1) == upper).astype(jnp.int32)
    at = jnp.bitwise_and(label, 1)

    def among(values, group):
        chosen = label[:, None] == jnp.arange(2, dtype=jnp.int32)[None, :] + 2 * group
        return jnp.sum(jnp.where(chosen, values[:, None], 0), axis=0)

    keep, send = among(slots, upper), among(slots, 1 - upper)

    one = pack_slab(slab, virt_energy, parity[None])
    y_one = along_y(one)
    local = to_mirror(pack_tiles(send, send, amp, ints, False))

    irrep = jnp.bitwise_xor(occ_irrep[pair_list[:, 0]], occ_irrep[pair_list[:, 1]])
    step, flip = jnp.right_shift(irrep, 1), jnp.bitwise_and(irrep, 1)
    keep_step, keep_flip = among(step, upper), among(flip, upper)
    kept_tiles = pack_tiles(keep, keep_flip, amp, ints, True)
    pair_energy = occ_energy[pair_list[:, 0]] + occ_energy[pair_list[:, 1]]
    near = jnp.broadcast_to(virt_energy.astype(F32).reshape(2, W, 1), (2, W, 128))

    def sources(step, flip):
        apart = jnp.bitwise_and(jnp.bitwise_xor(virt, step) - virt, 3)[:, None]
        second = (jnp.bitwise_xor(jnp.arange(2)[None, :], flip[:, None]) != parity).astype(jnp.int32)
        side = jnp.where(apart == 3 - 2 * core, 2, 4)
        start = jnp.where(apart == 0, 0, jnp.where(apart == 2, 6, side))
        return (start + second).reshape(-1)

    keep_source, source = sources(keep_step, keep_flip), sources(step, flip)
    ready = pair_list[0, 0] >= 0
    (
        y_one, kept_tiles, keep_step, keep_flip, pair_energy, near, keep_source, source
    ) = together(
        y_one, kept_tiles, keep_step, keep_flip, pair_energy, near, keep_source, source
    )

    def bring(y_one, kept_tiles, keep_step, slab, virt_energy):
        scattered = exchange(kept_tiles)
        x_one = along_x(y_one)
        y_far = along_y(lax.dynamic_slice(y_one, (0, core * (DEEP - PART)), (TALL, PART)))
        cross = exchange(reorder(scattered, jnp.concatenate([keep_step, keep_step])))
        two = pack_slab(slab, virt_energy, 1 - parity[None])
        return (
            two, x_one, swap_cores(y_one), swap_cores(x_one),
            y_far, along_x(y_far), swap_cores(y_far), cross,
        )

    brought = as_unit(ready, bring, y_one, kept_tiles, keep_step, slab, virt_energy)
    two, x_one, y_swap, x_swap, y_far, x_far, y_far_swap, cross, local = together(*brought, local)
    full = (one, two, y_one, x_one, y_swap, x_swap)
    parts = (y_far, x_far, y_far_swap, swap_cores(x_far))

    half_done, both_ints = first_half(slab, local, cross)
    result, table = symmetric_units(
        keep_source, core[None], half_done, both_ints, full, parts
    )
    mirrored = to_mirror(result)
    scattered = exchange(result)
    crossed = as_unit(ready, lambda x: exchange(reorder(x, keep_step)), scattered)
    new = update(
        kept, at, flip, source, pair_energy, amp, crossed, mirrored, table, near
    )
    return new.reshape(amplitudes.shape)


def solution(mesh):
    return jax.shard_map(
        on_device,
        mesh=mesh,
        in_specs=(
            P("pair", "virt", None),
            P("pair", "virt", None),
            P(None, "virt", None),
            P("pair", None),
            P("pair"),
            P(),
            P(),
            P("virt"),
        ),
        out_specs=P("pair", "virt", None),
        check_vma=False,
    )
```

```python
import functools

import jax
import jax.numpy as jnp
from jax import lax
from jax.experimental import pallas as pl
from jax.experimental.pallas import tpu as pltpu
from jax.sharding import PartitionSpec as P

W = 200
NQ = 16
DEEP = NQ * W
TALL = 208
PART = 1664
PIECE = 160
UNIT = 4 * PIECE
BF = jnp.bfloat16
F32 = jnp.float32
VMEM_LIMIT = 20 * 1024 * 1024


def permute(value, move):
    layers, halves, width, cores, lines = lax.axis_size("pair") // 16, 2, 4, 2, 4
    pairs = []
    for z in range(layers):
        for y in range(halves * lines):
            for x in range(width):
                for core in range(cores):
                    ends = []
                    for tz, ty, tx, tc in ((z, y, x, core), move(z, y, x, core)):
                        tz, ty, tx, tc = tz % layers, ty % (halves * lines), tx % width, tc % cores
                        pair = ((tz * halves + ty // lines) * width + tx) * cores + tc
                        ends.append(pair * lines + ty % lines)
                    pairs.append(tuple(ends))
    return lax.ppermute(value, ("pair", "virt"), pairs)


def along_y(value):
    return permute(value, lambda z, y, x, core: (z, y + 1 - 2 * core, x, core))


def along_x(value):
    return permute(value, lambda z, y, x, core: (z, y, x + 1 - 2 * core, core))


def swap_cores(value):
    return permute(value, lambda z, y, x, core: (z, y, x, 1 - core))


def to_mirror(value):
    half = lax.axis_size("pair") // 32
    return permute(value, lambda z, y, x, core: (z + half, y, x, core))


def exchange(units):
    return lax.all_to_all(units, "virt", 0, 0, tiled=True)


def reorder(scattered, step):
    index = jnp.bitwise_xor(jnp.arange(4, dtype=jnp.int32)[:, None], step[None, :])
    return scattered[index, jnp.arange(scattered.shape[1], dtype=jnp.int32)[None, :]]


def together(*values):
    return lax.optimization_barrier(values)


def as_unit(ready, work, *values):
    def empty(*values):
        return jax.tree.map(lambda x: jnp.zeros(x.shape, x.dtype), jax.eval_shape(work, *values))

    return lax.cond(ready, work, empty, *values)


def params(*semantics):
    return pltpu.CompilerParams(
        dimension_semantics=semantics or None, vmem_limit_bytes=VMEM_LIMIT
    )


def cost(flops, moved):
    return pl.CostEstimate(flops=flops, bytes_accessed=moved, transcendentals=0)


def in_vmem(*values):
    return [pltpu.with_memory_space_constraint(x, pltpu.VMEM) for x in values]


WHOLE = pl.BlockSpec(memory_space=pltpu.VMEM)
SCALARS = pl.BlockSpec(memory_space=pltpu.SMEM)


def pack_kernel(order_ref, *refs):
    *slab_refs, energy_ref, out_ref = refs
    for q in range(NQ):
        out_ref[0:W, q * W : (q + 1) * W] = slab_refs[q // 4][q % 4, 0]
    both = jnp.broadcast_to(energy_ref[...].reshape(1, 2 * W), (TALL - W, 2 * W))
    out_ref[W:TALL, 0:W] = jnp.where(order_ref[0] == 0, both[:, 0:W], both[:, W : 2 * W])
    out_ref[W:TALL, W:DEEP] = jnp.zeros((TALL - W, DEEP - W), BF)


def pack_slab(slab, energy, block):
    return pl.pallas_call(
        pack_kernel,
        out_shape=jax.ShapeDtypeStruct((TALL, DEEP), BF),
        grid_spec=pltpu.PrefetchScalarGridSpec(
            num_scalar_prefetch=1,
            grid=(1,),
            in_specs=[
                pl.BlockSpec((4, 1, W, W), lambda i, order, part=part: (part, order[0], 0, 0))
                for part in range(4)
            ]
            + [pl.BlockSpec((2 * W,), lambda i, order: (0,))],
            out_specs=pl.BlockSpec((TALL, DEEP), lambda i, order: (0, 0)),
        ),
        compiler_params=params("arbitrary"),
        cost_estimate=cost(0, 3_000_000),
    )(block, slab, slab, slab, slab, energy)


def put_tile(unit_ref, block, tile):
    unit_ref[block * W : (block + 1) * W, :] = tile[:, 0:128]
    unit_ref[2 * W : 3 * W, block * 64 : (block + 1) * 64] = tile[:, 128:192]
    base = 3 * W + 16 * block
    for c in range(13):
        rows = min(16, W - 16 * c)
        unit_ref[base : base + rows, 8 * c : 8 * c + 8] = tile[16 * c : 16 * c + rows, 192:200]


def get_tile(unit, block):
    base = 3 * W + 16 * block
    tail = [
        unit[base : base + min(16, W - 16 * c), 8 * c : 8 * c + 8] for c in range(13)
    ]
    return jnp.concatenate(
        [
            unit[block * W : (block + 1) * W, :],
            unit[2 * W : 3 * W, block * 64 : (block + 1) * 64],
            jnp.concatenate(tail, axis=0),
        ],
        axis=1,
    )


def whole_unit(j, *refs):
    pieces = [ref[i, j].astype(F32) for ref in refs for i in range(ref.shape[0])]
    return jnp.concatenate(pieces, axis=0)


def turned(tile):
    return jnp.pad(tile, ((0, 56), (0, 56))).T[0:W, 0:W]


def tiles_kernel(turn, pick_ref, flip_ref, amp_ref, int_ref, out_ref, unit):
    unit[3 * W : UNIT, :] = jnp.zeros((UNIT - 3 * W, 128), F32)
    j = pl.program_id(0)
    for kind, ref in enumerate((amp_ref, int_ref)):
        tiles = [ref[0, block].astype(F32) for block in range(2)]
        if turn:
            straight = flip_ref[j] == 0
            tiles = [turned(jnp.where(straight, tiles[b], tiles[1 - b])) for b in range(2)]
        for block in range(2):
            put_tile(unit, block, tiles[block])
        for i in range(4):
            out_ref[i, 2 * kind + j] = unit[i * PIECE : (i + 1) * PIECE, :].astype(BF)


def pack_tiles(pick, flip, amplitudes, integrals, turn):
    tile = pl.BlockSpec((1, 2, W, W), lambda j, pick, flip: (pick[j], 0, 0, 0))
    shape = (4, 4, PIECE, 128)
    return pl.pallas_call(
        functools.partial(tiles_kernel, turn),
        out_shape=jax.ShapeDtypeStruct(shape, BF),
        grid_spec=pltpu.PrefetchScalarGridSpec(
            num_scalar_prefetch=2,
            grid=(2,),
            in_specs=[tile, tile],
            out_specs=pl.BlockSpec(shape, lambda j, pick, flip: (0, 0, 0, 0)),
            scratch_shapes=[pltpu.VMEM((UNIT, 128), F32)],
        ),
        compiler_params=params("arbitrary"),
        cost_estimate=cost(0, 1_500_000),
    )(pick, flip, amplitudes, integrals)


def half_kernel(slab_ref, local_ref, cross_ref, half_ref, int_ref):
    for i in range(4):
        for j in range(2):
            int_ref[i, j] = local_ref[i, 2 + j].astype(F32) + cross_ref[i, 2 + j].astype(F32)

    @pl.loop(0, 2)
    def _(j):
        unit = whole_unit(j, local_ref) + whole_unit(j, cross_ref)
        for b in range(2):
            both = get_tile(unit, b).astype(BF)
            for q in range(NQ):
                half_ref[2 * j + b, :, q * W : (q + 1) * W] = jnp.dot(
                    slab_ref[q, b], both, preferred_element_type=F32
                ).astype(BF)


def first_half(slab, local, cross):
    return pl.pallas_call(
        half_kernel,
        out_shape=(pltpu.VMEM((4, W, DEEP), BF), pltpu.VMEM((4, 2, PIECE, 128), F32)),
        in_specs=[WHOLE] * 3,
        out_specs=[WHOLE] * 2,
        compiler_params=params(),
        cost_estimate=cost(8 * NQ * W**3, 4_000_000),
    )(slab, local, cross)


def ladder_kernel(source_ref, core_ref, half_ref, int_ref, *refs):
    full, (near, near_x, far, far_x), (out_ref, table_ref, unit, sums) = (
        refs[:6], refs[6:10], refs[10:]
    )
    even = core_ref[0] == 0
    odd = core_ref[0] != 0
    split = ((even, near, far), (even, near_x, far_x), (odd, far, near), (odd, far_x, near_x))
    dims = (((1,), (1,)), ((), ()))

    @pl.loop(0, 4)
    def _(t):
        for r in range(6):

            @pl.when(source_ref[t] == r)
            def _():
                sums[t] = lax.dot_general(
                    half_ref[t], full[r][0:W, :], dims, preferred_element_type=F32
                )

        for r, (on, low, high) in enumerate(split):

            @pl.when(jnp.logical_and(on, source_ref[t] == 6 + r % 2))
            def _():
                sums[t] = lax.dot_general(
                    half_ref[t, :, 0:PART], low[0:W, :], dims, preferred_element_type=F32
                ) + lax.dot_general(
                    half_ref[t, :, PART:DEEP],
                    high[0:W, 2 * PART - DEEP : PART],
                    dims,
                    preferred_element_type=F32,
                )

    for r in range(6):
        table_ref[r] = full[r][W:TALL, 0:W].astype(F32)
    for r, (on, low, _) in enumerate(split):

        @pl.when(on)
        def _():
            table_ref[6 + r % 2] = low[W:TALL, 0:W].astype(F32)

    unit[3 * W : UNIT, :] = jnp.zeros((UNIT - 3 * W, 128), F32)
    for j in range(2):
        for b in range(2):
            put_tile(unit, b, sums[2 * j + b])
        for i in range(4):
            out_ref[i, j] = (unit[i * PIECE : (i + 1) * PIECE, :] + int_ref[i, j]).astype(BF)


def symmetric_units(source, core, half_done, integrals, full, parts):
    return pl.pallas_call(
        ladder_kernel,
        out_shape=(
            jax.ShapeDtypeStruct((4, 2, PIECE, 128), BF),
            jax.ShapeDtypeStruct((8, TALL - W, W), F32),
        ),
        in_specs=[SCALARS, SCALARS] + [WHOLE] * 12,
        out_specs=[WHOLE] * 2,
        scratch_shapes=[pltpu.VMEM((UNIT, 128), F32), pltpu.VMEM((4, W, W), F32)],
        compiler_params=params(),
        cost_estimate=cost(8 * NQ * W**3, 3_000_000),
    )(source, core, *in_vmem(half_done, integrals, *full, *parts))


def update_kernel(
    kept_ref, at_ref, flip_ref, source_ref, pair_ref,
    amp_ref, cross_ref, mirror_ref, table_ref, near_ref, out_ref
):
    p = pl.program_id(0)

    def finish(block, symmetric):
        far = table_ref[source_ref[2 * p + block], 0:1, :]
        denominator = pair_ref[p] - near_ref[block, :, 0:1] - far
        old = amp_ref[0, block].astype(F32)
        out_ref[0, block] = (old + symmetric / denominator).astype(BF)

    @pl.when(kept_ref[p] == 1)
    def _():
        unit = whole_unit(0, cross_ref)
        tiles = [get_tile(unit, b) for b in range(2)]
        straight = flip_ref[p] == 0
        for b in range(2):
            finish(b, turned(jnp.where(straight, tiles[b], tiles[1 - b])))

    @pl.when(kept_ref[p] == 0)
    def _():
        unit = whole_unit(0, mirror_ref)
        for b in range(2):
            finish(b, get_tile(unit, b))


def update(kept, at, flip, source, pair_energy, amplitudes, cross, mirror, table, near):
    pairs = amplitudes.shape[0]
    pick = lambda p, k, a, f, s, e: (0, a[p], 0, 0)
    here = lambda p, k, a, f, s, e: (p, 0, 0, 0)
    fixed = lambda p, k, a, f, s, e: (0, 0, 0)
    return pl.pallas_call(
        update_kernel,
        out_shape=jax.ShapeDtypeStruct((pairs, 2, W, W), BF),
        grid_spec=pltpu.PrefetchScalarGridSpec(
            num_scalar_prefetch=5,
            grid=(pairs,),
            in_specs=[
                pl.BlockSpec((1, 2, W, W), here),
                pl.BlockSpec((4, 1, PIECE, 128), pick),
                pl.BlockSpec((4, 1, PIECE, 128), pick),
                pl.BlockSpec((8, TALL - W, W), fixed),
                pl.BlockSpec((2, W, 128), fixed),
            ],
            out_specs=pl.BlockSpec((1, 2, W, W), here),
        ),
        compiler_params=params("arbitrary"),
    )(kept, at, flip, source, pair_energy, amplitudes, cross, mirror, table, near)


def on_device(
    amplitudes, integrals, ladder_slab, pair_list, mirror_slot, occ_irrep, occ_energy, virt_energy
):
    pairs = amplitudes.shape[0]
    amp = amplitudes.reshape(pairs, 2, W, W)
    ints = integrals.reshape(pairs, 2, W, W)
    slab = ladder_slab.reshape(NQ, 2, W, W)
    place = lax.axis_index("pair").astype(jnp.int32)
    virt = lax.axis_index("virt").astype(jnp.int32)
    core = jnp.bitwise_and(place, 1)
    parity = jnp.bitwise_and(jnp.right_shift(place, 1), 1)
    upper = (place >= lax.axis_size("pair") // 2).astype(jnp.int32)

    slots = jnp.arange(pairs, dtype=jnp.int32)
    label = jnp.where(upper == 0, slots, mirror_slot)
    kept = (jnp.right_shift(label, 1) == upper).astype(jnp.int32)
    at = jnp.bitwise_and(label, 1)

    def among(values, group):
        chosen = label[:, None] == jnp.arange(2, dtype=jnp.int32)[None, :] + 2 * group
        return jnp.sum(jnp.where(chosen, values[:, None], 0), axis=0)

    keep, send = among(slots, upper), among(slots, 1 - upper)

    one = pack_slab(slab, virt_energy, parity[None])
    y_one = along_y(one)
    local = to_mirror(pack_tiles(send, send, amp, ints, False))

    irrep = jnp.bitwise_xor(occ_irrep[pair_list[:, 0]], occ_irrep[pair_list[:, 1]])
    step, flip = jnp.right_shift(irrep, 1), jnp.bitwise_and(irrep, 1)
    keep_step, keep_flip = among(step, upper), among(flip, upper)
    kept_tiles = pack_tiles(keep, keep_flip, amp, ints, True)

    def sources(step, flip):
        apart = jnp.bitwise_and(jnp.bitwise_xor(virt, step) - virt, 3)[:, None]
        second = (jnp.bitwise_xor(jnp.arange(2)[None, :], flip[:, None]) != parity).astype(jnp.int32)
        side = jnp.where(apart == 3 - 2 * core, 2, 4)
        start = jnp.where(apart == 0, 0, jnp.where(apart == 2, 6, side))
        return (start + second).reshape(-1)

    ready = pair_list[0, 0] >= 0
    y_one, kept_tiles, keep_step = together(y_one, kept_tiles, keep_step)

    def bring(y_one, kept_tiles, keep_step, keep_flip, step, flip, slab, virt_energy):
        scattered = exchange(kept_tiles)
        y_part = lax.dynamic_slice(y_one, (0, core * (DEEP - PART)), (TALL, PART))
        x_one = along_x(y_one)
        y_far = along_y(y_part)
        scalars = (
            occ_energy[pair_list[:, 0]] + occ_energy[pair_list[:, 1]],
            jnp.broadcast_to(virt_energy.astype(F32).reshape(2, W, 1), (2, W, 128)),
            sources(keep_step, keep_flip),
            sources(step, flip),
        )
        cross = exchange(reorder(scattered, jnp.concatenate([keep_step, keep_step])))
        two = pack_slab(slab, virt_energy, 1 - parity[None])
        return (
            two, x_one, swap_cores(y_one), swap_cores(x_one),
            y_far, along_x(y_far), swap_cores(y_far), cross, *scalars,
        )

    brought = as_unit(
        ready, bring, y_one, kept_tiles, keep_step, keep_flip, step, flip, slab, virt_energy
    )
    *brought, pair_energy, near, keep_source, source = brought
    two, x_one, y_swap, x_swap, y_far, x_far, y_far_swap, cross, local = together(*brought, local)
    full = (one, two, y_one, x_one, y_swap, x_swap)
    parts = (y_far, x_far, y_far_swap, swap_cores(x_far))

    half_done, both_ints = first_half(slab, local, cross)
    result, table = symmetric_units(
        keep_source, core[None], half_done, both_ints, full, parts
    )
    mirrored = to_mirror(result)
    scattered = exchange(result)
    crossed = as_unit(ready, lambda x: exchange(reorder(x, keep_step)), scattered)
    new = update(
        kept, at, flip, source, pair_energy, amp, crossed, mirrored, table, near
    )
    return new.reshape(amplitudes.shape)


def solution(mesh):
    return jax.shard_map(
        on_device,
        mesh=mesh,
        in_specs=(
            P("pair", "virt", None),
            P("pair", "virt", None),
            P(None, "virt", None),
            P("pair", None),
            P("pair"),
            P(),
            P(),
            P("virt"),
        ),
        out_specs=P("pair", "virt", None),
        check_vma=False,
    )
```

```python
import functools

import jax
import jax.numpy as jnp
from jax import lax
from jax.experimental import pallas as pl
from jax.experimental.pallas import tpu as pltpu
from jax.sharding import PartitionSpec as P

W = 200
NQ = 16
DEEP = NQ * W
TALL = 208
PART = 1664
PIECE = 160
UNIT = 4 * PIECE
BF = jnp.bfloat16
F32 = jnp.float32
VMEM_LIMIT = 20 * 1024 * 1024


def permute(value, move):
    layers, halves, width, cores, lines = lax.axis_size("pair") // 16, 2, 4, 2, 4
    pairs = []
    for z in range(layers):
        for y in range(halves * lines):
            for x in range(width):
                for core in range(cores):
                    ends = []
                    for tz, ty, tx, tc in ((z, y, x, core), move(z, y, x, core)):
                        tz, ty, tx, tc = tz % layers, ty % (halves * lines), tx % width, tc % cores
                        pair = ((tz * halves + ty // lines) * width + tx) * cores + tc
                        ends.append(pair * lines + ty % lines)
                    pairs.append(tuple(ends))
    return lax.ppermute(value, ("pair", "virt"), pairs)


def along_y(value):
    return permute(value, lambda z, y, x, core: (z, y + 1 - 2 * core, x, core))


def along_x(value):
    return permute(value, lambda z, y, x, core: (z, y, x + 1 - 2 * core, core))


def swap_cores(value):
    return permute(value, lambda z, y, x, core: (z, y, x, 1 - core))


def to_mirror(value):
    half = lax.axis_size("pair") // 32
    return permute(value, lambda z, y, x, core: (z + half, y, x, core))


def exchange(units):
    return lax.all_to_all(units, "virt", 0, 0, tiled=True)


def reorder(scattered, step):
    index = jnp.bitwise_xor(jnp.arange(4, dtype=jnp.int32)[:, None], step[None, :])
    return scattered[index, jnp.arange(scattered.shape[1], dtype=jnp.int32)[None, :]]


def together(*values):
    return lax.optimization_barrier(values)


def as_unit(ready, work, *values):
    def empty(*values):
        return jax.tree.map(lambda x: jnp.zeros(x.shape, x.dtype), jax.eval_shape(work, *values))

    return lax.cond(ready, work, empty, *values)


def params(*semantics):
    return pltpu.CompilerParams(
        dimension_semantics=semantics or None, vmem_limit_bytes=VMEM_LIMIT
    )


def cost(flops, moved):
    return pl.CostEstimate(flops=flops, bytes_accessed=moved, transcendentals=0)


def in_vmem(*values):
    return [pltpu.with_memory_space_constraint(x, pltpu.VMEM) for x in values]


WHOLE = pl.BlockSpec(memory_space=pltpu.VMEM)
SCALARS = pl.BlockSpec(memory_space=pltpu.SMEM)


def pack_kernel(order_ref, *refs):
    *slab_refs, energy_ref, out_ref = refs
    for q in range(NQ):
        out_ref[0:W, q * W : (q + 1) * W] = slab_refs[q // 4][q % 4, 0]
    both = jnp.broadcast_to(energy_ref[...].reshape(1, 2 * W), (TALL - W, 2 * W))
    out_ref[W:TALL, 0:W] = jnp.where(order_ref[0] == 0, both[:, 0:W], both[:, W : 2 * W])
    out_ref[W:TALL, W:DEEP] = jnp.zeros((TALL - W, DEEP - W), BF)


def pack_slab(slab, energy, block):
    return pl.pallas_call(
        pack_kernel,
        out_shape=jax.ShapeDtypeStruct((TALL, DEEP), BF),
        grid_spec=pltpu.PrefetchScalarGridSpec(
            num_scalar_prefetch=1,
            grid=(1,),
            in_specs=[
                pl.BlockSpec((4, 1, W, W), lambda i, order, part=part: (part, order[0], 0, 0))
                for part in range(4)
            ]
            + [pl.BlockSpec((2 * W,), lambda i, order: (0,))],
            out_specs=pl.BlockSpec((TALL, DEEP), lambda i, order: (0, 0)),
        ),
        compiler_params=params("arbitrary"),
        cost_estimate=cost(0, 3_000_000),
    )(block, slab, slab, slab, slab, energy)


def put_tile(unit_ref, block, tile):
    unit_ref[block * W : (block + 1) * W, :] = tile[:, 0:128]
    unit_ref[2 * W : 3 * W, block * 64 : (block + 1) * 64] = tile[:, 128:192]
    base = 3 * W + 16 * block
    for c in range(13):
        rows = min(16, W - 16 * c)
        unit_ref[base : base + rows, 8 * c : 8 * c + 8] = tile[16 * c : 16 * c + rows, 192:200]


def get_tile(unit, block):
    base = 3 * W + 16 * block
    tail = [
        unit[base : base + min(16, W - 16 * c), 8 * c : 8 * c + 8] for c in range(13)
    ]
    return jnp.concatenate(
        [
            unit[block * W : (block + 1) * W, :],
            unit[2 * W : 3 * W, block * 64 : (block + 1) * 64],
            jnp.concatenate(tail, axis=0),
        ],
        axis=1,
    )


def whole_unit(j, *refs):
    pieces = [ref[i, j].astype(F32) for ref in refs for i in range(ref.shape[0])]
    return jnp.concatenate(pieces, axis=0)


def turned(tile):
    return jnp.pad(tile, ((0, 56), (0, 56))).T[0:W, 0:W]


def tiles_kernel(turn, pick_ref, flip_ref, amp_ref, int_ref, out_ref, unit):
    unit[3 * W : UNIT, :] = jnp.zeros((UNIT - 3 * W, 128), F32)
    j = pl.program_id(0)
    for kind, ref in enumerate((amp_ref, int_ref)):
        tiles = [ref[0, block].astype(F32) for block in range(2)]
        if turn:
            straight = flip_ref[j] == 0
            tiles = [turned(jnp.where(straight, tiles[b], tiles[1 - b])) for b in range(2)]
        for block in range(2):
            put_tile(unit, block, tiles[block])
        for i in range(4):
            out_ref[i, 2 * kind + j] = unit[i * PIECE : (i + 1) * PIECE, :].astype(BF)


def pack_tiles(pick, flip, amplitudes, integrals, turn):
    tile = pl.BlockSpec((1, 2, W, W), lambda j, pick, flip: (pick[j], 0, 0, 0))
    shape = (4, 4, PIECE, 128)
    return pl.pallas_call(
        functools.partial(tiles_kernel, turn),
        out_shape=jax.ShapeDtypeStruct(shape, BF),
        grid_spec=pltpu.PrefetchScalarGridSpec(
            num_scalar_prefetch=2,
            grid=(2,),
            in_specs=[tile, tile],
            out_specs=pl.BlockSpec(shape, lambda j, pick, flip: (0, 0, 0, 0)),
            scratch_shapes=[pltpu.VMEM((UNIT, 128), F32)],
        ),
        compiler_params=params("arbitrary"),
        cost_estimate=cost(0, 1_500_000),
    )(pick, flip, amplitudes, integrals)


def half_kernel(slab_ref, local_ref, cross_ref, half_ref, int_ref):
    for i in range(4):
        for j in range(2):
            int_ref[i, j] = local_ref[i, 2 + j].astype(F32) + cross_ref[i, 2 + j].astype(F32)

    @pl.loop(0, 2)
    def _(j):
        unit = whole_unit(j, local_ref) + whole_unit(j, cross_ref)
        for b in range(2):
            both = get_tile(unit, b).astype(BF)
            for q in range(NQ):
                half_ref[2 * j + b, :, q * W : (q + 1) * W] = jnp.dot(
                    slab_ref[q, b], both, preferred_element_type=F32
                ).astype(BF)


def first_half(slab, local, cross):
    return pl.pallas_call(
        half_kernel,
        out_shape=(pltpu.VMEM((4, W, DEEP), BF), pltpu.VMEM((4, 2, PIECE, 128), F32)),
        in_specs=[WHOLE] * 3,
        out_specs=[WHOLE] * 2,
        compiler_params=params(),
        cost_estimate=cost(8 * NQ * W**3, 4_000_000),
    )(slab, local, cross)


def ladder_kernel(source_ref, core_ref, half_ref, int_ref, *refs):
    full, (near, near_x, far, far_x), (out_ref, table_ref, unit, sums) = (
        refs[:6], refs[6:10], refs[10:]
    )
    even = core_ref[0] == 0
    odd = core_ref[0] != 0
    split = ((even, near, far), (even, near_x, far_x), (odd, far, near), (odd, far_x, near_x))
    dims = (((1,), (1,)), ((), ()))

    @pl.loop(0, 4)
    def _(t):
        for r in range(6):

            @pl.when(source_ref[t] == r)
            def _():
                sums[t] = lax.dot_general(
                    half_ref[t], full[r][0:W, :], dims, preferred_element_type=F32
                )

        for r, (on, low, high) in enumerate(split):

            @pl.when(jnp.logical_and(on, source_ref[t] == 6 + r % 2))
            def _():
                sums[t] = lax.dot_general(
                    half_ref[t, :, 0:PART], low[0:W, :], dims, preferred_element_type=F32
                ) + lax.dot_general(
                    half_ref[t, :, PART:DEEP],
                    high[0:W, 2 * PART - DEEP : PART],
                    dims,
                    preferred_element_type=F32,
                )

    for r in range(6):
        table_ref[r] = full[r][W:TALL, 0:W].astype(F32)
    for r, (on, low, _) in enumerate(split):

        @pl.when(on)
        def _():
            table_ref[6 + r % 2] = low[W:TALL, 0:W].astype(F32)

    unit[3 * W : UNIT, :] = jnp.zeros((UNIT - 3 * W, 128), F32)
    for j in range(2):
        for b in range(2):
            put_tile(unit, b, sums[2 * j + b])
        for i in range(4):
            out_ref[i, j] = (unit[i * PIECE : (i + 1) * PIECE, :] + int_ref[i, j]).astype(BF)


def symmetric_units(source, core, half_done, integrals, full, parts):
    return pl.pallas_call(
        ladder_kernel,
        out_shape=(
            jax.ShapeDtypeStruct((4, 2, PIECE, 128), BF),
            jax.ShapeDtypeStruct((8, TALL - W, W), F32),
        ),
        in_specs=[SCALARS, SCALARS] + [WHOLE] * 12,
        out_specs=[WHOLE] * 2,
        scratch_shapes=[pltpu.VMEM((UNIT, 128), F32), pltpu.VMEM((4, W, W), F32)],
        compiler_params=params(),
        cost_estimate=cost(8 * NQ * W**3, 3_000_000),
    )(source, core, *in_vmem(half_done, integrals, *full, *parts))


def update_kernel(
    kept_ref, at_ref, flip_ref, source_ref, pair_ref,
    amp_ref, cross_ref, mirror_ref, table_ref, near_ref, out_ref
):
    p = pl.program_id(0)

    def finish(block, symmetric):
        far = table_ref[source_ref[2 * p + block], 0:1, :]
        denominator = pair_ref[p] - near_ref[block, :, 0:1] - far
        old = amp_ref[0, block].astype(F32)
        out_ref[0, block] = (old + symmetric / denominator).astype(BF)

    @pl.when(kept_ref[p] == 1)
    def _():
        unit = whole_unit(0, cross_ref)
        tiles = [get_tile(unit, b) for b in range(2)]
        straight = flip_ref[p] == 0
        for b in range(2):
            finish(b, turned(jnp.where(straight, tiles[b], tiles[1 - b])))

    @pl.when(kept_ref[p] == 0)
    def _():
        unit = whole_unit(0, mirror_ref)
        for b in range(2):
            finish(b, get_tile(unit, b))


def update(kept, at, flip, source, pair_energy, amplitudes, cross, mirror, table, near):
    pairs = amplitudes.shape[0]
    pick = lambda p, k, a, f, s, e: (0, a[p], 0, 0)
    here = lambda p, k, a, f, s, e: (p, 0, 0, 0)
    fixed = lambda p, k, a, f, s, e: (0, 0, 0)
    return pl.pallas_call(
        update_kernel,
        out_shape=jax.ShapeDtypeStruct((pairs, 2, W, W), BF),
        grid_spec=pltpu.PrefetchScalarGridSpec(
            num_scalar_prefetch=5,
            grid=(pairs,),
            in_specs=[
                pl.BlockSpec((1, 2, W, W), here),
                pl.BlockSpec((4, 1, PIECE, 128), pick),
                pl.BlockSpec((4, 1, PIECE, 128), pick),
                pl.BlockSpec((8, TALL - W, W), fixed),
                pl.BlockSpec((2, W, 128), fixed),
            ],
            out_specs=pl.BlockSpec((1, 2, W, W), here),
        ),
        compiler_params=params("arbitrary"),
    )(kept, at, flip, source, pair_energy, amplitudes, cross, mirror, table, near)


def on_device(
    amplitudes, integrals, ladder_slab, pair_list, mirror_slot, occ_irrep, occ_energy, virt_energy
):
    pairs = amplitudes.shape[0]
    amp = amplitudes.reshape(pairs, 2, W, W)
    ints = integrals.reshape(pairs, 2, W, W)
    slab = ladder_slab.reshape(NQ, 2, W, W)
    place = lax.axis_index("pair").astype(jnp.int32)
    virt = lax.axis_index("virt").astype(jnp.int32)
    core = jnp.bitwise_and(place, 1)
    parity = jnp.bitwise_and(jnp.right_shift(place, 1), 1)
    upper = (place >= lax.axis_size("pair") // 2).astype(jnp.int32)

    slots = jnp.arange(pairs, dtype=jnp.int32)
    label = jnp.where(upper == 0, slots, mirror_slot)
    kept = (jnp.right_shift(label, 1) == upper).astype(jnp.int32)
    at = jnp.bitwise_and(label, 1)

    def among(values, group):
        chosen = label[:, None] == jnp.arange(2, dtype=jnp.int32)[None, :] + 2 * group
        return jnp.sum(jnp.where(chosen, values[:, None], 0), axis=0)

    keep, send = among(slots, upper), among(slots, 1 - upper)

    one = pack_slab(slab, virt_energy, parity[None])
    y_one = along_y(one)
    local = to_mirror(pack_tiles(send, send, amp, ints, False))

    irrep = jnp.bitwise_xor(occ_irrep[pair_list[:, 0]], occ_irrep[pair_list[:, 1]])
    step, flip = jnp.right_shift(irrep, 1), jnp.bitwise_and(irrep, 1)
    keep_step, keep_flip = among(step, upper), among(flip, upper)
    kept_tiles = pack_tiles(keep, keep_flip, amp, ints, True)

    def sources(step, flip):
        apart = jnp.bitwise_and(jnp.bitwise_xor(virt, step) - virt, 3)[:, None]
        second = (jnp.bitwise_xor(jnp.arange(2)[None, :], flip[:, None]) != parity).astype(jnp.int32)
        side = jnp.where(apart == 3 - 2 * core, 2, 4)
        start = jnp.where(apart == 0, 0, jnp.where(apart == 2, 6, side))
        return (start + second).reshape(-1)

    ready = pair_list[0, 0] >= 0
    y_one, kept_tiles, keep_step = together(y_one, kept_tiles, keep_step)

    def bring(y_one, kept_tiles, keep_step, keep_flip, step, flip, slab, virt_energy):
        scattered = exchange(kept_tiles)
        y_part = lax.dynamic_slice(y_one, (0, core * (DEEP - PART)), (TALL, PART))
        x_one = along_x(y_one)
        y_far = along_y(y_part)
        scalars = (
            occ_energy[pair_list[:, 0]] + occ_energy[pair_list[:, 1]],
            sources(keep_step, keep_flip),
            sources(step, flip),
        )
        cross = exchange(reorder(scattered, jnp.concatenate([keep_step, keep_step])))
        two = pack_slab(slab, virt_energy, 1 - parity[None])
        return (
            two, x_one, swap_cores(y_one), swap_cores(x_one),
            y_far, along_x(y_far), swap_cores(y_far), cross, *scalars,
        )

    brought = as_unit(
        ready, bring, y_one, kept_tiles, keep_step, keep_flip, step, flip, slab, virt_energy
    )
    *brought, pair_energy, keep_source, source = brought
    two, x_one, y_swap, x_swap, y_far, x_far, y_far_swap, cross, local = together(*brought, local)
    full = (one, two, y_one, x_one, y_swap, x_swap)
    parts = (y_far, x_far, y_far_swap, swap_cores(x_far))

    half_done, both_ints = first_half(slab, local, cross)
    result, table = symmetric_units(
        keep_source, core[None], half_done, both_ints, full, parts
    )
    mirrored = to_mirror(result)

    def finish(result, keep_step, virt_energy):
        scattered = exchange(result)
        near = jnp.broadcast_to(virt_energy.astype(F32).reshape(2, W, 1), (2, W, 128))
        return exchange(reorder(scattered, keep_step)), near

    crossed, near = as_unit(ready, finish, result, keep_step, virt_energy)
    new = update(
        kept, at, flip, source, pair_energy, amp, crossed, mirrored, table, near
    )
    return new.reshape(amplitudes.shape)


def solution(mesh):
    return jax.shard_map(
        on_device,
        mesh=mesh,
        in_specs=(
            P("pair", "virt", None),
            P("pair", "virt", None),
            P(None, "virt", None),
            P("pair", None),
            P("pair"),
            P(),
            P(),
            P("virt"),
        ),
        out_specs=P("pair", "virt", None),
        check_vma=False,
    )
```

```python
import functools

import jax
import jax.numpy as jnp
from jax import lax
from jax.experimental import pallas as pl
from jax.experimental.pallas import tpu as pltpu
from jax.sharding import PartitionSpec as P

W = 200
NQ = 16
DEEP = NQ * W
TALL = 208
PART = 1664
PIECE = 160
UNIT = 4 * PIECE
BF = jnp.bfloat16
F32 = jnp.float32
VMEM_LIMIT = 20 * 1024 * 1024


def permute(value, move):
    layers, halves, width, cores, lines = lax.axis_size("pair") // 16, 2, 4, 2, 4
    pairs = []
    for z in range(layers):
        for y in range(halves * lines):
            for x in range(width):
                for core in range(cores):
                    ends = []
                    for tz, ty, tx, tc in ((z, y, x, core), move(z, y, x, core)):
                        tz, ty, tx, tc = tz % layers, ty % (halves * lines), tx % width, tc % cores
                        pair = ((tz * halves + ty // lines) * width + tx) * cores + tc
                        ends.append(pair * lines + ty % lines)
                    pairs.append(tuple(ends))
    return lax.ppermute(value, ("pair", "virt"), pairs)


def along_y(value):
    return permute(value, lambda z, y, x, core: (z, y + 1 - 2 * core, x, core))


def along_x(value):
    return permute(value, lambda z, y, x, core: (z, y, x + 1 - 2 * core, core))


def swap_cores(value):
    return permute(value, lambda z, y, x, core: (z, y, x, 1 - core))


def to_mirror(value):
    half = lax.axis_size("pair") // 32
    return permute(value, lambda z, y, x, core: (z + half, y, x, core))


def exchange(units):
    return lax.all_to_all(units, "virt", 0, 0, tiled=True)


def reorder(scattered, step):
    index = jnp.bitwise_xor(jnp.arange(4, dtype=jnp.int32)[:, None], step[None, :])
    return scattered[index, jnp.arange(scattered.shape[1], dtype=jnp.int32)[None, :]]


def together(*values):
    return lax.optimization_barrier(values)


def as_unit(ready, work, *values):
    def empty(*values):
        return jax.tree.map(lambda x: jnp.zeros(x.shape, x.dtype), jax.eval_shape(work, *values))

    return lax.cond(ready, work, empty, *values)


def params(*semantics):
    return pltpu.CompilerParams(
        dimension_semantics=semantics or None, vmem_limit_bytes=VMEM_LIMIT
    )


def cost(flops, moved):
    return pl.CostEstimate(flops=flops, bytes_accessed=moved, transcendentals=0)


def in_vmem(*values):
    return [pltpu.with_memory_space_constraint(x, pltpu.VMEM) for x in values]


WHOLE = pl.BlockSpec(memory_space=pltpu.VMEM)
SCALARS = pl.BlockSpec(memory_space=pltpu.SMEM)


def pack_kernel(order_ref, *refs):
    *slab_refs, energy_ref, out_ref = refs
    for q in range(NQ):
        out_ref[0:W, q * W : (q + 1) * W] = slab_refs[q // 4][q % 4, 0]
    both = jnp.broadcast_to(energy_ref[...].reshape(1, 2 * W), (TALL - W, 2 * W))
    out_ref[W:TALL, 0:W] = jnp.where(order_ref[0] == 0, both[:, 0:W], both[:, W : 2 * W])
    out_ref[W:TALL, W:DEEP] = jnp.zeros((TALL - W, DEEP - W), BF)


def pack_slab(slab, energy, block):
    return pl.pallas_call(
        pack_kernel,
        out_shape=jax.ShapeDtypeStruct((TALL, DEEP), BF),
        grid_spec=pltpu.PrefetchScalarGridSpec(
            num_scalar_prefetch=1,
            grid=(1,),
            in_specs=[
                pl.BlockSpec((4, 1, W, W), lambda i, order, part=part: (part, order[0], 0, 0))
                for part in range(4)
            ]
            + [pl.BlockSpec((2 * W,), lambda i, order: (0,))],
            out_specs=pl.BlockSpec((TALL, DEEP), lambda i, order: (0, 0)),
        ),
        compiler_params=params("arbitrary"),
        cost_estimate=cost(0, 3_000_000),
    )(block, slab, slab, slab, slab, energy)


def put_tile(unit_ref, block, tile):
    unit_ref[block * W : (block + 1) * W, :] = tile[:, 0:128]
    unit_ref[2 * W : 3 * W, block * 64 : (block + 1) * 64] = tile[:, 128:192]
    base = 3 * W + 16 * block
    for c in range(13):
        rows = min(16, W - 16 * c)
        unit_ref[base : base + rows, 8 * c : 8 * c + 8] = tile[16 * c : 16 * c + rows, 192:200]


def get_tile(unit, block):
    base = 3 * W + 16 * block
    tail = [
        unit[base : base + min(16, W - 16 * c), 8 * c : 8 * c + 8] for c in range(13)
    ]
    return jnp.concatenate(
        [
            unit[block * W : (block + 1) * W, :],
            unit[2 * W : 3 * W, block * 64 : (block + 1) * 64],
            jnp.concatenate(tail, axis=0),
        ],
        axis=1,
    )


def whole_unit(j, *refs):
    pieces = [ref[i, j].astype(F32) for ref in refs for i in range(ref.shape[0])]
    return jnp.concatenate(pieces, axis=0)


def turned(tile):
    return jnp.pad(tile, ((0, 56), (0, 56))).T[0:W, 0:W]


def tiles_kernel(turn, pick_ref, flip_ref, amp_ref, int_ref, out_ref, unit):
    unit[3 * W : UNIT, :] = jnp.zeros((UNIT - 3 * W, 128), F32)
    j = pl.program_id(0)
    for kind, ref in enumerate((amp_ref, int_ref)):
        tiles = [ref[0, block].astype(F32) for block in range(2)]
        if turn:
            straight = flip_ref[j] == 0
            tiles = [turned(jnp.where(straight, tiles[b], tiles[1 - b])) for b in range(2)]
        for block in range(2):
            put_tile(unit, block, tiles[block])
        for i in range(4):
            out_ref[i, 2 * kind + j] = unit[i * PIECE : (i + 1) * PIECE, :].astype(BF)


def pack_tiles(pick, flip, amplitudes, integrals, turn):
    tile = pl.BlockSpec((1, 2, W, W), lambda j, pick, flip: (pick[j], 0, 0, 0))
    shape = (4, 4, PIECE, 128)
    return pl.pallas_call(
        functools.partial(tiles_kernel, turn),
        out_shape=jax.ShapeDtypeStruct(shape, BF),
        grid_spec=pltpu.PrefetchScalarGridSpec(
            num_scalar_prefetch=2,
            grid=(2,),
            in_specs=[tile, tile],
            out_specs=pl.BlockSpec(shape, lambda j, pick, flip: (0, 0, 0, 0)),
            scratch_shapes=[pltpu.VMEM((UNIT, 128), F32)],
        ),
        compiler_params=params("arbitrary"),
        cost_estimate=cost(0, 1_500_000),
    )(pick, flip, amplitudes, integrals)


def half_kernel(slab_ref, local_ref, cross_ref, half_ref, int_ref):
    for i in range(4):
        for j in range(2):
            int_ref[i, j] = local_ref[i, 2 + j].astype(F32) + cross_ref[i, 2 + j].astype(F32)

    @pl.loop(0, 2)
    def _(j):
        unit = whole_unit(j, local_ref) + whole_unit(j, cross_ref)
        for b in range(2):
            both = get_tile(unit, b).astype(BF)
            for q in range(NQ):
                half_ref[2 * j + b, :, q * W : (q + 1) * W] = jnp.dot(
                    slab_ref[q, b], both, preferred_element_type=F32
                ).astype(BF)


def first_half(slab, local, cross):
    return pl.pallas_call(
        half_kernel,
        out_shape=(pltpu.VMEM((4, W, DEEP), BF), pltpu.VMEM((4, 2, PIECE, 128), F32)),
        in_specs=[WHOLE] * 3,
        out_specs=[WHOLE] * 2,
        compiler_params=params(),
        cost_estimate=cost(8 * NQ * W**3, 4_000_000),
    )(slab, local, cross)


def ladder_kernel(source_ref, core_ref, half_ref, int_ref, *refs):
    full, (near, near_x, far, far_x), (out_ref, table_ref, unit, sums) = (
        refs[:6], refs[6:10], refs[10:]
    )
    even = core_ref[0] == 0
    odd = core_ref[0] != 0
    split = ((even, near, far), (even, near_x, far_x), (odd, far, near), (odd, far_x, near_x))
    dims = (((1,), (1,)), ((), ()))

    @pl.loop(0, 4)
    def _(t):
        for r in range(6):

            @pl.when(source_ref[t] == r)
            def _():
                sums[t] = lax.dot_general(
                    half_ref[t], full[r][0:W, :], dims, preferred_element_type=F32
                )

        for r, (on, low, high) in enumerate(split):

            @pl.when(jnp.logical_and(on, source_ref[t] == 6 + r % 2))
            def _():
                sums[t] = lax.dot_general(
                    half_ref[t, :, 0:PART], low[0:W, :], dims, preferred_element_type=F32
                ) + lax.dot_general(
                    half_ref[t, :, PART:DEEP],
                    high[0:W, 2 * PART - DEEP : PART],
                    dims,
                    preferred_element_type=F32,
                )

    for r in range(6):
        table_ref[r] = full[r][W:TALL, 0:W].astype(F32)
    for r, (on, low, _) in enumerate(split):

        @pl.when(on)
        def _():
            table_ref[6 + r % 2] = low[W:TALL, 0:W].astype(F32)

    unit[3 * W : UNIT, :] = jnp.zeros((UNIT - 3 * W, 128), F32)
    for j in range(2):
        for b in range(2):
            put_tile(unit, b, sums[2 * j + b])
        for i in range(4):
            out_ref[i, j] = (unit[i * PIECE : (i + 1) * PIECE, :] + int_ref[i, j]).astype(BF)


def symmetric_units(source, core, half_done, integrals, full, parts):
    return pl.pallas_call(
        ladder_kernel,
        out_shape=(
            jax.ShapeDtypeStruct((4, 2, PIECE, 128), BF),
            jax.ShapeDtypeStruct((8, TALL - W, W), F32),
        ),
        in_specs=[SCALARS, SCALARS] + [WHOLE] * 12,
        out_specs=[WHOLE] * 2,
        scratch_shapes=[pltpu.VMEM((UNIT, 128), F32), pltpu.VMEM((4, W, W), F32)],
        compiler_params=params(),
        cost_estimate=cost(8 * NQ * W**3, 3_000_000),
    )(source, core, *in_vmem(half_done, integrals, *full, *parts))


def update_kernel(
    kept_ref, at_ref, flip_ref, source_ref, pair_ref,
    amp_ref, cross_ref, mirror_ref, table_ref, near_ref, out_ref
):
    p = pl.program_id(0)

    def finish(block, symmetric):
        far = table_ref[source_ref[2 * p + block], 0:1, :]
        denominator = pair_ref[p] - near_ref[block, :, 0:1] - far
        old = amp_ref[0, block].astype(F32)
        out_ref[0, block] = (old + symmetric / denominator).astype(BF)

    @pl.when(kept_ref[p] == 1)
    def _():
        unit = whole_unit(0, cross_ref)
        tiles = [get_tile(unit, b) for b in range(2)]
        straight = flip_ref[p] == 0
        for b in range(2):
            finish(b, turned(jnp.where(straight, tiles[b], tiles[1 - b])))

    @pl.when(kept_ref[p] == 0)
    def _():
        unit = whole_unit(0, mirror_ref)
        for b in range(2):
            finish(b, get_tile(unit, b))


def update(kept, at, flip, source, pair_energy, amplitudes, cross, mirror, table, near):
    pairs = amplitudes.shape[0]
    pick = lambda p, k, a, f, s, e: (0, a[p], 0, 0)
    here = lambda p, k, a, f, s, e: (p, 0, 0, 0)
    fixed = lambda p, k, a, f, s, e: (0, 0, 0)
    return pl.pallas_call(
        update_kernel,
        out_shape=jax.ShapeDtypeStruct((pairs, 2, W, W), BF),
        grid_spec=pltpu.PrefetchScalarGridSpec(
            num_scalar_prefetch=5,
            grid=(pairs,),
            in_specs=[
                pl.BlockSpec((1, 2, W, W), here),
                pl.BlockSpec((4, 1, PIECE, 128), pick),
                pl.BlockSpec((4, 1, PIECE, 128), pick),
                pl.BlockSpec((8, TALL - W, W), fixed),
                pl.BlockSpec((2, W, 128), fixed),
            ],
            out_specs=pl.BlockSpec((1, 2, W, W), here),
        ),
        compiler_params=params("arbitrary"),
    )(kept, at, flip, source, pair_energy, amplitudes, cross, mirror, table, near)


def on_device(
    amplitudes, integrals, ladder_slab, pair_list, mirror_slot, occ_irrep, occ_energy, virt_energy
):
    pairs = amplitudes.shape[0]
    amp = amplitudes.reshape(pairs, 2, W, W)
    ints = integrals.reshape(pairs, 2, W, W)
    slab = ladder_slab.reshape(NQ, 2, W, W)
    place = lax.axis_index("pair").astype(jnp.int32)
    virt = lax.axis_index("virt").astype(jnp.int32)
    core = jnp.bitwise_and(place, 1)
    parity = jnp.bitwise_and(jnp.right_shift(place, 1), 1)
    upper = (place >= lax.axis_size("pair") // 2).astype(jnp.int32)

    slots = jnp.arange(pairs, dtype=jnp.int32)
    label = jnp.where(upper == 0, slots, mirror_slot)
    kept = (jnp.right_shift(label, 1) == upper).astype(jnp.int32)
    at = jnp.bitwise_and(label, 1)

    def among(values, group):
        chosen = label[:, None] == jnp.arange(2, dtype=jnp.int32)[None, :] + 2 * group
        return jnp.sum(jnp.where(chosen, values[:, None], 0), axis=0)

    keep, send = among(slots, upper), among(slots, 1 - upper)

    one = pack_slab(slab, virt_energy, parity[None])
    y_one = along_y(one)
    local = to_mirror(pack_tiles(send, send, amp, ints, False))

    irrep = jnp.bitwise_xor(occ_irrep[pair_list[:, 0]], occ_irrep[pair_list[:, 1]])
    step, flip = jnp.right_shift(irrep, 1), jnp.bitwise_and(irrep, 1)
    keep_step, keep_flip = among(step, upper), among(flip, upper)
    kept_tiles = pack_tiles(keep, keep_flip, amp, ints, True)

    def sources(step, flip):
        apart = jnp.bitwise_and(jnp.bitwise_xor(virt, step) - virt, 3)[:, None]
        second = (jnp.bitwise_xor(jnp.arange(2)[None, :], flip[:, None]) != parity).astype(jnp.int32)
        side = jnp.where(apart == 3 - 2 * core, 2, 4)
        start = jnp.where(apart == 0, 0, jnp.where(apart == 2, 6, side))
        return (start + second).reshape(-1)

    ready = pair_list[0, 0] >= 0
    y_one, kept_tiles, keep_step = together(y_one, kept_tiles, keep_step)

    def bring(y_one, kept_tiles, keep_step, keep_flip, step, flip, slab, virt_energy):
        scattered = exchange(kept_tiles)
        y_part = lax.dynamic_slice(y_one, (0, core * (DEEP - PART)), (TALL, PART))
        x_one = along_x(y_one)
        y_far = along_y(y_part)
        scalars = (
            occ_energy[pair_list[:, 0]] + occ_energy[pair_list[:, 1]],
            sources(keep_step, keep_flip),
            sources(step, flip),
        )
        cross = exchange(reorder(scattered, jnp.concatenate([keep_step, keep_step])))
        two = pack_slab(slab, virt_energy, 1 - parity[None])
        return (
            two, x_one, swap_cores(y_one), swap_cores(x_one),
            y_far, along_x(y_far), swap_cores(y_far), cross, *scalars,
        )

    brought = as_unit(
        ready, bring, y_one, kept_tiles, keep_step, keep_flip, step, flip, slab, virt_energy
    )
    *brought, pair_energy, keep_source, source = brought
    two, x_one, y_swap, x_swap, y_far, x_far, y_far_swap, cross, local = together(*brought, local)
    full = (one, two, y_one, x_one, y_swap, x_swap)
    parts = (y_far, x_far, y_far_swap, swap_cores(x_far))

    half_done, both_ints = first_half(slab, local, cross)
    result, table = symmetric_units(
        keep_source, core[None], half_done, both_ints, full, parts
    )
    mirrored = to_mirror(result)
    scattered = exchange(result)
    crossed = as_unit(ready, lambda x: exchange(reorder(x, keep_step)), scattered)
    near = jnp.broadcast_to(virt_energy.astype(F32).reshape(2, W, 1), (2, W, 128))
    new = update(
        kept, at, flip, source, pair_energy, amp, crossed, mirrored, table, near
    )
    return new.reshape(amplitudes.shape)


def solution(mesh):
    return jax.shard_map(
        on_device,
        mesh=mesh,
        in_specs=(
            P("pair", "virt", None),
            P("pair", "virt", None),
            P(None, "virt", None),
            P("pair", None),
            P("pair"),
            P(),
            P(),
            P("virt"),
        ),
        out_specs=P("pair", "virt", None),
        check_vma=False,
    )
```
